512 devices in a mesh: seq: 128 (over x_hi, z, y), tp: 4 (over x_lo, core).
Axes of the slice: x: 4 (x_hi: 2, x_lo: 2; x = x_hi * 2 + x_lo), y: 8, z: 8, core: 2. Of those that a mesh axis runs over, the one named last changes fastest.
Arguments:
- frames: bfloat16 [6144, 1024], P('seq'), may hold values from -6 to 6
- query_rows: bfloat16 [6144, 1024], P('seq', 'tp'), may hold values from -6 to 6
- key_rows: bfloat16 [6144, 1024], P('seq', 'tp'), may hold values from -6 to 6
- value_rows: bfloat16 [6144, 1024], P('seq', 'tp'), may hold values from -48 to 48
- w_out: bfloat16 [1024, 1024], P('tp'), may hold values from -0.1875 to 0.1875
- w_in: bfloat16 [1024, 2, 2048], P(None, None, 'tp'), may hold values from -0.84375 to 0.84375
- w_conv: float32 [31, 2048], P(None, 'tp'), may hold values from -1 to 1
- w_proj: bfloat16 [2048, 1024], P('tp'), may hold values from -0.125 to 0.125
- w_blend: float32 [31, 2, 1024], P(None, None, 'tp'), may hold values from -1 to 1
- w_merge: bfloat16 [2, 1024, 1024], P(None, 'tp'), may hold values from -0.125 to 0.125
Outputs:
- merged: bfloat16 [6144, 1024], P('seq', 'tp')
The draws below stay inside these ranges and needn't reach their ends.
All inputs are finite; a program needn't handle non-finite values.
Results may differ from the reference program's by a relative error of at most 0.023.
Values may be sent and summed in bfloat16 or wider, within the bound.
A program may use at most 64 MiB of HBM per device.

```python
import math
import jax
import jax.numpy as jnp
from jax import lax

D = 1024
HEADS = 16
HEAD = 64
KCONV = 31
KMERGE = 31
CH = 2048
HD = 1024
TOKENS = 6144


def draw_query_rows(key, part):
    key = jax.random.fold_in(key, 7)
    base_draw = jnp.clip(1.41 * jax.random.normal(key, (TOKENS, HEADS * HEAD)), -6.0, 6.0)
    return base_draw.astype(jnp.bfloat16)


def draw_key_rows(key, part):
    key = jax.random.fold_in(key, 8)
    base_draw = jnp.clip(1.41 * jax.random.normal(key, (TOKENS, HEADS * HEAD)), -6.0, 6.0)
    return base_draw.astype(jnp.bfloat16)


def draw_w_in(key, part):
    key = jax.random.fold_in(key, 31)
    base_key, jitter_key = jax.random.split(key)
    base_draw = jnp.clip(jax.random.normal(base_key, (D, 2, CH)), -6.0, 6.0)
    channel = jnp.arange(CH, dtype=jnp.float32) / CH
    rising = jnp.stack([jnp.ones((CH,), jnp.float32), 3.0 ** channel])
    jitter = jnp.exp(jax.random.uniform(jitter_key, (1, 2, CH), minval=-0.4, maxval=0.4))
    return (base_draw * D ** (-0.5) * rising[None] * jitter).astype(jnp.bfloat16)


def level_of(own_key, extent, cuts, smallest, largest):
    factor_of, own = 1.0, jax.random.fold_in(own_key, 6)
    for dim, blocks in cuts:
        steps = jnp.exp(jax.random.uniform(jax.random.fold_in(own, dim), (blocks,), jnp.float32, smallest / len(cuts), largest / len(cuts)))
        factor_of = factor_of * jnp.repeat(steps, extent[dim] // blocks).reshape([-1 if axis == dim else 1 for axis in range(len(extent))])
    return factor_of


def normal_values(key, dims, spread, limit, shards=(), kind=jnp.bfloat16):
    drawn = spread * jax.random.normal(key, dims, jnp.float32)
    if shards:
        drawn = drawn * level_of(key, dims, shards, -0.22, 0.18)
    return jnp.clip(drawn, -limit, limit).astype(kind)


def setup_inputs(seed: int = 0) -> dict:
    arg_keys = jax.random.split(jax.random.key(seed), 11)
    frames = normal_values(arg_keys[0], (TOKENS, D), 1.0, 6.0, ((0, 128),))
    query_rows = draw_query_rows(jax.random.fold_in(arg_keys[10], 71), 0)
    key_rows = draw_key_rows(jax.random.fold_in(arg_keys[10], 71), 0)
    value_rows = normal_values(arg_keys[3], (TOKENS, HD), 8.0, 48.0, ((0, 128), (1, 4)))
    w_out = normal_values(arg_keys[4], (HD, D), HD ** -0.5, 0.1875, ((0, 4),))
    w_in = draw_w_in(jax.random.fold_in(arg_keys[10], 71), 0)
    w_conv = normal_values(arg_keys[6], (KCONV, CH), KCONV ** -0.5, 1.0, ((1, 4),), jnp.float32)
    w_proj = normal_values(arg_keys[7], (CH, D), CH ** -0.5, 0.125, ((0, 4),))
    w_blend = normal_values(arg_keys[8], (KMERGE, 2, D), KMERGE ** -0.5, 1.0, ((2, 4),), jnp.float32)
    w_merge = normal_values(arg_keys[9], (2, D, D), (2 * D) ** -0.5, 0.125, ((1, 4),))
    return {"frames": frames, "query_rows": query_rows, "key_rows": key_rows, "value_rows": value_rows, "w_out": w_out, "w_in": w_in, "w_conv": w_conv, "w_proj": w_proj, "w_blend": w_blend, "w_merge": w_merge}


def normalize_rows(features):
    average = lax.optimization_barrier(jnp.mean(features, -1, keepdims=True))
    centered = features - average
    variance = lax.optimization_barrier(jnp.mean(centered * centered, -1, keepdims=True))
    return centered * lax.rsqrt(variance + 1e-05)

def depthwise(padded, tap_weights, row_count):
    result = jnp.zeros((row_count, padded.shape[1]), jnp.float32)
    for offset in range(tap_weights.shape[0]):
        result = result + tap_weights[offset] * padded[offset:offset + row_count].astype(jnp.float32)
    return result

def head_attention(query_head, key_head, value_head):
    block_rows = math.gcd(TOKENS, 512)
    scale_factor = HEAD ** (-0.5)
    key_float = key_head.astype(jnp.float32)
    value_float = value_head.astype(jnp.float32)
    blocks = query_head.reshape(TOKENS // block_rows, block_rows, HEAD)

    def one_block(query_block):
        scores = jnp.dot(query_block.astype(jnp.float32), key_float.T) * scale_factor
        peak_score = lax.optimization_barrier(jnp.max(scores, -1, keepdims=True))
        exp_scores = jnp.exp(scores - peak_score)
        prob_total = lax.optimization_barrier(jnp.sum(exp_scores, -1, keepdims=True))
        weights = lax.optimization_barrier(exp_scores.astype(jnp.bfloat16)).astype(jnp.float32)
        return (jnp.dot(weights, value_float) / prob_total).astype(jnp.bfloat16)
    return lax.map(one_block, blocks).reshape(TOKENS, HEAD)

def reference(frames, query_rows, key_rows, value_rows, w_out, w_in, w_conv, w_proj, w_blend, w_merge):
    head_outputs = []
    for head_index in range(HEADS):
        head_start = head_index * HEAD
        head_outputs.append(head_attention(query_rows[:, head_start:head_start + HEAD], key_rows[:, head_start:head_start + HEAD], value_rows[:, head_start:head_start + HEAD]))
    attended = jnp.concatenate(head_outputs, axis=1)
    att_out = jnp.dot(attended, w_out, preferred_element_type=jnp.float32).astype(jnp.bfloat16)
    normed = normalize_rows(frames.astype(jnp.float32)).astype(jnp.bfloat16)
    hidden = jax.nn.gelu(jnp.dot(normed, w_in.reshape(D, 2 * CH), preferred_element_type=jnp.float32), approximate=False).astype(jnp.bfloat16)
    resid_half = hidden[:, :CH]
    gate_half = hidden[:, CH:]
    gate_float = gate_half.astype(jnp.float32)
    average = lax.optimization_barrier(jnp.sum(gate_float, -1)) / CH
    variance = lax.optimization_barrier(jnp.sum(gate_float * gate_float, -1)) / CH - average * average
    gate_norm = ((gate_float - average[:, None]) * lax.rsqrt(variance + 1e-05)[:, None]).astype(jnp.bfloat16)
    halo_reach = (KCONV - 1) // 2
    padded = jnp.pad(gate_norm, ((halo_reach, halo_reach), (0, 0)))
    conv_out = depthwise(padded, w_conv, TOKENS)
    gated_rows = (resid_half.astype(jnp.float32) * conv_out).astype(jnp.bfloat16)
    cg_out = jnp.dot(gated_rows, w_proj, preferred_element_type=jnp.float32).astype(jnp.bfloat16)
    joined = jnp.concatenate([att_out, cg_out], axis=1)
    merge_reach = (KMERGE - 1) // 2
    joined_pad = jnp.pad(joined, ((merge_reach, merge_reach), (0, 0)))
    mixture = (joined.astype(jnp.float32) + depthwise(joined_pad, w_blend.reshape(KMERGE, 2 * D), TOKENS)).astype(jnp.bfloat16)
    merged = frames.astype(jnp.float32) + jnp.dot(mixture, w_merge.reshape(2 * D, D), preferred_element_type=jnp.float32)
    return merged.astype(jnp.bfloat16)
```

```python
import functools

import jax
import jax.numpy as jnp
from jax import lax
from jax.experimental import pallas as pl
from jax.experimental.pallas import tpu as pltpu
from jax.sharding import PartitionSpec as P

HEAD = 64
CH = 2048
TAPS = 31
HALO = 16
HEADS_HERE = 4
RING = 8
LOG2E = 1.4426950408889634
LN2 = 0.6931471805599453
F32 = jnp.float32
BF16 = jnp.bfloat16
MESH = pl.DeviceIdType.MESH


def low_lanes(rows):
    return lax.broadcasted_iota(jnp.int32, (rows, 128), 1) < HEAD


def depthwise(pad_ref, taps_ref, column, rows):
    lanes = pl.ds(column, 128)
    total = jnp.zeros((rows, 128), F32)
    for phase in range(8):
        shifted = pad_ref[pl.ds(phase, rows + 24 if phase else rows + 32), lanes]
        for start in range(0, 33, 8):
            j = start + phase - 1
            if 0 <= j < TAPS:
                total = total + taps_ref[pl.ds(j, 1), lanes] * shifted[start : start + rows]
    return total


def kernel(
    seq_size,
    tp_size,
    frames,
    query,
    key,
    value,
    w_out_hbm,
    w_in_hbm,
    w_conv_hbm,
    w_proj_hbm,
    w_blend_hbm,
    w_merge_hbm,
    out,
    w_out,
    w_in,
    w_conv,
    w_proj,
    w_blend,
    w_merge,
    kv_send,
    q_send,
    kv_all,
    kv_ones,
    q_all,
    o_send,
    o_recv,
    gate_half,
    resid_half,
    gate_prev,
    gate_next,
    stat_send,
    stat_recv,
    stat_prev,
    stat_next,
    gate_pad,
    part_send,
    part_recv,
    part_prev,
    part_next,
    blend_pad,
    taps_pad,
    fin_acc,
    fin_send,
    fin_recv,
    weight_sem,
    kv_ss,
    kv_rs,
    ring_ss,
    ring_rs,
    q_ss,
    q_rs,
    o_ss,
    o_rs,
    gate_ss,
    gate_rs,
    stat_ss,
    stat_rs,
    stat_hs,
    stat_hr,
    part_ss,
    part_rs,
    part_hs,
    part_hr,
    fin_ss,
    fin_rs,
):
    rows = query.shape[0]
    wide = rows + 2 * HALO
    seq = lax.axis_index("seq")
    tp = lax.axis_index("tp")
    groups = seq_size // RING
    lane_at = lax.rem(seq, RING)
    group = seq // RING
    head_at = lax.rem(group, HEADS_HERE)
    block = group // HEADS_HERE
    after = lax.rem(seq + 1, seq_size)
    before = lax.rem(seq + seq_size - 1, seq_size)

    def head_peer(i):
        other = lax.rem(head_at + i, HEADS_HERE)
        return other, (block * HEADS_HERE + other) * RING + lane_at

    def group_peer(i):
        other = lax.rem(group + i, groups)
        return other, other * RING + lane_at

    def ring_peer(i):
        other = lax.rem(lane_at + i, RING)
        return group * RING + other

    def tp_peer(i):
        return lax.rem(tp + i, tp_size)

    def send(src, dst, send_sem, recv_sem, to_seq, to_tp):
        return pltpu.make_async_remote_copy(
            src_ref=src,
            dst_ref=dst,
            send_sem=send_sem,
            recv_sem=recv_sem,
            device_id=(to_seq, to_tp),
            device_id_type=MESH,
        )

    weights = [
        pltpu.make_async_copy(src, dst, weight_sem.at[i])
        for i, (src, dst) in enumerate(
            (
                (w_in_hbm, w_in),
                (w_conv_hbm, w_conv),
                (w_proj_hbm, w_proj),
                (w_blend_hbm, w_blend),
                (w_merge_hbm, w_merge),
                (w_out_hbm, w_out),
            )
        )
    ]
    for copy in weights:
        copy.start()

    barrier = pltpu.get_barrier_semaphore()

    def greet(to_seq, to_tp):
        pl.semaphore_signal(barrier, inc=1, device_id=(to_seq, to_tp), device_id_type=MESH)

    @pl.loop(1, groups)
    def _(i):
        greet(group_peer(i)[1], tp)

    @pl.loop(1, RING)
    def _(i):
        greet(ring_peer(i), tp)

    @pl.loop(1, tp_size)
    def _(i):
        greet(seq, tp_peer(i))

    @pl.loop(0, tp_size)
    def _(i):
        greet(after, i)
        greet(before, i)

    low = low_lanes(rows)
    for pair in range(HEADS_HERE // 2):
        lanes = pl.ds(pair * 128, 128)
        k2 = key[:, lanes].astype(F32)
        v2 = value[:, lanes].astype(F32)
        q2 = query[:, lanes].astype(F32)
        kv_send[2 * pair] = jnp.where(low, k2, pltpu.roll(v2, HEAD, 1)).astype(BF16)
        kv_send[2 * pair + 1] = jnp.where(low, pltpu.roll(k2, HEAD, 1), v2).astype(BF16)
        q_send[2 * pair] = jnp.where(low, q2, 0.0).astype(BF16)
        q_send[2 * pair + 1] = jnp.where(low, pltpu.roll(q2, HEAD, 1), 0.0).astype(BF16)
    kv_all[lane_at, head_at] = kv_send[head_at]
    q_all[group] = q_send[head_at]

    pl.semaphore_wait(barrier, (groups - 1) + (RING - 1) + (tp_size - 1) + 2 * tp_size)

    def kv_copy(i):
        other, to = head_peer(i)
        return send(
            kv_send.at[other], kv_all.at[lane_at, head_at], kv_ss.at[i], kv_rs.at[i], to, tp
        )

    def q_copy(i):
        other, to = group_peer(i)
        return send(
            q_send.at[lax.rem(other, HEADS_HERE)],
            q_all.at[group],
            q_ss.at[i],
            q_rs.at[i],
            to,
            tp,
        )

    def ring_copy(i):
        return send(
            kv_all.at[lane_at], kv_all.at[lane_at], ring_ss.at[i], ring_rs.at[i], ring_peer(i), tp
        )

    @pl.loop(1, HEADS_HERE)
    def _(i):
        kv_copy(i).start()

    @pl.loop(1, groups)
    def _(i):
        q_copy(i).start()

    features = frames[...].astype(F32)
    centered = features - jnp.mean(features, -1, keepdims=True)
    variance = jnp.mean(centered * centered, -1, keepdims=True)
    normed = (centered * lax.rsqrt(variance + 1e-05)).astype(BF16)

    @pl.loop(1, HEADS_HERE)
    def _(i):
        kv_copy(i).wait_recv()

    @pl.loop(1, RING)
    def _(i):
        ring_copy(i).start()

    weights[0].wait()

    def hidden_half(half):
        product = jnp.dot(normed, w_in[:, half, :], preferred_element_type=F32)
        return (0.5 * product * (1.0 + lax.erf(product * 0.7071067811865476))).astype(BF16)

    gate = hidden_half(1)
    gate_half[...] = gate
    gate_float = gate.astype(F32)
    sums = jnp.sum(gate_float, -1, keepdims=True)
    squares = jnp.sum(gate_float * gate_float, -1, keepdims=True)
    stat_send[...] = jnp.where(low, sums, squares)

    tail = pl.ds(rows - HALO, HALO)
    head = pl.ds(0, HALO)

    def gate_copies():
        return (
            send(gate_half.at[tail], gate_prev, gate_ss.at[0], gate_rs.at[0], after, tp),
            send(gate_half.at[head], gate_next, gate_ss.at[1], gate_rs.at[1], before, tp),
        )

    def stat_copy(i):
        return send(
            stat_send, stat_recv.at[tp], stat_ss.at[i], stat_rs.at[i], seq, tp_peer(i)
        )

    def stat_halo(i):
        to = tp_peer(i)
        return (
            send(
                stat_send.at[tail], stat_prev.at[tp], stat_hs.at[0, i], stat_hr.at[0, i], after, to
            ),
            send(
                stat_send.at[head], stat_next.at[tp], stat_hs.at[1, i], stat_hr.at[1, i], before, to
            ),
        )

    @pl.loop(1, tp_size)
    def _(i):
        stat_copy(i).start()

    @pl.loop(0, tp_size)
    def _(i):
        for copy in stat_halo(i):
            copy.start()

    for copy in gate_copies():
        copy.start()
    stat_recv[tp] = stat_send[...]

    resid_half[...] = hidden_half(0)

    @pl.loop(1, tp_size)
    def _(i):
        stat_copy(i).wait_recv()

    @pl.loop(0, tp_size)
    def _(i):
        for copy in stat_halo(i):
            copy.wait_recv()

    for copy in gate_copies():
        copy.wait_recv()

    def gate_normed(part, stats, keep):
        total = jnp.sum(stats[...], 0)
        average = total[:, 0:1] / CH
        variance = total[:, HEAD : HEAD + 1] / CH - average * average
        result = (part[...].astype(F32) - average) * lax.rsqrt(variance + 1e-05)
        result = result.astype(BF16).astype(F32)
        return result if keep is None else jnp.where(keep, result, 0.0)

    first, last = seq == 0, seq == seq_size - 1
    gate_pad[pl.ds(0, HALO)] = gate_normed(gate_prev, stat_prev, jnp.logical_not(first))
    gate_pad[pl.ds(HALO, rows)] = gate_normed(gate_half, stat_recv, None)
    gate_pad[pl.ds(HALO + rows, HALO)] = gate_normed(gate_next, stat_next, jnp.logical_not(last))
    weights[1].wait()
    weights[2].wait()
    cg_part = jnp.zeros((rows, w_proj.shape[1]), F32)
    gated = []
    for column in range(0, resid_half.shape[1], 128):
        conv = depthwise(gate_pad, w_conv, column, rows)
        resid = resid_half[:, pl.ds(column, 128)].astype(F32)
        gated.append((resid * conv).astype(BF16))
    cg_part = jnp.dot(jnp.concatenate(gated, 1), w_proj[...], preferred_element_type=F32)

    width = out.shape[1]

    def part_copy(which, i):
        to = tp_peer(i)
        return send(
            part_send.at[which, to],
            part_recv.at[which, tp],
            part_ss.at[which, i],
            part_rs.at[which, i],
            seq,
            to,
        )

    def part_halo(which, i):
        to = tp_peer(i)
        return (
            send(
                part_send.at[which, to, tail],
                part_prev.at[which, tp],
                part_hs.at[which, 0, i],
                part_hr.at[which, 0, i],
                after,
                to,
            ),
            send(
                part_send.at[which, to, head],
                part_next.at[which, tp],
                part_hs.at[which, 1, i],
                part_hr.at[which, 1, i],
                before,
                to,
            ),
        )

    def scatter_part(which, part):
        for i in range(tp_size):
            part_send[which, i] = part[:, i * width : (i + 1) * width].astype(BF16)

        @pl.loop(1, tp_size)
        def _(i):
            part_copy(which, i).start()

        @pl.loop(0, tp_size)
        def _(i):
            for copy in part_halo(which, i):
                copy.start()

        part_recv[which, tp] = part_send[which, tp]

    def merge_part(which):
        @pl.loop(1, tp_size)
        def _(i):
            part_copy(which, i).wait_recv()

        @pl.loop(0, tp_size)
        def _(i):
            for copy in part_halo(which, i):
                copy.wait_recv()

        def joined(ref):
            return jnp.sum(ref[which].astype(F32), 0).astype(BF16).astype(F32)

        own = joined(part_recv)
        blend_pad[pl.ds(0, HALO)] = jnp.where(first, 0.0, joined(part_prev))
        blend_pad[pl.ds(HALO, rows)] = own
        blend_pad[pl.ds(HALO + rows, HALO)] = jnp.where(last, 0.0, joined(part_next))
        taps_pad[...] = w_blend[:, which, :]
        mixture = [
            (own[:, c : c + 128] + depthwise(blend_pad, taps_pad, c, rows)).astype(BF16)
            for c in range(0, width, 128)
        ]
        return jnp.dot(jnp.concatenate(mixture, 1), w_merge[which], preferred_element_type=F32)

    scatter_part(1, cg_part)

    @pl.loop(1, groups)
    def _(i):
        q_copy(i).wait_recv()

    @pl.loop(1, RING)
    def _(i):
        ring_copy(i).wait_recv()

    keys = RING * HEADS_HERE * rows
    kv = kv_all[...].reshape(keys, 128)
    kv_ones[...] = jnp.where(low_lanes(keys), jnp.ones((), BF16), kv)

    def o_copy(other):
        return send(
            o_send.at[other], o_recv.at[group], o_ss.at[other], o_rs.at[group], other * RING + lane_at, tp
        )

    per_step = 4

    @pl.loop(0, groups // per_step)
    def _(step):
        count = per_step * rows
        q = q_all[pl.ds(step * per_step, per_step)].reshape(count, 128)
        kv = kv_all[...].reshape(keys, 128)
        scores = lax.dot_general(q, kv, (((1,), (1,)), ((), ())), preferred_element_type=F32)
        peak = jnp.max(scores, -1, keepdims=True)
        weight = jnp.exp2((scores - peak) * (LOG2E * HEAD**-0.5)).astype(BF16)
        mixed = jnp.dot(weight, kv_ones[...], preferred_element_type=F32)
        low_q = low_lanes(count)
        total = jnp.where(low_q, mixed, pltpu.roll(mixed, HEAD, 1))
        level = peak * HEAD**-0.5 + jnp.log(total)
        level_high = level.astype(BF16).astype(F32)
        lane = lax.broadcasted_iota(jnp.int32, (count, 128), 1)
        packed = jnp.where(
            low_q,
            jnp.where(lane < HEAD // 2, level_high, level - level_high),
            mixed / total,
        ).astype(BF16)
        o_send[pl.ds(step * per_step, per_step)] = packed.reshape(per_step, rows, 128)
        for i in range(per_step):
            other = step * per_step + i

            @pl.when(other != group)
            def _():
                o_copy(other).start()

            @pl.when(other == group)
            def _():
                o_recv[other] = o_send[other]

    for i in (3, 4):
        weights[i].wait()
    fin_acc[...] = merge_part(1)
    weights[5].wait()

    def o_arrival(other):
        return send(
            o_send.at[other], o_recv.at[other], o_ss.at[other], o_rs.at[other], other * RING + lane_at, tp
        )

    @pl.loop(1, groups)
    def _(i):
        o_arrival(group_peer(i)[0]).wait_recv()

    heads = []
    for h in range(HEADS_HERE):
        pieces = [
            o_recv[b * HEADS_HERE + h].astype(F32) for b in range(groups // HEADS_HERE)
        ]
        levels = [p[:, 0:1] + p[:, HEAD // 2 : HEAD // 2 + 1] for p in pieces]
        peak = functools.reduce(jnp.maximum, levels)
        shares = [jnp.exp(level - peak) for level in levels]
        whole = functools.reduce(jnp.add, shares)
        mixed = functools.reduce(jnp.add, [s * p for s, p in zip(shares, pieces)])
        heads.append(mixed / whole)
    attended = jnp.concatenate(
        [
            jnp.where(low, pltpu.roll(heads[2 * pair], HEAD, 1), heads[2 * pair + 1]).astype(BF16)
            for pair in range(HEADS_HERE // 2)
        ],
        1,
    )
    scatter_part(0, jnp.dot(attended, w_out[...], preferred_element_type=F32))
    merged = fin_acc[...] + merge_part(0)

    def fin_copy(i):
        to = tp_peer(i)
        return send(fin_send.at[to], fin_recv.at[tp], fin_ss.at[i], fin_rs.at[i], seq, to)

    for i in range(tp_size):
        fin_send[i] = merged[:, i * width : (i + 1) * width].astype(BF16)

    @pl.loop(1, tp_size)
    def _(i):
        fin_copy(i).start()

    fin_recv[tp] = fin_send[tp]

    @pl.loop(1, tp_size)
    def _(i):
        fin_copy(i).wait_recv()

    own = frames[:, pl.ds(pl.multiple_of(tp * width, width), width)].astype(F32)
    out[...] = (own + jnp.sum(fin_recv[...].astype(F32), 0)).astype(BF16)

    @pl.loop(1, HEADS_HERE)
    def _(i):
        kv_copy(i).wait_send()

    @pl.loop(1, groups)
    def _(i):
        q_copy(i).wait_send()
        o_arrival(group_peer(i)[0]).wait_send()

    @pl.loop(1, RING)
    def _(i):
        ring_copy(i).wait_send()

    for copy in gate_copies():
        copy.wait_send()

    @pl.loop(1, tp_size)
    def _(i):
        stat_copy(i).wait_send()
        part_copy(0, i).wait_send()
        part_copy(1, i).wait_send()
        fin_copy(i).wait_send()

    @pl.loop(0, tp_size)
    def _(i):
        for copy in stat_halo(i) + part_halo(0, i) + part_halo(1, i):
            copy.wait_send()


def solution(mesh):
    seq_size, tp_size = mesh.shape["seq"], mesh.shape["tp"]

    def on_device(*args):
        frames, query, key, value, w_out, w_in, w_conv, w_proj, w_blend, w_merge = args
        rows, width = query.shape
        features = frames.shape[1]
        units = w_in.shape[2]
        groups = seq_size // RING
        wide = rows + 2 * HALO
        dma = pltpu.SemaphoreType.DMA
        vmem = pltpu.VMEM
        return pl.pallas_call(
            functools.partial(kernel, seq_size, tp_size),
            out_shape=jax.ShapeDtypeStruct((rows, width), BF16),
            in_specs=[pl.BlockSpec(memory_space=pltpu.VMEM)] * 4
            + [pl.BlockSpec(memory_space=pl.ANY)] * 6,
            out_specs=pl.BlockSpec(memory_space=pltpu.VMEM),
            scratch_shapes=[
                vmem(w_out.shape, BF16),
                vmem(w_in.shape, BF16),
                vmem(w_conv.shape, F32),
                vmem(w_proj.shape, BF16),
                vmem(w_blend.shape, F32),
                vmem(w_merge.shape, BF16),
                vmem((HEADS_HERE, rows, 128), BF16),
                vmem((HEADS_HERE, rows, 128), BF16),
                vmem((RING, HEADS_HERE, rows, 128), BF16),
                vmem((RING * HEADS_HERE * rows, 128), BF16),
                vmem((groups, rows, 128), BF16),
                vmem((groups, rows, 128), BF16),
                vmem((groups, rows, 128), BF16),
                vmem((rows, units), BF16),
                vmem((rows, units), BF16),
                vmem((HALO, units), BF16),
                vmem((HALO, units), BF16),
                vmem((rows, 128), F32),
                vmem((tp_size, rows, 128), F32),
                vmem((tp_size, HALO, 128), F32),
                vmem((tp_size, HALO, 128), F32),
                vmem((wide, units), F32),
                vmem((2, tp_size, rows, width), BF16),
                vmem((2, tp_size, rows, width), BF16),
                vmem((2, tp_size, HALO, width), BF16),
                vmem((2, tp_size, HALO, width), BF16),
                vmem((wide, width), F32),
                vmem((TAPS, width), F32),
                vmem((rows, features), F32),
                vmem((tp_size, rows, width), BF16),
                vmem((tp_size, rows, width), BF16),
                dma((6,)),
                dma((HEADS_HERE,)),
                dma((HEADS_HERE,)),
                dma((RING,)),
                dma((RING,)),
                dma((groups,)),
                dma((groups,)),
                dma((groups,)),
                dma((groups,)),
                dma((2,)),
                dma((2,)),
                dma((tp_size,)),
                dma((tp_size,)),
                dma((2, tp_size)),
                dma((2, tp_size)),
                dma((2, tp_size)),
                dma((2, tp_size)),
                dma((2, 2, tp_size)),
                dma((2, 2, tp_size)),
                dma((tp_size,)),
                dma((tp_size,)),
            ],
            compiler_params=pltpu.CompilerParams(
                collective_id=0,
                has_side_effects=True,
                vmem_limit_bytes=48 * 1024 * 1024,
            ),
        )(*args)

    return jax.shard_map(
        on_device,
        mesh=mesh,
        in_specs=(
            P("seq", None),
            P("seq", "tp"),
            P("seq", "tp"),
            P("seq", "tp"),
            P("tp", None),
            P(None, None, "tp"),
            P(None, "tp"),
            P("tp", None),
            P(None, None, "tp"),
            P(None, "tp", None),
        ),
        out_specs=P("seq", "tp"),
        check_vma=False,
    )
```

```python
import functools

import jax
import jax.numpy as jnp
from jax import lax
from jax.experimental import pallas as pl
from jax.experimental.pallas import tpu as pltpu
from jax.sharding import PartitionSpec as P

HEAD = 64
CH = 2048
TAPS = 31
HALO = 16
HEADS_HERE = 4
RING = 8
LOG2E = 1.4426950408889634
LN2 = 0.6931471805599453
F32 = jnp.float32
BF16 = jnp.bfloat16
MESH = pl.DeviceIdType.MESH


def low_lanes(rows):
    return lax.broadcasted_iota(jnp.int32, (rows, 128), 1) < HEAD


def depthwise(pad_ref, taps_ref, column, rows):
    lanes = pl.ds(column, 128)
    total = jnp.zeros((rows, 128), F32)
    for phase in range(8):
        shifted = pad_ref[pl.ds(phase, rows + 24 if phase else rows + 32), lanes]
        for start in range(0, 33, 8):
            j = start + phase - 1
            if 0 <= j < TAPS:
                total = total + taps_ref[pl.ds(j, 1), lanes] * shifted[start : start + rows]
    return total


def kernel(
    seq_size,
    tp_size,
    frames_hbm,
    query_hbm,
    key_hbm,
    value_hbm,
    w_out_hbm,
    w_in_hbm,
    w_conv_hbm,
    w_proj_hbm,
    w_blend_hbm,
    w_merge_hbm,
    out,
    frames,
    query,
    key,
    value,
    w_out,
    w_in,
    w_conv,
    w_proj,
    w_blend,
    w_merge,
    kv_send,
    q_send,
    kv_all,
    kv_ones,
    q_all,
    o_send,
    o_recv,
    gate_half,
    resid_half,
    gate_prev,
    gate_next,
    stat_send,
    stat_recv,
    stat_prev,
    stat_next,
    gate_pad,
    part_send,
    part_recv,
    part_prev,
    part_next,
    blend_pad,
    taps_pad,
    fin_acc,
    fin_send,
    fin_recv,
    near_sem,
    weight_sem,
    kv_ss,
    kv_rs,
    ring_ss,
    ring_rs,
    q_ss,
    q_rs,
    o_ss,
    o_rs,
    gate_ss,
    gate_rs,
    stat_ss,
    stat_rs,
    stat_hs,
    stat_hr,
    part_ss,
    part_rs,
    part_hs,
    part_hr,
    fin_ss,
    fin_rs,
):
    rows = query.shape[0]
    wide = rows + 2 * HALO
    seq = lax.axis_index("seq")
    tp = lax.axis_index("tp")
    groups = seq_size // RING
    lane_at = lax.rem(seq, RING)
    group = seq // RING
    head_at = lax.rem(group, HEADS_HERE)
    block = group // HEADS_HERE
    after = lax.rem(seq + 1, seq_size)
    before = lax.rem(seq + seq_size - 1, seq_size)

    def head_peer(i):
        other = lax.rem(head_at + i, HEADS_HERE)
        return other, (block * HEADS_HERE + other) * RING + lane_at

    def group_peer(i):
        other = lax.rem(group + i, groups)
        return other, other * RING + lane_at

    def ring_peer(i):
        other = lax.rem(lane_at + i, RING)
        return group * RING + other

    def tp_peer(i):
        return lax.rem(tp + i, tp_size)

    def send(src, dst, send_sem, recv_sem, to_seq, to_tp):
        return pltpu.make_async_remote_copy(
            src_ref=src,
            dst_ref=dst,
            send_sem=send_sem,
            recv_sem=recv_sem,
            device_id=(to_seq, to_tp),
            device_id_type=MESH,
        )

    near = [
        pltpu.make_async_copy(src, dst, near_sem.at[i])
        for i, (src, dst) in enumerate(
            (
                (key_hbm, key),
                (value_hbm, value),
                (query_hbm, query),
                (frames_hbm, frames),
            )
        )
    ]
    weights = [
        pltpu.make_async_copy(src, dst, weight_sem.at[i])
        for i, (src, dst) in enumerate(
            (
                (w_in_hbm, w_in),
                (w_conv_hbm, w_conv),
                (w_proj_hbm, w_proj),
                (w_blend_hbm, w_blend),
                (w_merge_hbm, w_merge),
                (w_out_hbm, w_out),
            )
        )
    ]
    for copy in near + weights:
        copy.start()

    barrier = pltpu.get_barrier_semaphore()

    def greet(to_seq, to_tp):
        pl.semaphore_signal(barrier, inc=1, device_id=(to_seq, to_tp), device_id_type=MESH)

    @pl.loop(1, groups)
    def _(i):
        greet(group_peer(i)[1], tp)

    @pl.loop(1, RING)
    def _(i):
        greet(ring_peer(i), tp)

    @pl.loop(1, tp_size)
    def _(i):
        greet(seq, tp_peer(i))

    @pl.loop(0, tp_size)
    def _(i):
        greet(after, i)
        greet(before, i)

    for copy in near[:3]:
        copy.wait()
    low = low_lanes(rows)
    for pair in range(HEADS_HERE // 2):
        lanes = pl.ds(pair * 128, 128)
        k2 = key[:, lanes].astype(F32)
        v2 = value[:, lanes].astype(F32)
        q2 = query[:, lanes].astype(F32)
        kv_send[2 * pair] = jnp.where(low, k2, pltpu.roll(v2, HEAD, 1)).astype(BF16)
        kv_send[2 * pair + 1] = jnp.where(low, pltpu.roll(k2, HEAD, 1), v2).astype(BF16)
        q_send[2 * pair] = jnp.where(low, q2, 0.0).astype(BF16)
        q_send[2 * pair + 1] = jnp.where(low, pltpu.roll(q2, HEAD, 1), 0.0).astype(BF16)
    kv_all[lane_at, head_at] = kv_send[head_at]
    q_all[group] = q_send[head_at]

    pl.semaphore_wait(barrier, (groups - 1) + (RING - 1) + (tp_size - 1) + 2 * tp_size)

    def kv_copy(i):
        other, to = head_peer(i)
        return send(
            kv_send.at[other], kv_all.at[lane_at, head_at], kv_ss.at[i], kv_rs.at[i], to, tp
        )

    def q_copy(i):
        other, to = group_peer(i)
        return send(
            q_send.at[lax.rem(other, HEADS_HERE)],
            q_all.at[group],
            q_ss.at[i],
            q_rs.at[i],
            to,
            tp,
        )

    def ring_copy(i):
        return send(
            kv_all.at[lane_at], kv_all.at[lane_at], ring_ss.at[i], ring_rs.at[i], ring_peer(i), tp
        )

    @pl.loop(1, HEADS_HERE)
    def _(i):
        kv_copy(i).start()

    @pl.loop(1, groups)
    def _(i):
        q_copy(i).start()

    near[3].wait()
    features = frames[...].astype(F32)
    centered = features - jnp.mean(features, -1, keepdims=True)
    variance = jnp.mean(centered * centered, -1, keepdims=True)
    normed = (centered * lax.rsqrt(variance + 1e-05)).astype(BF16)

    @pl.loop(1, HEADS_HERE)
    def _(i):
        kv_copy(i).wait_recv()

    @pl.loop(1, RING)
    def _(i):
        ring_copy(i).start()

    weights[0].wait()

    def hidden_half(half):
        product = jnp.dot(normed, w_in[:, half, :], preferred_element_type=F32)
        return (0.5 * product * (1.0 + lax.erf(product * 0.7071067811865476))).astype(BF16)

    gate = hidden_half(1)
    gate_half[...] = gate
    gate_float = gate.astype(F32)
    sums = jnp.sum(gate_float, -1, keepdims=True)
    squares = jnp.sum(gate_float * gate_float, -1, keepdims=True)
    stat_send[...] = jnp.where(low, sums, squares)

    tail = pl.ds(rows - HALO, HALO)
    head = pl.ds(0, HALO)

    def gate_copies():
        return (
            send(gate_half.at[tail], gate_prev, gate_ss.at[0], gate_rs.at[0], after, tp),
            send(gate_half.at[head], gate_next, gate_ss.at[1], gate_rs.at[1], before, tp),
        )

    def stat_copy(i):
        return send(
            stat_send, stat_recv.at[tp], stat_ss.at[i], stat_rs.at[i], seq, tp_peer(i)
        )

    def stat_halo(i):
        to = tp_peer(i)
        return (
            send(
                stat_send.at[tail], stat_prev.at[tp], stat_hs.at[0, i], stat_hr.at[0, i], after, to
            ),
            send(
                stat_send.at[head], stat_next.at[tp], stat_hs.at[1, i], stat_hr.at[1, i], before, to
            ),
        )

    @pl.loop(1, tp_size)
    def _(i):
        stat_copy(i).start()

    @pl.loop(0, tp_size)
    def _(i):
        for copy in stat_halo(i):
            copy.start()

    for copy in gate_copies():
        copy.start()
    stat_recv[tp] = stat_send[...]

    resid_half[...] = hidden_half(0)

    @pl.loop(1, tp_size)
    def _(i):
        stat_copy(i).wait_recv()

    @pl.loop(0, tp_size)
    def _(i):
        for copy in stat_halo(i):
            copy.wait_recv()

    for copy in gate_copies():
        copy.wait_recv()

    def gate_normed(part, stats, keep):
        total = jnp.sum(stats[...], 0)
        average = total[:, 0:1] / CH
        variance = total[:, HEAD : HEAD + 1] / CH - average * average
        result = (part[...].astype(F32) - average) * lax.rsqrt(variance + 1e-05)
        result = result.astype(BF16).astype(F32)
        return result if keep is None else jnp.where(keep, result, 0.0)

    first, last = seq == 0, seq == seq_size - 1
    gate_pad[pl.ds(0, HALO)] = gate_normed(gate_prev, stat_prev, jnp.logical_not(first))
    gate_pad[pl.ds(HALO, rows)] = gate_normed(gate_half, stat_recv, None)
    gate_pad[pl.ds(HALO + rows, HALO)] = gate_normed(gate_next, stat_next, jnp.logical_not(last))
    weights[1].wait()
    weights[2].wait()
    cg_part = jnp.zeros((rows, w_proj.shape[1]), F32)
    gated = []
    for column in range(0, resid_half.shape[1], 128):
        conv = depthwise(gate_pad, w_conv, column, rows)
        resid = resid_half[:, pl.ds(column, 128)].astype(F32)
        gated.append((resid * conv).astype(BF16))
    cg_part = jnp.dot(jnp.concatenate(gated, 1), w_proj[...], preferred_element_type=F32)

    width = out.shape[1]

    def part_copy(which, i):
        to = tp_peer(i)
        return send(
            part_send.at[which, to],
            part_recv.at[which, tp],
            part_ss.at[which, i],
            part_rs.at[which, i],
            seq,
            to,
        )

    def part_halo(which, i):
        to = tp_peer(i)
        return (
            send(
                part_send.at[which, to, tail],
                part_prev.at[which, tp],
                part_hs.at[which, 0, i],
                part_hr.at[which, 0, i],
                after,
                to,
            ),
            send(
                part_send.at[which, to, head],
                part_next.at[which, tp],
                part_hs.at[which, 1, i],
                part_hr.at[which, 1, i],
                before,
                to,
            ),
        )

    def scatter_part(which, part):
        for i in range(tp_size):
            part_send[which, i] = part[:, i * width : (i + 1) * width].astype(BF16)

        @pl.loop(1, tp_size)
        def _(i):
            part_copy(which, i).start()

        @pl.loop(0, tp_size)
        def _(i):
            for copy in part_halo(which, i):
                copy.start()

        part_recv[which, tp] = part_send[which, tp]

    def merge_part(which):
        @pl.loop(1, tp_size)
        def _(i):
            part_copy(which, i).wait_recv()

        @pl.loop(0, tp_size)
        def _(i):
            for copy in part_halo(which, i):
                copy.wait_recv()

        def joined(ref):
            return jnp.sum(ref[which].astype(F32), 0).astype(BF16).astype(F32)

        own = joined(part_recv)
        blend_pad[pl.ds(0, HALO)] = jnp.where(first, 0.0, joined(part_prev))
        blend_pad[pl.ds(HALO, rows)] = own
        blend_pad[pl.ds(HALO + rows, HALO)] = jnp.where(last, 0.0, joined(part_next))
        taps_pad[...] = w_blend[:, which, :]
        mixture = [
            (own[:, c : c + 128] + depthwise(blend_pad, taps_pad, c, rows)).astype(BF16)
            for c in range(0, width, 128)
        ]
        return jnp.dot(jnp.concatenate(mixture, 1), w_merge[which], preferred_element_type=F32)

    scatter_part(1, cg_part)

    @pl.loop(1, groups)
    def _(i):
        q_copy(i).wait_recv()

    @pl.loop(1, RING)
    def _(i):
        ring_copy(i).wait_recv()

    keys = RING * HEADS_HERE * rows
    kv = kv_all[...].reshape(keys, 128)
    kv_ones[...] = jnp.where(low_lanes(keys), jnp.ones((), BF16), kv)

    def o_copy(other):
        return send(
            o_send.at[other], o_recv.at[group], o_ss.at[other], o_rs.at[group], other * RING + lane_at, tp
        )

    per_step = 4

    @pl.loop(0, groups // per_step)
    def _(step):
        count = per_step * rows
        q = q_all[pl.ds(step * per_step, per_step)].reshape(count, 128)
        kv = kv_all[...].reshape(keys, 128)
        scores = lax.dot_general(q, kv, (((1,), (1,)), ((), ())), preferred_element_type=F32)
        peak = jnp.max(scores, -1, keepdims=True)
        weight = jnp.exp2((scores - peak) * (LOG2E * HEAD**-0.5)).astype(BF16)
        mixed = jnp.dot(weight, kv_ones[...], preferred_element_type=F32)
        low_q = low_lanes(count)
        total = jnp.where(low_q, mixed, pltpu.roll(mixed, HEAD, 1))
        level = peak * HEAD**-0.5 + jnp.log(total)
        level_high = level.astype(BF16).astype(F32)
        lane = lax.broadcasted_iota(jnp.int32, (count, 128), 1)
        packed = jnp.where(
            low_q,
            jnp.where(lane < HEAD // 2, level_high, level - level_high),
            mixed / total,
        ).astype(BF16)
        o_send[pl.ds(step * per_step, per_step)] = packed.reshape(per_step, rows, 128)
        for i in range(per_step):
            other = step * per_step + i

            @pl.when(other != group)
            def _():
                o_copy(other).start()

            @pl.when(other == group)
            def _():
                o_recv[other] = o_send[other]

    for i in (3, 4):
        weights[i].wait()
    fin_acc[...] = merge_part(1)
    weights[5].wait()

    def o_arrival(other):
        return send(
            o_send.at[other], o_recv.at[other], o_ss.at[other], o_rs.at[other], other * RING + lane_at, tp
        )

    @pl.loop(1, groups)
    def _(i):
        o_arrival(group_peer(i)[0]).wait_recv()

    heads = []
    for h in range(HEADS_HERE):
        pieces = [
            o_recv[b * HEADS_HERE + h].astype(F32) for b in range(groups // HEADS_HERE)
        ]
        levels = [p[:, 0:1] + p[:, HEAD // 2 : HEAD // 2 + 1] for p in pieces]
        peak = functools.reduce(jnp.maximum, levels)
        shares = [jnp.exp(level - peak) for level in levels]
        whole = functools.reduce(jnp.add, shares)
        mixed = functools.reduce(jnp.add, [s * p for s, p in zip(shares, pieces)])
        heads.append(mixed / whole)
    attended = jnp.concatenate(
        [
            jnp.where(low, pltpu.roll(heads[2 * pair], HEAD, 1), heads[2 * pair + 1]).astype(BF16)
            for pair in range(HEADS_HERE // 2)
        ],
        1,
    )
    scatter_part(0, jnp.dot(attended, w_out[...], preferred_element_type=F32))
    merged = fin_acc[...] + merge_part(0)

    def fin_copy(i):
        to = tp_peer(i)
        return send(fin_send.at[to], fin_recv.at[tp], fin_ss.at[i], fin_rs.at[i], seq, to)

    for i in range(tp_size):
        fin_send[i] = merged[:, i * width : (i + 1) * width].astype(BF16)

    @pl.loop(1, tp_size)
    def _(i):
        fin_copy(i).start()

    fin_recv[tp] = fin_send[tp]

    @pl.loop(1, tp_size)
    def _(i):
        fin_copy(i).wait_recv()

    own = frames[:, pl.ds(pl.multiple_of(tp * width, width), width)].astype(F32)
    out[...] = (own + jnp.sum(fin_recv[...].astype(F32), 0)).astype(BF16)

    @pl.loop(1, HEADS_HERE)
    def _(i):
        kv_copy(i).wait_send()

    @pl.loop(1, groups)
    def _(i):
        q_copy(i).wait_send()
        o_arrival(group_peer(i)[0]).wait_send()

    @pl.loop(1, RING)
    def _(i):
        ring_copy(i).wait_send()

    for copy in gate_copies():
        copy.wait_send()

    @pl.loop(1, tp_size)
    def _(i):
        stat_copy(i).wait_send()
        part_copy(0, i).wait_send()
        part_copy(1, i).wait_send()
        fin_copy(i).wait_send()

    @pl.loop(0, tp_size)
    def _(i):
        for copy in stat_halo(i) + part_halo(0, i) + part_halo(1, i):
            copy.wait_send()


def solution(mesh):
    seq_size, tp_size = mesh.shape["seq"], mesh.shape["tp"]

    def on_device(*args):
        frames, query, key, value, w_out, w_in, w_conv, w_proj, w_blend, w_merge = args
        rows, width = query.shape
        features = frames.shape[1]
        units = w_in.shape[2]
        groups = seq_size // RING
        wide = rows + 2 * HALO
        dma = pltpu.SemaphoreType.DMA
        vmem = pltpu.VMEM
        return pl.pallas_call(
            functools.partial(kernel, seq_size, tp_size),
            out_shape=jax.ShapeDtypeStruct((rows, width), BF16),
            in_specs=[pl.BlockSpec(memory_space=pltpu.HBM)] * 10,
            out_specs=pl.BlockSpec(memory_space=pltpu.VMEM),
            scratch_shapes=[
                vmem(frames.shape, BF16),
                vmem(query.shape, BF16),
                vmem(key.shape, BF16),
                vmem(value.shape, BF16),
                vmem(w_out.shape, BF16),
                vmem(w_in.shape, BF16),
                vmem(w_conv.shape, F32),
                vmem(w_proj.shape, BF16),
                vmem(w_blend.shape, F32),
                vmem(w_merge.shape, BF16),
                vmem((HEADS_HERE, rows, 128), BF16),
                vmem((HEADS_HERE, rows, 128), BF16),
                vmem((RING, HEADS_HERE, rows, 128), BF16),
                vmem((RING * HEADS_HERE * rows, 128), BF16),
                vmem((groups, rows, 128), BF16),
                vmem((groups, rows, 128), BF16),
                vmem((groups, rows, 128), BF16),
                vmem((rows, units), BF16),
                vmem((rows, units), BF16),
                vmem((HALO, units), BF16),
                vmem((HALO, units), BF16),
                vmem((rows, 128), F32),
                vmem((tp_size, rows, 128), F32),
                vmem((tp_size, HALO, 128), F32),
                vmem((tp_size, HALO, 128), F32),
                vmem((wide, units), F32),
                vmem((2, tp_size, rows, width), BF16),
                vmem((2, tp_size, rows, width), BF16),
                vmem((2, tp_size, HALO, width), BF16),
                vmem((2, tp_size, HALO, width), BF16),
                vmem((wide, width), F32),
                vmem((TAPS, width), F32),
                vmem((rows, features), F32),
                vmem((tp_size, rows, width), BF16),
                vmem((tp_size, rows, width), BF16),
                dma((4,)),
                dma((6,)),
                dma((HEADS_HERE,)),
                dma((HEADS_HERE,)),
                dma((RING,)),
                dma((RING,)),
                dma((groups,)),
                dma((groups,)),
                dma((groups,)),
                dma((groups,)),
                dma((2,)),
                dma((2,)),
                dma((tp_size,)),
                dma((tp_size,)),
                dma((2, tp_size)),
                dma((2, tp_size)),
                dma((2, tp_size)),
                dma((2, tp_size)),
                dma((2, 2, tp_size)),
                dma((2, 2, tp_size)),
                dma((tp_size,)),
                dma((tp_size,)),
            ],
            compiler_params=pltpu.CompilerParams(
                collective_id=0,
                has_side_effects=True,
                vmem_limit_bytes=63 * 1024 * 1024,
            ),
        )(*args)

    return jax.shard_map(
        on_device,
        mesh=mesh,
        in_specs=(
            P("seq", None),
            P("seq", "tp"),
            P("seq", "tp"),
            P("seq", "tp"),
            P("tp", None),
            P(None, None, "tp"),
            P(None, "tp"),
            P("tp", None),
            P(None, None, "tp"),
            P(None, "tp", None),
        ),
        out_specs=P("seq", "tp"),
        check_vma=False,
    )
```

```python
import functools

import jax
import jax.numpy as jnp
from jax import lax
from jax.experimental import pallas as pl
from jax.experimental.pallas import tpu as pltpu
from jax.sharding import PartitionSpec as P

HEAD = 64
CH = 2048
TAPS = 31
HALO = 16
HEADS_HERE = 4
RING = 8
DEPTH = 8
LOG2E = 1.4426950408889634
LN2 = 0.6931471805599453
F32 = jnp.float32
BF16 = jnp.bfloat16
MESH = pl.DeviceIdType.MESH


def low_lanes(rows):
    return lax.broadcasted_iota(jnp.int32, (rows, 128), 1) < HEAD


def depthwise(pad_ref, taps_ref, column, rows):
    lanes = pl.ds(column, 128)
    total = jnp.zeros((rows, 128), F32)
    for phase in range(8):
        shifted = pad_ref[pl.ds(phase, rows + 24 if phase else rows + 32), lanes]
        for start in range(0, 33, 8):
            j = start + phase - 1
            if 0 <= j < TAPS:
                total = total + taps_ref[pl.ds(j, 1), lanes] * shifted[start : start + rows]
    return total


def kernel(
    seq_size,
    tp_size,
    frames_hbm,
    query_hbm,
    key_hbm,
    value_hbm,
    w_out_hbm,
    w_in_hbm,
    w_conv_hbm,
    w_proj_hbm,
    w_blend_hbm,
    w_merge_hbm,
    out,
    frames,
    query,
    key,
    value,
    w_out,
    w_in,
    w_conv,
    w_proj,
    w_blend,
    w_merge,
    kv_send,
    q_send,
    kv_all,
    kv_ones,
    q_all,
    o_send,
    o_recv,
    gate_half,
    resid_half,
    gate_prev,
    gate_next,
    stat_send,
    stat_recv,
    stat_prev,
    stat_next,
    gate_pad,
    part_send,
    part_recv,
    part_prev,
    part_next,
    blend_pad,
    taps_pad,
    fin_acc,
    fin_send,
    fin_recv,
    near_sem,
    weight_sem,
    kv_ss,
    kv_rs,
    q_ss,
    q_rs,
    o_ss,
    o_rs,
    gate_ss,
    gate_rs,
    stat_ss,
    stat_rs,
    stat_hs,
    stat_hr,
    part_ss,
    part_rs,
    part_hs,
    part_hr,
    fin_ss,
    fin_rs,
):
    rows = query.shape[0]
    wide = rows + 2 * HALO
    seq = lax.axis_index("seq")
    tp = lax.axis_index("tp")
    groups = 2 * DEPTH
    sides = seq_size // (RING * DEPTH)
    sources = sides * 2 * RING
    y_at = lax.rem(seq, RING)
    z_at = lax.rem(seq // RING, DEPTH)
    x_at = seq // (RING * DEPTH)
    group = 2 * z_at + lax.rem(y_at, 2)
    head_at = lax.rem(group, HEADS_HERE)
    source = (x_at * 2 + lax.rem(z_at, 2)) * RING + y_at
    after = lax.rem(seq + 1, seq_size)
    before = lax.rem(seq + seq_size - 1, seq_size)

    def group_seq(other):
        return (x_at * DEPTH + other // 2) * RING + 2 * (y_at // 2) + lax.rem(other, 2)

    def group_peer(i):
        other = lax.rem(group + i, groups)
        return other, group_seq(other)

    def key_peer(i):
        y = lax.rem(y_at + lax.rem(i, RING), RING)
        z_low = lax.rem(z_at + lax.rem(i // RING, 2), 2)
        x = lax.rem(x_at + i // (2 * RING), sides)
        return 2 * z_low + lax.rem(y, 2), (x * DEPTH + 2 * (z_at // 2) + z_low) * RING + y

    def tp_peer(i):
        return lax.rem(tp + i, tp_size)

    def send(src, dst, send_sem, recv_sem, to_seq, to_tp):
        return pltpu.make_async_remote_copy(
            src_ref=src,
            dst_ref=dst,
            send_sem=send_sem,
            recv_sem=recv_sem,
            device_id=(to_seq, to_tp),
            device_id_type=MESH,
        )

    near = [
        pltpu.make_async_copy(src, dst, near_sem.at[i])
        for i, (src, dst) in enumerate(
            (
                (key_hbm, key),
                (value_hbm, value),
                (query_hbm, query),
                (frames_hbm, frames),
            )
        )
    ]
    weights = [
        pltpu.make_async_copy(src, dst, weight_sem.at[i])
        for i, (src, dst) in enumerate(
            (
                (w_in_hbm, w_in),
                (w_conv_hbm, w_conv),
                (w_proj_hbm, w_proj),
                (w_blend_hbm, w_blend),
                (w_merge_hbm, w_merge),
                (w_out_hbm, w_out),
            )
        )
    ]
    for copy in near + weights:
        copy.start()

    barrier = pltpu.get_barrier_semaphore()

    def greet(to_seq, to_tp):
        pl.semaphore_signal(barrier, inc=1, device_id=(to_seq, to_tp), device_id_type=MESH)

    @pl.loop(1, groups)
    def _(i):
        greet(group_peer(i)[1], tp)

    @pl.loop(1, sources)
    def _(i):
        greet(key_peer(i)[1], tp)

    @pl.loop(1, tp_size)
    def _(i):
        greet(seq, tp_peer(i))

    @pl.loop(0, tp_size)
    def _(i):
        greet(after, i)
        greet(before, i)

    for copy in near[:3]:
        copy.wait()
    low = low_lanes(rows)
    for pair in range(HEADS_HERE // 2):
        lanes = pl.ds(pair * 128, 128)
        k2 = key[:, lanes].astype(F32)
        v2 = value[:, lanes].astype(F32)
        q2 = query[:, lanes].astype(F32)
        kv_send[2 * pair] = jnp.where(low, k2, pltpu.roll(v2, HEAD, 1)).astype(BF16)
        kv_send[2 * pair + 1] = jnp.where(low, pltpu.roll(k2, HEAD, 1), v2).astype(BF16)
        for h, q in ((2 * pair, q2), (2 * pair + 1, pltpu.roll(q2, HEAD, 1))):
            q_send[h, pl.ds(0, HALO)] = jnp.where(
                low_lanes(HALO), q[:HALO], pltpu.roll(q[2 * HALO :], HEAD, 1)
            ).astype(BF16)
            q_send[h, pl.ds(HALO, HALO)] = q[HALO : 2 * HALO].astype(BF16)
    kv_all[source] = kv_send[head_at]
    q_all[group] = q_send[head_at]

    pl.semaphore_wait(barrier, (groups - 1) + (sources - 1) + (tp_size - 1) + 2 * tp_size)

    def kv_copy(i):
        other, to = key_peer(i)
        return send(kv_send.at[other], kv_all.at[source], kv_ss.at[i], kv_rs.at[i], to, tp)

    def q_copy(i):
        other, to = group_peer(i)
        return send(
            q_send.at[lax.rem(other, HEADS_HERE)],
            q_all.at[group],
            q_ss.at[i],
            q_rs.at[i],
            to,
            tp,
        )

    order = sorted(
        range(1, sources), key=lambda i: -(min(i % RING, RING - i % RING) + 2 * (i // (2 * RING)))
    )
    for i in order:
        kv_copy(i).start()

    @pl.loop(1, groups)
    def _(i):
        q_copy(i).start()

    near[3].wait()
    features = frames[...].astype(F32)
    centered = features - jnp.mean(features, -1, keepdims=True)
    variance = jnp.mean(centered * centered, -1, keepdims=True)
    normed = (centered * lax.rsqrt(variance + 1e-05)).astype(BF16)

    weights[0].wait()

    def hidden_half(half):
        product = jnp.dot(normed, w_in[:, half, :], preferred_element_type=F32)
        return (0.5 * product * (1.0 + lax.erf(product * 0.7071067811865476))).astype(BF16)

    gate = hidden_half(1)
    gate_half[...] = gate
    gate_float = gate.astype(F32)
    sums = jnp.sum(gate_float, -1, keepdims=True)
    squares = jnp.sum(gate_float * gate_float, -1, keepdims=True)
    stat_lane = lax.broadcasted_iota(jnp.int32, (8, 128), 1)
    stats = jnp.zeros((8, 128), F32)
    for k in range(rows // 8):
        at = slice(8 * k, 8 * k + 8)
        stats = jnp.where(stat_lane // 8 == k, sums[at], stats)
        stats = jnp.where(stat_lane // 8 == 8 + k, squares[at], stats)
    stat_send[...] = stats

    tail = pl.ds(rows - HALO, HALO)
    head = pl.ds(0, HALO)

    def gate_copies():
        return (
            send(gate_half.at[tail], gate_prev, gate_ss.at[0], gate_rs.at[0], after, tp),
            send(gate_half.at[head], gate_next, gate_ss.at[1], gate_rs.at[1], before, tp),
        )

    def stat_copy(i):
        return send(
            stat_send, stat_recv.at[tp], stat_ss.at[i], stat_rs.at[i], seq, tp_peer(i)
        )

    def stat_halo(i):
        to = tp_peer(i)
        return (
            send(stat_send, stat_prev.at[tp], stat_hs.at[0, i], stat_hr.at[0, i], after, to),
            send(stat_send, stat_next.at[tp], stat_hs.at[1, i], stat_hr.at[1, i], before, to),
        )

    @pl.loop(1, tp_size)
    def _(i):
        stat_copy(i).start()

    @pl.loop(0, tp_size)
    def _(i):
        for copy in stat_halo(i):
            copy.start()

    for copy in gate_copies():
        copy.start()
    stat_recv[tp] = stat_send[...]

    resid_half[...] = hidden_half(0)

    @pl.loop(1, tp_size)
    def _(i):
        stat_copy(i).wait_recv()

    @pl.loop(0, tp_size)
    def _(i):
        for copy in stat_halo(i):
            copy.wait_recv()

    for copy in gate_copies():
        copy.wait_recv()

    def gate_normed(part, stats, blocks, keep):
        total = jnp.sum(stats[...], 0) / CH
        average = jnp.concatenate([total[:, 8 * k : 8 * k + 1] for k in blocks], 0)
        square = jnp.concatenate([total[:, HEAD + 8 * k : HEAD + 8 * k + 1] for k in blocks], 0)
        variance = square - average * average
        result = (part[...].astype(F32) - average) * lax.rsqrt(variance + 1e-05)
        result = result.astype(BF16).astype(F32)
        return result if keep is None else jnp.where(keep, result, 0.0)

    first, last = seq == 0, seq == seq_size - 1
    gate_pad[pl.ds(0, HALO)] = gate_normed(gate_prev, stat_prev, range(rows // 8 - 2, rows // 8), jnp.logical_not(first))
    gate_pad[pl.ds(HALO, rows)] = gate_normed(gate_half, stat_recv, range(rows // 8), None)
    gate_pad[pl.ds(HALO + rows, HALO)] = gate_normed(gate_next, stat_next, range(2), jnp.logical_not(last))
    weights[1].wait()
    weights[2].wait()
    cg_part = jnp.zeros((rows, w_proj.shape[1]), F32)
    gated = []
    for column in range(0, resid_half.shape[1], 128):
        conv = depthwise(gate_pad, w_conv, column, rows)
        resid = resid_half[:, pl.ds(column, 128)].astype(F32)
        gated.append((resid * conv).astype(BF16))
    cg_part = jnp.dot(jnp.concatenate(gated, 1), w_proj[...], preferred_element_type=F32)

    width = out.shape[1]

    def part_copy(which, i):
        to = tp_peer(i)
        return send(
            part_send.at[which, to],
            part_recv.at[which, tp],
            part_ss.at[which, i],
            part_rs.at[which, i],
            seq,
            to,
        )

    def part_halo(which, i):
        to = tp_peer(i)
        return (
            send(
                part_send.at[which, to, tail],
                part_prev.at[which, tp],
                part_hs.at[which, 0, i],
                part_hr.at[which, 0, i],
                after,
                to,
            ),
            send(
                part_send.at[which, to, head],
                part_next.at[which, tp],
                part_hs.at[which, 1, i],
                part_hr.at[which, 1, i],
                before,
                to,
            ),
        )

    def scatter_part(which, part):
        for i in range(tp_size):
            part_send[which, i] = part[:, i * width : (i + 1) * width].astype(BF16)

        @pl.loop(1, tp_size)
        def _(i):
            part_copy(which, i).start()

        @pl.loop(0, tp_size)
        def _(i):
            for copy in part_halo(which, i):
                copy.start()

        part_recv[which, tp] = part_send[which, tp]

    def merge_part(which):
        @pl.loop(1, tp_size)
        def _(i):
            part_copy(which, i).wait_recv()

        @pl.loop(0, tp_size)
        def _(i):
            for copy in part_halo(which, i):
                copy.wait_recv()

        def joined(ref):
            return jnp.sum(ref[which].astype(F32), 0).astype(BF16).astype(F32)

        own = joined(part_recv)
        blend_pad[pl.ds(0, HALO)] = jnp.where(first, 0.0, joined(part_prev))
        blend_pad[pl.ds(HALO, rows)] = own
        blend_pad[pl.ds(HALO + rows, HALO)] = jnp.where(last, 0.0, joined(part_next))
        taps_pad[...] = w_blend[:, which, :]
        mixture = [
            (own[:, c : c + 128] + depthwise(blend_pad, taps_pad, c, rows)).astype(BF16)
            for c in range(0, width, 128)
        ]
        return jnp.dot(jnp.concatenate(mixture, 1), w_merge[which], preferred_element_type=F32)

    scatter_part(1, cg_part)

    @pl.loop(1, groups)
    def _(i):
        q_copy(i).wait_recv()

    @pl.loop(1, sources)
    def _(i):
        kv_copy(i).wait_recv()

    keys = sources * rows
    kv = kv_all[...].reshape(keys, 128)
    kv_ones[...] = jnp.where(low_lanes(keys), jnp.ones((), BF16), kv)

    def o_copy(other):
        return send(
            o_send.at[other], o_recv.at[group], o_ss.at[other], o_rs.at[group], group_seq(other), tp
        )

    per_step = 4

    @pl.loop(0, groups // per_step)
    def _(step):
        count = per_step * rows
        pieces = []
        for i in range(per_step):
            q = q_all[step * per_step + i]
            q_end = pltpu.roll(q[:HALO].astype(F32), HEAD, 1).astype(BF16)
            pieces += [q, q_end]
        q = jnp.concatenate(pieces, 0)
        q = jnp.where(low_lanes(count), q, jnp.zeros((), BF16))
        kv = kv_all[...].reshape(keys, 128)
        scores = lax.dot_general(q, kv, (((1,), (1,)), ((), ())), preferred_element_type=F32)
        peak = jnp.max(scores, -1, keepdims=True)
        weight = jnp.exp2((scores - peak) * (LOG2E * HEAD**-0.5)).astype(BF16)
        mixed = jnp.dot(weight, kv_ones[...], preferred_element_type=F32)
        low_q = low_lanes(count)
        total = jnp.where(low_q, mixed, pltpu.roll(mixed, HEAD, 1))
        level = peak * HEAD**-0.5 + jnp.log(total)
        level_high = level.astype(BF16).astype(F32)
        level_low = level - level_high
        mixed = mixed / total
        lane = lax.broadcasted_iota(jnp.int32, (HALO, 128), 1)
        for i in range(per_step):
            thirds = [slice(i * rows + k * HALO, i * rows + (k + 1) * HALO) for k in range(3)]
            spare = jnp.zeros((HALO, 128), F32)
            for k, at in enumerate(thirds):
                spare = jnp.where(lane // 8 == 2 * k, level_high[at], spare)
                spare = jnp.where(lane // 8 == 2 * k + 1, level_low[at], spare)
            o_low = low_lanes(HALO)
            first_rows = jnp.where(o_low, pltpu.roll(mixed[thirds[2]], HEAD, 1), mixed[thirds[0]])
            other = step * per_step + i
            o_send[other, pl.ds(0, HALO)] = first_rows.astype(BF16)
            o_send[other, pl.ds(HALO, HALO)] = jnp.where(o_low, spare, mixed[thirds[1]]).astype(
                BF16
            )
        for i in range(per_step):
            other = step * per_step + i

            @pl.when(other != group)
            def _():
                o_copy(other).start()

            @pl.when(other == group)
            def _():
                o_recv[other] = o_send[other]

    for i in (3, 4):
        weights[i].wait()
    fin_acc[...] = merge_part(1)
    weights[5].wait()

    def o_arrival(other):
        return send(
            o_send.at[other], o_recv.at[other], o_ss.at[other], o_rs.at[other], group_seq(other), tp
        )

    @pl.loop(1, groups)
    def _(i):
        o_arrival(group_peer(i)[0]).wait_recv()

    heads = []
    for h in range(HEADS_HERE):
        pieces, levels = [], []
        for b in range(groups // HEADS_HERE):
            piece = o_recv[b * HEADS_HERE + h].astype(F32)
            spare = piece[HALO:]
            pieces.append(jnp.concatenate([piece, pltpu.roll(piece[:HALO], HEAD, 1)], 0))
            levels.append(
                jnp.concatenate(
                    [
                        spare[:, 16 * k : 16 * k + 1] + spare[:, 16 * k + 8 : 16 * k + 9]
                        for k in range(3)
                    ],
                    0,
                )
            )
        peak = functools.reduce(jnp.maximum, levels)
        shares = [jnp.exp(level - peak) for level in levels]
        whole = functools.reduce(jnp.add, shares)
        mixed = functools.reduce(jnp.add, [s * p for s, p in zip(shares, pieces)])
        heads.append(mixed / whole)
    attended = jnp.concatenate(
        [
            jnp.where(low, pltpu.roll(heads[2 * pair], HEAD, 1), heads[2 * pair + 1]).astype(BF16)
            for pair in range(HEADS_HERE // 2)
        ],
        1,
    )
    scatter_part(0, jnp.dot(attended, w_out[...], preferred_element_type=F32))
    merged = fin_acc[...] + merge_part(0)

    def fin_copy(i):
        to = tp_peer(i)
        return send(fin_send.at[to], fin_recv.at[tp], fin_ss.at[i], fin_rs.at[i], seq, to)

    for i in range(tp_size):
        fin_send[i] = merged[:, i * width : (i + 1) * width].astype(BF16)

    @pl.loop(1, tp_size)
    def _(i):
        fin_copy(i).start()

    fin_recv[tp] = fin_send[tp]

    @pl.loop(1, tp_size)
    def _(i):
        fin_copy(i).wait_recv()

    own = frames[:, pl.ds(pl.multiple_of(tp * width, width), width)].astype(F32)
    out[...] = (own + jnp.sum(fin_recv[...].astype(F32), 0)).astype(BF16)

    @pl.loop(1, sources)
    def _(i):
        kv_copy(i).wait_send()

    @pl.loop(1, groups)
    def _(i):
        q_copy(i).wait_send()
        o_arrival(group_peer(i)[0]).wait_send()

    for copy in gate_copies():
        copy.wait_send()

    @pl.loop(1, tp_size)
    def _(i):
        stat_copy(i).wait_send()
        part_copy(0, i).wait_send()
        part_copy(1, i).wait_send()
        fin_copy(i).wait_send()

    @pl.loop(0, tp_size)
    def _(i):
        for copy in stat_halo(i) + part_halo(0, i) + part_halo(1, i):
            copy.wait_send()


def solution(mesh):
    seq_size, tp_size = mesh.shape["seq"], mesh.shape["tp"]

    def on_device(*args):
        frames, query, key, value, w_out, w_in, w_conv, w_proj, w_blend, w_merge = args
        rows, width = query.shape
        features = frames.shape[1]
        units = w_in.shape[2]
        groups = 2 * DEPTH
        sources = seq_size // DEPTH * 2
        wide = rows + 2 * HALO
        dma = pltpu.SemaphoreType.DMA
        vmem = pltpu.VMEM
        return pl.pallas_call(
            functools.partial(kernel, seq_size, tp_size),
            out_shape=jax.ShapeDtypeStruct((rows, width), BF16),
            in_specs=[pl.BlockSpec(memory_space=pltpu.HBM)] * 10,
            out_specs=pl.BlockSpec(memory_space=pltpu.VMEM),
            scratch_shapes=[
                vmem(frames.shape, BF16),
                vmem(query.shape, BF16),
                vmem(key.shape, BF16),
                vmem(value.shape, BF16),
                vmem(w_out.shape, BF16),
                vmem(w_in.shape, BF16),
                vmem(w_conv.shape, F32),
                vmem(w_proj.shape, BF16),
                vmem(w_blend.shape, F32),
                vmem(w_merge.shape, BF16),
                vmem((HEADS_HERE, rows, 128), BF16),
                vmem((HEADS_HERE, 2 * HALO, 128), BF16),
                vmem((sources, rows, 128), BF16),
                vmem((sources * rows, 128), BF16),
                vmem((groups, 2 * HALO, 128), BF16),
                vmem((groups, 2 * HALO, 128), BF16),
                vmem((groups, 2 * HALO, 128), BF16),
                vmem((rows, units), BF16),
                vmem((rows, units), BF16),
                vmem((HALO, units), BF16),
                vmem((HALO, units), BF16),
                vmem((8, 128), F32),
                vmem((tp_size, 8, 128), F32),
                vmem((tp_size, 8, 128), F32),
                vmem((tp_size, 8, 128), F32),
                vmem((wide, units), F32),
                vmem((2, tp_size, rows, width), BF16),
                vmem((2, tp_size, rows, width), BF16),
                vmem((2, tp_size, HALO, width), BF16),
                vmem((2, tp_size, HALO, width), BF16),
                vmem((wide, width), F32),
                vmem((TAPS, width), F32),
                vmem((rows, features), F32),
                vmem((tp_size, rows, width), BF16),
                vmem((tp_size, rows, width), BF16),
                dma((4,)),
                dma((6,)),
                dma((sources,)),
                dma((sources,)),
                dma((groups,)),
                dma((groups,)),
                dma((groups,)),
                dma((groups,)),
                dma((2,)),
                dma((2,)),
                dma((tp_size,)),
                dma((tp_size,)),
                dma((2, tp_size)),
                dma((2, tp_size)),
                dma((2, tp_size)),
                dma((2, tp_size)),
                dma((2, 2, tp_size)),
                dma((2, 2, tp_size)),
                dma((tp_size,)),
                dma((tp_size,)),
            ],
            compiler_params=pltpu.CompilerParams(
                collective_id=0,
                has_side_effects=True,
                vmem_limit_bytes=63 * 1024 * 1024,
            ),
        )(*args)

    return jax.shard_map(
        on_device,
        mesh=mesh,
        in_specs=(
            P("seq", None),
            P("seq", "tp"),
            P("seq", "tp"),
            P("seq", "tp"),
            P("tp", None),
            P(None, None, "tp"),
            P(None, "tp"),
            P("tp", None),
            P(None, None, "tp"),
            P(None, "tp", None),
        ),
        out_specs=P("seq", "tp"),
        check_vma=False,
    )
```

```python
import functools

import jax
import jax.numpy as jnp
from jax import lax
from jax.experimental import pallas as pl
from jax.experimental.pallas import tpu as pltpu
from jax.sharding import PartitionSpec as P

HEAD = 64
CH = 2048
TAPS = 31
HALO = 16
HEADS_HERE = 4
RING = 8
DEPTH = 8
LOG2E = 1.4426950408889634
LN2 = 0.6931471805599453
F32 = jnp.float32
BF16 = jnp.bfloat16
MESH = pl.DeviceIdType.MESH


def low_lanes(rows):
    return lax.broadcasted_iota(jnp.int32, (rows, 128), 1) < HEAD


def depthwise(pad_ref, taps_ref, column, rows):
    lanes = pl.ds(column, 128)
    total = jnp.zeros((rows, 128), F32)
    for phase in range(8):
        shifted = pad_ref[pl.ds(phase, rows + 24 if phase else rows + 32), lanes]
        for start in range(0, 33, 8):
            j = start + phase - 1
            if 0 <= j < TAPS:
                total = total + taps_ref[pl.ds(j, 1), lanes] * shifted[start : start + rows]
    return total


def kernel(
    seq_size,
    tp_size,
    frames_hbm,
    query_hbm,
    key_hbm,
    value_hbm,
    w_out_hbm,
    w_in_hbm,
    w_conv_hbm,
    w_proj_hbm,
    w_blend_hbm,
    w_merge_hbm,
    out,
    frames,
    query,
    key,
    value,
    w_out,
    w_in,
    w_conv,
    w_proj,
    w_blend,
    w_merge,
    kv_send,
    q_send,
    kv_all,
    kv_ones,
    q_all,
    o_send,
    o_recv,
    gate_half,
    resid_half,
    gate_prev,
    gate_next,
    stat_send,
    stat_recv,
    stat_prev,
    stat_next,
    gate_pad,
    part_send,
    part_recv,
    part_prev,
    part_next,
    blend_pad,
    taps_pad,
    fin_acc,
    fin_send,
    fin_recv,
    near_sem,
    weight_sem,
    kv_ss,
    kv_rs,
    across_ss,
    across_rs,
    q_ss,
    q_rs,
    o_ss,
    o_rs,
    gate_ss,
    gate_rs,
    stat_ss,
    stat_rs,
    stat_hs,
    stat_hr,
    part_ss,
    part_rs,
    part_hs,
    part_hr,
    fin_ss,
    fin_rs,
):
    rows = query.shape[0]
    wide = rows + 2 * HALO
    seq = lax.axis_index("seq")
    tp = lax.axis_index("tp")
    groups = 2 * DEPTH
    sides = seq_size // (RING * DEPTH)
    nearby = 2 * RING
    y_at = lax.rem(seq, RING)
    z_at = lax.rem(seq // RING, DEPTH)
    x_at = seq // (RING * DEPTH)
    group = 2 * z_at + lax.rem(y_at, 2)
    head_at = lax.rem(group, HEADS_HERE)
    place = lax.rem(z_at, 2) * RING + y_at
    across = lax.rem(seq + RING * DEPTH, seq_size)
    after = lax.rem(seq + 1, seq_size)
    before = lax.rem(seq + seq_size - 1, seq_size)

    def group_seq(other):
        return (x_at * DEPTH + other // 2) * RING + 2 * (y_at // 2) + lax.rem(other, 2)

    def group_peer(i):
        other = lax.rem(group + i, groups)
        return other, group_seq(other)

    def key_peer(i):
        y = lax.rem(y_at + lax.rem(i, RING), RING)
        z_low = lax.rem(z_at + i // RING, 2)
        return 2 * z_low + lax.rem(y, 2), (x_at * DEPTH + 2 * (z_at // 2) + z_low) * RING + y

    def key_place(i):
        y = lax.rem(y_at + RING - lax.rem(i, RING), RING)
        return lax.rem(z_at + i // RING, 2) * RING + y

    def tp_peer(i):
        return lax.rem(tp + i, tp_size)

    def send(src, dst, send_sem, recv_sem, to_seq, to_tp):
        return pltpu.make_async_remote_copy(
            src_ref=src,
            dst_ref=dst,
            send_sem=send_sem,
            recv_sem=recv_sem,
            device_id=(to_seq, to_tp),
            device_id_type=MESH,
        )

    near = [
        pltpu.make_async_copy(src, dst, near_sem.at[i])
        for i, (src, dst) in enumerate(
            (
                (key_hbm, key),
                (value_hbm, value),
                (query_hbm, query),
                (frames_hbm, frames),
            )
        )
    ]
    weights = [
        pltpu.make_async_copy(src, dst, weight_sem.at[i])
        for i, (src, dst) in enumerate(
            (
                (w_in_hbm, w_in),
                (w_conv_hbm, w_conv),
                (w_proj_hbm, w_proj),
                (w_blend_hbm, w_blend),
                (w_merge_hbm, w_merge),
                (w_out_hbm, w_out),
            )
        )
    ]
    for copy in near + weights:
        copy.start()

    barrier = pltpu.get_barrier_semaphore()

    def greet(to_seq, to_tp):
        pl.semaphore_signal(barrier, inc=1, device_id=(to_seq, to_tp), device_id_type=MESH)

    @pl.loop(1, groups)
    def _(i):
        greet(group_peer(i)[1], tp)

    @pl.loop(1, nearby)
    def _(i):
        greet(key_peer(i)[1], tp)

    greet(across, tp)

    @pl.loop(1, tp_size)
    def _(i):
        greet(seq, tp_peer(i))

    @pl.loop(0, tp_size)
    def _(i):
        greet(after, i)
        greet(before, i)

    for copy in near[:3]:
        copy.wait()
    low = low_lanes(rows)
    for pair in range(HEADS_HERE // 2):
        lanes = pl.ds(pair * 128, 128)
        k2 = key[:, lanes].astype(F32)
        v2 = value[:, lanes].astype(F32)
        q2 = query[:, lanes].astype(F32)
        kv_send[2 * pair] = jnp.where(low, k2, pltpu.roll(v2, HEAD, 1)).astype(BF16)
        kv_send[2 * pair + 1] = jnp.where(low, pltpu.roll(k2, HEAD, 1), v2).astype(BF16)
        for h, q in ((2 * pair, q2), (2 * pair + 1, pltpu.roll(q2, HEAD, 1))):
            q_send[h, pl.ds(0, HALO)] = jnp.where(
                low_lanes(HALO), q[:HALO], pltpu.roll(q[2 * HALO :], HEAD, 1)
            ).astype(BF16)
            q_send[h, pl.ds(HALO, HALO)] = q[HALO : 2 * HALO].astype(BF16)
    kv_all[x_at * nearby + place] = kv_send[head_at]
    q_all[group] = q_send[head_at]

    pl.semaphore_wait(barrier, (groups - 1) + nearby + (tp_size - 1) + 2 * tp_size)

    def kv_copy(i):
        other, to = key_peer(i)
        return send(
            kv_send.at[other], kv_all.at[x_at * nearby + place], kv_ss.at[i], kv_rs.at[i], to, tp
        )

    def across_copy(at):
        slot = kv_all.at[x_at * nearby + at]
        return send(slot, slot, across_ss.at[at], across_rs.at[at], across, tp)

    def q_copy(i):
        other, to = group_peer(i)
        return send(
            q_send.at[lax.rem(other, HEADS_HERE)],
            q_all.at[group],
            q_ss.at[i],
            q_rs.at[i],
            to,
            tp,
        )

    def hops(kv, i):
        if kv:
            return min(i % RING, RING - i % RING) + i // RING
        return min(i // 2, DEPTH - i // 2) + i % 2

    order = [(kv, i) for kv in (True, False) for i in range(1, nearby)]
    for kv, i in sorted(order, key=lambda copy: -hops(*copy)):
        (kv_copy if kv else q_copy)(i).start()
    across_copy(place).start()

    near[3].wait()
    features = frames[...].astype(F32)
    centered = features - jnp.mean(features, -1, keepdims=True)
    variance = jnp.mean(centered * centered, -1, keepdims=True)
    normed = (centered * lax.rsqrt(variance + 1e-05)).astype(BF16)

    weights[0].wait()

    def hidden_half(half):
        product = jnp.dot(normed, w_in[:, half, :], preferred_element_type=F32)
        return (0.5 * product * (1.0 + lax.erf(product * 0.7071067811865476))).astype(BF16)

    gate = hidden_half(1)
    gate_half[...] = gate
    gate_float = gate.astype(F32)
    sums = jnp.sum(gate_float, -1, keepdims=True)
    squares = jnp.sum(gate_float * gate_float, -1, keepdims=True)
    stat_lane = lax.broadcasted_iota(jnp.int32, (8, 128), 1)
    stats = jnp.zeros((8, 128), F32)
    for k in range(rows // 8):
        at = slice(8 * k, 8 * k + 8)
        stats = jnp.where(stat_lane // 8 == k, sums[at], stats)
        stats = jnp.where(stat_lane // 8 == 8 + k, squares[at], stats)
    stat_send[...] = stats

    tail = pl.ds(rows - HALO, HALO)
    head = pl.ds(0, HALO)

    def gate_copies():
        return (
            send(gate_half.at[tail], gate_prev, gate_ss.at[0], gate_rs.at[0], after, tp),
            send(gate_half.at[head], gate_next, gate_ss.at[1], gate_rs.at[1], before, tp),
        )

    def stat_copy(i):
        return send(
            stat_send, stat_recv.at[tp], stat_ss.at[i], stat_rs.at[i], seq, tp_peer(i)
        )

    def stat_halo(i):
        to = tp_peer(i)
        return (
            send(stat_send, stat_prev.at[tp], stat_hs.at[0, i], stat_hr.at[0, i], after, to),
            send(stat_send, stat_next.at[tp], stat_hs.at[1, i], stat_hr.at[1, i], before, to),
        )

    @pl.loop(1, tp_size)
    def _(i):
        stat_copy(i).start()

    @pl.loop(0, tp_size)
    def _(i):
        for copy in stat_halo(i):
            copy.start()

    for copy in gate_copies():
        copy.start()
    stat_recv[tp] = stat_send[...]

    resid_half[...] = hidden_half(0)

    for i in sorted(range(1, nearby), key=lambda i: hops(True, i)):
        kv_copy(i).wait_recv()
        across_copy(key_place(i)).start()

    @pl.loop(1, tp_size)
    def _(i):
        stat_copy(i).wait_recv()

    @pl.loop(0, tp_size)
    def _(i):
        for copy in stat_halo(i):
            copy.wait_recv()

    for copy in gate_copies():
        copy.wait_recv()

    def gate_normed(part, stats, blocks, keep):
        total = jnp.sum(stats[...], 0) / CH
        average = jnp.concatenate([total[:, 8 * k : 8 * k + 1] for k in blocks], 0)
        square = jnp.concatenate([total[:, HEAD + 8 * k : HEAD + 8 * k + 1] for k in blocks], 0)
        variance = square - average * average
        result = (part[...].astype(F32) - average) * lax.rsqrt(variance + 1e-05)
        result = result.astype(BF16).astype(F32)
        return result if keep is None else jnp.where(keep, result, 0.0)

    first, last = seq == 0, seq == seq_size - 1
    gate_pad[pl.ds(0, HALO)] = gate_normed(gate_prev, stat_prev, range(rows // 8 - 2, rows // 8), jnp.logical_not(first))
    gate_pad[pl.ds(HALO, rows)] = gate_normed(gate_half, stat_recv, range(rows // 8), None)
    gate_pad[pl.ds(HALO + rows, HALO)] = gate_normed(gate_next, stat_next, range(2), jnp.logical_not(last))
    weights[1].wait()
    weights[2].wait()
    cg_part = jnp.zeros((rows, w_proj.shape[1]), F32)
    gated = []
    for column in range(0, resid_half.shape[1], 128):
        conv = depthwise(gate_pad, w_conv, column, rows)
        resid = resid_half[:, pl.ds(column, 128)].astype(F32)
        gated.append((resid * conv).astype(BF16))
    cg_part = jnp.dot(jnp.concatenate(gated, 1), w_proj[...], preferred_element_type=F32)

    width = out.shape[1]

    def part_copy(which, i):
        to = tp_peer(i)
        return send(
            part_send.at[which, to],
            part_recv.at[which, tp],
            part_ss.at[which, i],
            part_rs.at[which, i],
            seq,
            to,
        )

    def part_halo(which, i):
        to = tp_peer(i)
        return (
            send(
                part_send.at[which, to, tail],
                part_prev.at[which, tp],
                part_hs.at[which, 0, i],
                part_hr.at[which, 0, i],
                after,
                to,
            ),
            send(
                part_send.at[which, to, head],
                part_next.at[which, tp],
                part_hs.at[which, 1, i],
                part_hr.at[which, 1, i],
                before,
                to,
            ),
        )

    def scatter_part(which, part):
        for i in range(tp_size):
            part_send[which, i] = part[:, i * width : (i + 1) * width].astype(BF16)

        @pl.loop(1, tp_size)
        def _(i):
            part_copy(which, i).start()

        @pl.loop(0, tp_size)
        def _(i):
            for copy in part_halo(which, i):
                copy.start()

        part_recv[which, tp] = part_send[which, tp]

    def merge_part(which):
        @pl.loop(1, tp_size)
        def _(i):
            part_copy(which, i).wait_recv()

        @pl.loop(0, tp_size)
        def _(i):
            for copy in part_halo(which, i):
                copy.wait_recv()

        def joined(ref):
            return jnp.sum(ref[which].astype(F32), 0).astype(BF16).astype(F32)

        own = joined(part_recv)
        blend_pad[pl.ds(0, HALO)] = jnp.where(first, 0.0, joined(part_prev))
        blend_pad[pl.ds(HALO, rows)] = own
        blend_pad[pl.ds(HALO + rows, HALO)] = jnp.where(last, 0.0, joined(part_next))
        taps_pad[...] = w_blend[:, which, :]
        mixture = [
            (own[:, c : c + 128] + depthwise(blend_pad, taps_pad, c, rows)).astype(BF16)
            for c in range(0, width, 128)
        ]
        return jnp.dot(jnp.concatenate(mixture, 1), w_merge[which], preferred_element_type=F32)

    scatter_part(1, cg_part)

    @pl.loop(1, groups)
    def _(i):
        q_copy(i).wait_recv()

    @pl.loop(0, nearby)
    def _(i):
        across_copy(i).wait_recv()

    keys = sides * nearby * rows
    kv = kv_all[...].reshape(keys, 128)
    kv_ones[...] = jnp.where(low_lanes(keys), jnp.ones((), BF16), kv)

    def o_copy(other):
        return send(
            o_send.at[other], o_recv.at[group], o_ss.at[other], o_rs.at[group], group_seq(other), tp
        )

    per_step = 4

    @pl.loop(0, groups // per_step)
    def _(step):
        count = per_step * rows
        pieces = []
        for i in range(per_step):
            q = q_all[step * per_step + i]
            q_end = pltpu.roll(q[:HALO].astype(F32), HEAD, 1).astype(BF16)
            pieces += [q, q_end]
        q = jnp.concatenate(pieces, 0)
        q = jnp.where(low_lanes(count), q, jnp.zeros((), BF16))
        kv = kv_all[...].reshape(keys, 128)
        scores = lax.dot_general(q, kv, (((1,), (1,)), ((), ())), preferred_element_type=F32)
        peak = jnp.max(scores, -1, keepdims=True)
        weight = jnp.exp2((scores - peak) * (LOG2E * HEAD**-0.5)).astype(BF16)
        mixed = jnp.dot(weight, kv_ones[...], preferred_element_type=F32)
        low_q = low_lanes(count)
        total = jnp.where(low_q, mixed, pltpu.roll(mixed, HEAD, 1))
        level = peak * HEAD**-0.5 + jnp.log(total)
        level_high = level.astype(BF16).astype(F32)
        level_low = level - level_high
        mixed = mixed / total
        lane = lax.broadcasted_iota(jnp.int32, (HALO, 128), 1)
        for i in range(per_step):
            thirds = [slice(i * rows + k * HALO, i * rows + (k + 1) * HALO) for k in range(3)]
            spare = jnp.zeros((HALO, 128), F32)
            for k, at in enumerate(thirds):
                spare = jnp.where(lane // 8 == 2 * k, level_high[at], spare)
                spare = jnp.where(lane // 8 == 2 * k + 1, level_low[at], spare)
            o_low = low_lanes(HALO)
            first_rows = jnp.where(o_low, pltpu.roll(mixed[thirds[2]], HEAD, 1), mixed[thirds[0]])
            other = step * per_step + i
            o_send[other, pl.ds(0, HALO)] = first_rows.astype(BF16)
            o_send[other, pl.ds(HALO, HALO)] = jnp.where(o_low, spare, mixed[thirds[1]]).astype(
                BF16
            )
        for i in range(per_step):
            other = step * per_step + i

            @pl.when(other != group)
            def _():
                o_copy(other).start()

            @pl.when(other == group)
            def _():
                o_recv[other] = o_send[other]

    for i in (3, 4):
        weights[i].wait()
    fin_acc[...] = merge_part(1)
    weights[5].wait()

    def o_arrival(other):
        return send(
            o_send.at[other], o_recv.at[other], o_ss.at[other], o_rs.at[other], group_seq(other), tp
        )

    @pl.loop(1, groups)
    def _(i):
        o_arrival(group_peer(i)[0]).wait_recv()

    heads = []
    for h in range(HEADS_HERE):
        pieces, levels = [], []
        for b in range(groups // HEADS_HERE):
            piece = o_recv[b * HEADS_HERE + h].astype(F32)
            spare = piece[HALO:]
            pieces.append(jnp.concatenate([piece, pltpu.roll(piece[:HALO], HEAD, 1)], 0))
            levels.append(
                jnp.concatenate(
                    [
                        spare[:, 16 * k : 16 * k + 1] + spare[:, 16 * k + 8 : 16 * k + 9]
                        for k in range(3)
                    ],
                    0,
                )
            )
        peak = functools.reduce(jnp.maximum, levels)
        shares = [jnp.exp(level - peak) for level in levels]
        whole = functools.reduce(jnp.add, shares)
        mixed = functools.reduce(jnp.add, [s * p for s, p in zip(shares, pieces)])
        heads.append(mixed / whole)
    attended = jnp.concatenate(
        [
            jnp.where(low, pltpu.roll(heads[2 * pair], HEAD, 1), heads[2 * pair + 1]).astype(BF16)
            for pair in range(HEADS_HERE // 2)
        ],
        1,
    )
    scatter_part(0, jnp.dot(attended, w_out[...], preferred_element_type=F32))
    merged = fin_acc[...] + merge_part(0)

    def fin_copy(i):
        to = tp_peer(i)
        return send(fin_send.at[to], fin_recv.at[tp], fin_ss.at[i], fin_rs.at[i], seq, to)

    for i in range(tp_size):
        fin_send[i] = merged[:, i * width : (i + 1) * width].astype(BF16)

    @pl.loop(1, tp_size)
    def _(i):
        fin_copy(i).start()

    fin_recv[tp] = fin_send[tp]

    @pl.loop(1, tp_size)
    def _(i):
        fin_copy(i).wait_recv()

    own = frames[:, pl.ds(pl.multiple_of(tp * width, width), width)].astype(F32)
    out[...] = (own + jnp.sum(fin_recv[...].astype(F32), 0)).astype(BF16)

    @pl.loop(1, nearby)
    def _(i):
        kv_copy(i).wait_send()

    @pl.loop(0, nearby)
    def _(i):
        across_copy(i).wait_send()

    @pl.loop(1, groups)
    def _(i):
        q_copy(i).wait_send()
        o_arrival(group_peer(i)[0]).wait_send()

    for copy in gate_copies():
        copy.wait_send()

    @pl.loop(1, tp_size)
    def _(i):
        stat_copy(i).wait_send()
        part_copy(0, i).wait_send()
        part_copy(1, i).wait_send()
        fin_copy(i).wait_send()

    @pl.loop(0, tp_size)
    def _(i):
        for copy in stat_halo(i) + part_halo(0, i) + part_halo(1, i):
            copy.wait_send()


def solution(mesh):
    seq_size, tp_size = mesh.shape["seq"], mesh.shape["tp"]

    def on_device(*args):
        frames, query, key, value, w_out, w_in, w_conv, w_proj, w_blend, w_merge = args
        rows, width = query.shape
        features = frames.shape[1]
        units = w_in.shape[2]
        groups = 2 * DEPTH
        sources = seq_size // DEPTH * 2
        wide = rows + 2 * HALO
        dma = pltpu.SemaphoreType.DMA
        vmem = pltpu.VMEM
        return pl.pallas_call(
            functools.partial(kernel, seq_size, tp_size),
            out_shape=jax.ShapeDtypeStruct((rows, width), BF16),
            in_specs=[pl.BlockSpec(memory_space=pltpu.HBM)] * 10,
            out_specs=pl.BlockSpec(memory_space=pltpu.VMEM),
            scratch_shapes=[
                vmem(frames.shape, BF16),
                vmem(query.shape, BF16),
                vmem(key.shape, BF16),
                vmem(value.shape, BF16),
                vmem(w_out.shape, BF16),
                vmem(w_in.shape, BF16),
                vmem(w_conv.shape, F32),
                vmem(w_proj.shape, BF16),
                vmem(w_blend.shape, F32),
                vmem(w_merge.shape, BF16),
                vmem((HEADS_HERE, rows, 128), BF16),
                vmem((HEADS_HERE, 2 * HALO, 128), BF16),
                vmem((sources, rows, 128), BF16),
                vmem((sources * rows, 128), BF16),
                vmem((groups, 2 * HALO, 128), BF16),
                vmem((groups, 2 * HALO, 128), BF16),
                vmem((groups, 2 * HALO, 128), BF16),
                vmem((rows, units), BF16),
                vmem((rows, units), BF16),
                vmem((HALO, units), BF16),
                vmem((HALO, units), BF16),
                vmem((8, 128), F32),
                vmem((tp_size, 8, 128), F32),
                vmem((tp_size, 8, 128), F32),
                vmem((tp_size, 8, 128), F32),
                vmem((wide, units), F32),
                vmem((2, tp_size, rows, width), BF16),
                vmem((2, tp_size, rows, width), BF16),
                vmem((2, tp_size, HALO, width), BF16),
                vmem((2, tp_size, HALO, width), BF16),
                vmem((wide, width), F32),
                vmem((TAPS, width), F32),
                vmem((rows, features), F32),
                vmem((tp_size, rows, width), BF16),
                vmem((tp_size, rows, width), BF16),
                dma((4,)),
                dma((6,)),
                dma((2 * RING,)),
                dma((2 * RING,)),
                dma((2 * RING,)),
                dma((2 * RING,)),
                dma((groups,)),
                dma((groups,)),
                dma((groups,)),
                dma((groups,)),
                dma((2,)),
                dma((2,)),
                dma((tp_size,)),
                dma((tp_size,)),
                dma((2, tp_size)),
                dma((2, tp_size)),
                dma((2, tp_size)),
                dma((2, tp_size)),
                dma((2, 2, tp_size)),
                dma((2, 2, tp_size)),
                dma((tp_size,)),
                dma((tp_size,)),
            ],
            compiler_params=pltpu.CompilerParams(
                collective_id=0,
                has_side_effects=True,
                vmem_limit_bytes=63 * 1024 * 1024,
            ),
        )(*args)

    return jax.shard_map(
        on_device,
        mesh=mesh,
        in_specs=(
            P("seq", None),
            P("seq", "tp"),
            P("seq", "tp"),
            P("seq", "tp"),
            P("tp", None),
            P(None, None, "tp"),
            P(None, "tp"),
            P("tp", None),
            P(None, None, "tp"),
            P(None, "tp", None),
        ),
        out_specs=P("seq", "tp"),
        check_vma=False,
    )
```

```python
import functools

import jax
import jax.numpy as jnp
from jax import lax
from jax.experimental import pallas as pl
from jax.experimental.pallas import tpu as pltpu
from jax.sharding import PartitionSpec as P

HEAD = 64
CH = 2048
TAPS = 31
HALO = 16
HEADS_HERE = 4
RING = 8
DEPTH = 8
LOG2E = 1.4426950408889634
LN2 = 0.6931471805599453
F32 = jnp.float32
BF16 = jnp.bfloat16
MESH = pl.DeviceIdType.MESH


def low_lanes(rows):
    return lax.broadcasted_iota(jnp.int32, (rows, 128), 1) < HEAD


def depthwise(pad_ref, taps_ref, column, rows):
    lanes = pl.ds(column, 128)
    total = jnp.zeros((rows, 128), F32)
    for phase in range(8):
        shifted = pad_ref[pl.ds(phase, rows + 24 if phase else rows + 32), lanes]
        for start in range(0, 33, 8):
            j = start + phase - 1
            if 0 <= j < TAPS:
                total = total + taps_ref[pl.ds(j, 1), lanes] * shifted[start : start + rows]
    return total


def kernel(
    seq_size,
    tp_size,
    frames_hbm,
    query_hbm,
    key_hbm,
    value_hbm,
    w_out_hbm,
    w_in_hbm,
    w_conv_hbm,
    w_proj_hbm,
    w_blend_hbm,
    w_merge_hbm,
    out,
    frames,
    query,
    key,
    value,
    w_out,
    w_in,
    w_conv,
    w_proj,
    w_blend,
    w_merge,
    kv_send,
    q_send,
    kv_all,
    kv_ones,
    q_all,
    o_send,
    o_recv,
    gate_half,
    resid_half,
    gate_prev,
    gate_next,
    stat_send,
    stat_recv,
    stat_prev,
    stat_next,
    gate_pad,
    part_send,
    part_recv,
    part_prev,
    part_next,
    blend_pad,
    taps_pad,
    fin_acc,
    fin_send,
    fin_recv,
    near_sem,
    weight_sem,
    kv_ss,
    kv_rs,
    across_ss,
    direct_ss,
    across_rs,
    q_ss,
    q_rs,
    o_ss,
    o_rs,
    gate_ss,
    gate_rs,
    stat_ss,
    stat_rs,
    stat_hs,
    stat_hr,
    part_ss,
    part_rs,
    part_hs,
    part_hr,
    fin_ss,
    fin_rs,
):
    rows = query.shape[0]
    wide = rows + 2 * HALO
    seq = lax.axis_index("seq")
    tp = lax.axis_index("tp")
    groups = 2 * DEPTH
    sides = seq_size // (RING * DEPTH)
    nearby = 2 * RING
    y_at = lax.rem(seq, RING)
    z_at = lax.rem(seq // RING, DEPTH)
    x_at = seq // (RING * DEPTH)
    group = 2 * z_at + lax.rem(y_at, 2)
    head_at = lax.rem(group, HEADS_HERE)
    place = lax.rem(z_at, 2) * RING + y_at
    across = lax.rem(seq + RING * DEPTH, seq_size)
    after = lax.rem(seq + 1, seq_size)
    before = lax.rem(seq + seq_size - 1, seq_size)

    def group_seq(other):
        return (x_at * DEPTH + other // 2) * RING + 2 * (y_at // 2) + lax.rem(other, 2)

    def group_peer(i):
        other = lax.rem(group + i, groups)
        return other, group_seq(other)

    def key_peer(i):
        y = lax.rem(y_at + lax.rem(i, RING), RING)
        z_low = lax.rem(z_at + i // RING, 2)
        return 2 * z_low + lax.rem(y, 2), (x_at * DEPTH + 2 * (z_at // 2) + z_low) * RING + y

    def key_place(i):
        y = lax.rem(y_at + RING - lax.rem(i, RING), RING)
        return lax.rem(z_at + i // RING, 2) * RING + y

    def tp_peer(i):
        return 2 * lax.rem(tp // 2 + i // 2, tp_size // 2) + lax.rem(tp + i, 2)

    def send(src, dst, send_sem, recv_sem, to_seq, to_tp):
        return pltpu.make_async_remote_copy(
            src_ref=src,
            dst_ref=dst,
            send_sem=send_sem,
            recv_sem=recv_sem,
            device_id=(to_seq, to_tp),
            device_id_type=MESH,
        )

    near = [
        pltpu.make_async_copy(src, dst, near_sem.at[i])
        for i, (src, dst) in enumerate(
            (
                (key_hbm, key),
                (value_hbm, value),
                (query_hbm, query),
                (frames_hbm, frames),
            )
        )
    ]
    weights = [
        pltpu.make_async_copy(src, dst, weight_sem.at[i])
        for i, (src, dst) in enumerate(
            (
                (w_in_hbm, w_in),
                (w_conv_hbm, w_conv),
                (w_proj_hbm, w_proj),
                (w_blend_hbm, w_blend),
                (w_merge_hbm, w_merge),
                (w_out_hbm, w_out),
            )
        )
    ]
    for copy in near + weights:
        copy.start()

    def hops(i):
        return min(i % RING, RING - i % RING) + i // RING

    near_first = sorted(range(1, nearby), key=hops)
    direct = [i for i in range(1, nearby) if i % RING in (0, 1, RING - 1)]
    relayed = [i for i in near_first if i not in direct]

    barrier = pltpu.get_barrier_semaphore()

    def greet(to_seq, to_tp):
        pl.semaphore_signal(barrier, inc=1, device_id=(to_seq, to_tp), device_id_type=MESH)

    @pl.loop(1, groups)
    def _(i):
        greet(group_peer(i)[1], tp)

    @pl.loop(1, nearby)
    def _(i):
        greet(key_peer(i)[1], tp)

    greet(across, tp)
    for i in direct:
        greet(lax.rem(key_peer(i)[1] + RING * DEPTH, seq_size), tp)

    @pl.loop(1, tp_size)
    def _(i):
        greet(seq, tp_peer(i))

    @pl.loop(0, tp_size)
    def _(i):
        greet(after, i)
        greet(before, i)

    for copy in near[:3]:
        copy.wait()
    low = low_lanes(rows)
    for pair in range(HEADS_HERE // 2):
        lanes = pl.ds(pair * 128, 128)
        k2 = key[:, lanes].astype(F32)
        v2 = value[:, lanes].astype(F32)
        q2 = query[:, lanes].astype(F32)
        kv_send[2 * pair] = jnp.where(low, k2, pltpu.roll(v2, HEAD, 1)).astype(BF16)
        kv_send[2 * pair + 1] = jnp.where(low, pltpu.roll(k2, HEAD, 1), v2).astype(BF16)
        for h, q in ((2 * pair, q2), (2 * pair + 1, pltpu.roll(q2, HEAD, 1))):
            q_send[h, pl.ds(0, HALO)] = jnp.where(
                low_lanes(HALO), q[:HALO], pltpu.roll(q[2 * HALO :], HEAD, 1)
            ).astype(BF16)
            q_send[h, pl.ds(HALO, HALO)] = q[HALO : 2 * HALO].astype(BF16)
    kv_all[x_at * nearby + place] = kv_send[head_at]
    q_all[group] = q_send[head_at]

    pl.semaphore_wait(barrier, (groups - 1) + nearby + len(direct) + (tp_size - 1) + 2 * tp_size)

    def kv_copy(i):
        other, to = key_peer(i)
        return send(
            kv_send.at[other], kv_all.at[x_at * nearby + place], kv_ss.at[i], kv_rs.at[i], to, tp
        )

    def direct_copy(i):
        other, to = key_peer(i)
        to = lax.rem(to + RING * DEPTH, seq_size)
        return send(
            kv_send.at[other],
            kv_all.at[x_at * nearby + place],
            direct_ss.at[i],
            across_rs.at[place],
            to,
            tp,
        )

    def across_copy(at):
        slot = kv_all.at[x_at * nearby + at]
        return send(slot, slot, across_ss.at[at], across_rs.at[at], across, tp)

    def q_copy(i):
        other, to = group_peer(i)
        return send(
            q_send.at[lax.rem(other, HEADS_HERE)],
            q_all.at[group],
            q_ss.at[i],
            q_rs.at[i],
            to,
            tp,
        )

    for i in reversed(relayed):
        kv_copy(i).start()
    across_copy(place).start()
    for i in direct:
        direct_copy(i).start()
    for i in direct:
        kv_copy(i).start()

    near[3].wait()
    features = frames[...].astype(F32)
    centered = features - jnp.mean(features, -1, keepdims=True)
    variance = jnp.mean(centered * centered, -1, keepdims=True)
    normed = (centered * lax.rsqrt(variance + 1e-05)).astype(BF16)

    weights[0].wait()

    def hidden_half(half):
        product = jnp.dot(normed, w_in[:, half, :], preferred_element_type=F32)
        return (0.5 * product * (1.0 + lax.erf(product * 0.7071067811865476))).astype(BF16)

    gate = hidden_half(1)
    gate_half[...] = gate
    gate_float = gate.astype(F32)
    sums = jnp.sum(gate_float, -1, keepdims=True)
    squares = jnp.sum(gate_float * gate_float, -1, keepdims=True)
    stat_lane = lax.broadcasted_iota(jnp.int32, (8, 128), 1)
    stats = jnp.zeros((8, 128), F32)
    for k in range(rows // 8):
        at = slice(8 * k, 8 * k + 8)
        stats = jnp.where(stat_lane // 8 == k, sums[at], stats)
        stats = jnp.where(stat_lane // 8 == 8 + k, squares[at], stats)
    stat_send[...] = stats

    tail = pl.ds(rows - HALO, HALO)
    head = pl.ds(0, HALO)

    def gate_copies():
        return (
            send(gate_half.at[tail], gate_prev, gate_ss.at[0], gate_rs.at[0], after, tp),
            send(gate_half.at[head], gate_next, gate_ss.at[1], gate_rs.at[1], before, tp),
        )

    def stat_copy(i):
        return send(
            stat_send, stat_recv.at[tp], stat_ss.at[i], stat_rs.at[i], seq, tp_peer(i)
        )

    def stat_halo(i):
        to = tp_peer(i)
        return (
            send(stat_send, stat_prev.at[tp], stat_hs.at[0, i], stat_hr.at[0, i], after, to),
            send(stat_send, stat_next.at[tp], stat_hs.at[1, i], stat_hr.at[1, i], before, to),
        )

    for i in reversed(range(tp_size)):
        for copy in stat_halo(i):
            copy.start()
    for copy in gate_copies():
        copy.start()
    for i in reversed(range(1, tp_size)):
        stat_copy(i).start()
    stat_recv[tp] = stat_send[...]

    def hand_on(chosen):
        for i in chosen:
            kv_copy(i).wait_recv()
            across_copy(key_place(i)).start()

    hand_on(relayed[:4])
    for i in sorted(range(1, groups), key=lambda i: -min(i // 2, DEPTH - i // 2)):
        q_copy(i).start()
    resid_half[...] = hidden_half(0)
    hand_on(relayed[4:])
    for i in direct:
        kv_copy(i).wait_recv()

    @pl.loop(1, tp_size)
    def _(i):
        stat_copy(i).wait_recv()

    @pl.loop(0, tp_size)
    def _(i):
        for copy in stat_halo(i):
            copy.wait_recv()

    for copy in gate_copies():
        copy.wait_recv()

    def gate_normed(part, stats, blocks, keep):
        total = jnp.sum(stats[...], 0) / CH
        average = jnp.concatenate([total[:, 8 * k : 8 * k + 1] for k in blocks], 0)
        square = jnp.concatenate([total[:, HEAD + 8 * k : HEAD + 8 * k + 1] for k in blocks], 0)
        variance = square - average * average
        result = (part[...].astype(F32) - average) * lax.rsqrt(variance + 1e-05)
        result = result.astype(BF16).astype(F32)
        return result if keep is None else jnp.where(keep, result, 0.0)

    first, last = seq == 0, seq == seq_size - 1
    gate_pad[pl.ds(0, HALO)] = gate_normed(gate_prev, stat_prev, range(rows // 8 - 2, rows // 8), jnp.logical_not(first))
    gate_pad[pl.ds(HALO, rows)] = gate_normed(gate_half, stat_recv, range(rows // 8), None)
    gate_pad[pl.ds(HALO + rows, HALO)] = gate_normed(gate_next, stat_next, range(2), jnp.logical_not(last))
    weights[1].wait()
    weights[2].wait()
    cg_part = jnp.zeros((rows, w_proj.shape[1]), F32)
    gated = []
    for column in range(0, resid_half.shape[1], 128):
        conv = depthwise(gate_pad, w_conv, column, rows)
        resid = resid_half[:, pl.ds(column, 128)].astype(F32)
        gated.append((resid * conv).astype(BF16))
    cg_part = jnp.dot(jnp.concatenate(gated, 1), w_proj[...], preferred_element_type=F32)

    width = out.shape[1]

    def part_copy(which, i):
        to = tp_peer(i)
        return send(
            part_send.at[which, to],
            part_recv.at[which, tp],
            part_ss.at[which, i],
            part_rs.at[which, i],
            seq,
            to,
        )

    def part_halo(which, i):
        to = tp_peer(i)
        return (
            send(
                part_send.at[which, to, tail],
                part_prev.at[which, tp],
                part_hs.at[which, 0, i],
                part_hr.at[which, 0, i],
                after,
                to,
            ),
            send(
                part_send.at[which, to, head],
                part_next.at[which, tp],
                part_hs.at[which, 1, i],
                part_hr.at[which, 1, i],
                before,
                to,
            ),
        )

    def scatter_part(which, part):
        for i in range(tp_size):
            part_send[which, i] = part[:, i * width : (i + 1) * width].astype(BF16)

        for i in reversed(range(tp_size)):
            for copy in part_halo(which, i):
                copy.start()
        for i in reversed(range(1, tp_size)):
            part_copy(which, i).start()

        part_recv[which, tp] = part_send[which, tp]

    def merge_part(which):
        @pl.loop(1, tp_size)
        def _(i):
            part_copy(which, i).wait_recv()

        @pl.loop(0, tp_size)
        def _(i):
            for copy in part_halo(which, i):
                copy.wait_recv()

        def joined(ref):
            return jnp.sum(ref[which].astype(F32), 0).astype(BF16).astype(F32)

        own = joined(part_recv)
        blend_pad[pl.ds(0, HALO)] = jnp.where(first, 0.0, joined(part_prev))
        blend_pad[pl.ds(HALO, rows)] = own
        blend_pad[pl.ds(HALO + rows, HALO)] = jnp.where(last, 0.0, joined(part_next))
        taps_pad[...] = w_blend[:, which, :]
        mixture = [
            (own[:, c : c + 128] + depthwise(blend_pad, taps_pad, c, rows)).astype(BF16)
            for c in range(0, width, 128)
        ]
        return jnp.dot(jnp.concatenate(mixture, 1), w_merge[which], preferred_element_type=F32)

    scatter_part(1, cg_part)

    @pl.loop(1, groups)
    def _(i):
        q_copy(i).wait_recv()

    @pl.loop(0, nearby)
    def _(i):
        across_copy(i).wait_recv()

    keys = sides * nearby * rows
    kv = kv_all[...].reshape(keys, 128)
    kv_ones[...] = jnp.where(low_lanes(keys), jnp.ones((), BF16), kv)

    def o_copy(other):
        return send(
            o_send.at[other], o_recv.at[group], o_ss.at[other], o_rs.at[group], group_seq(other), tp
        )

    per_step = 4

    @pl.loop(0, groups // per_step)
    def _(step):
        start = group + groups + jnp.where(step < 2, 6 + 4 * step, 12 * step - 22)
        count = per_step * rows
        pieces = []
        for i in range(per_step):
            q = q_all[lax.rem(start + i, groups)]
            q_end = pltpu.roll(q[:HALO].astype(F32), HEAD, 1).astype(BF16)
            pieces += [q, q_end]
        q = jnp.concatenate(pieces, 0)
        q = jnp.where(low_lanes(count), q, jnp.zeros((), BF16))
        kv = kv_all[...].reshape(keys, 128)
        scores = lax.dot_general(q, kv, (((1,), (1,)), ((), ())), preferred_element_type=F32)
        peak = jnp.max(scores, -1, keepdims=True)
        weight = jnp.exp2((scores - peak) * (LOG2E * HEAD**-0.5)).astype(BF16)
        mixed = jnp.dot(weight, kv_ones[...], preferred_element_type=F32)
        low_q = low_lanes(count)
        total = jnp.where(low_q, mixed, pltpu.roll(mixed, HEAD, 1))
        level = peak * HEAD**-0.5 + jnp.log(total)
        level_high = level.astype(BF16).astype(F32)
        level_low = level - level_high
        mixed = mixed / total
        lane = lax.broadcasted_iota(jnp.int32, (HALO, 128), 1)
        for i in range(per_step):
            thirds = [slice(i * rows + k * HALO, i * rows + (k + 1) * HALO) for k in range(3)]
            spare = jnp.zeros((HALO, 128), F32)
            for k, at in enumerate(thirds):
                spare = jnp.where(lane // 8 == 2 * k, level_high[at], spare)
                spare = jnp.where(lane // 8 == 2 * k + 1, level_low[at], spare)
            o_low = low_lanes(HALO)
            first_rows = jnp.where(o_low, pltpu.roll(mixed[thirds[2]], HEAD, 1), mixed[thirds[0]])
            other = lax.rem(start + i, groups)
            o_send[other, pl.ds(0, HALO)] = first_rows.astype(BF16)
            o_send[other, pl.ds(HALO, HALO)] = jnp.where(o_low, spare, mixed[thirds[1]]).astype(
                BF16
            )
        for i in range(per_step):
            other = lax.rem(start + i, groups)

            @pl.when(other != group)
            def _():
                o_copy(other).start()

            @pl.when(other == group)
            def _():
                o_recv[other] = o_send[other]

    for i in (3, 4):
        weights[i].wait()
    fin_acc[...] = merge_part(1)
    weights[5].wait()

    def o_arrival(other):
        return send(
            o_send.at[other], o_recv.at[other], o_ss.at[other], o_rs.at[other], group_seq(other), tp
        )

    @pl.loop(1, groups)
    def _(i):
        o_arrival(group_peer(i)[0]).wait_recv()

    heads = []
    for h in range(HEADS_HERE):
        pieces, levels = [], []
        for b in range(groups // HEADS_HERE):
            piece = o_recv[b * HEADS_HERE + h].astype(F32)
            spare = piece[HALO:]
            pieces.append(jnp.concatenate([piece, pltpu.roll(piece[:HALO], HEAD, 1)], 0))
            levels.append(
                jnp.concatenate(
                    [
                        spare[:, 16 * k : 16 * k + 1] + spare[:, 16 * k + 8 : 16 * k + 9]
                        for k in range(3)
                    ],
                    0,
                )
            )
        peak = functools.reduce(jnp.maximum, levels)
        shares = [jnp.exp(level - peak) for level in levels]
        whole = functools.reduce(jnp.add, shares)
        mixed = functools.reduce(jnp.add, [s * p for s, p in zip(shares, pieces)])
        heads.append(mixed / whole)
    attended = jnp.concatenate(
        [
            jnp.where(low, pltpu.roll(heads[2 * pair], HEAD, 1), heads[2 * pair + 1]).astype(BF16)
            for pair in range(HEADS_HERE // 2)
        ],
        1,
    )
    scatter_part(0, jnp.dot(attended, w_out[...], preferred_element_type=F32))
    merged = fin_acc[...] + merge_part(0)

    def fin_copy(i):
        to = tp_peer(i)
        return send(fin_send.at[to], fin_recv.at[tp], fin_ss.at[i], fin_rs.at[i], seq, to)

    for i in range(tp_size):
        fin_send[i] = merged[:, i * width : (i + 1) * width].astype(BF16)

    for i in reversed(range(1, tp_size)):
        fin_copy(i).start()

    fin_recv[tp] = fin_send[tp]

    @pl.loop(1, tp_size)
    def _(i):
        fin_copy(i).wait_recv()

    own = frames[:, pl.ds(pl.multiple_of(tp * width, width), width)].astype(F32)
    out[...] = (own + jnp.sum(fin_recv[...].astype(F32), 0)).astype(BF16)

    @pl.loop(1, nearby)
    def _(i):
        kv_copy(i).wait_send()

    for i in direct:
        direct_copy(i).wait_send()
    for i in relayed:
        across_copy(key_place(i)).wait_send()
    across_copy(place).wait_send()

    @pl.loop(1, groups)
    def _(i):
        q_copy(i).wait_send()
        o_arrival(group_peer(i)[0]).wait_send()

    for copy in gate_copies():
        copy.wait_send()

    @pl.loop(1, tp_size)
    def _(i):
        stat_copy(i).wait_send()
        part_copy(0, i).wait_send()
        part_copy(1, i).wait_send()
        fin_copy(i).wait_send()

    @pl.loop(0, tp_size)
    def _(i):
        for copy in stat_halo(i) + part_halo(0, i) + part_halo(1, i):
            copy.wait_send()


def solution(mesh):
    seq_size, tp_size = mesh.shape["seq"], mesh.shape["tp"]

    def on_device(*args):
        frames, query, key, value, w_out, w_in, w_conv, w_proj, w_blend, w_merge = args
        rows, width = query.shape
        features = frames.shape[1]
        units = w_in.shape[2]
        groups = 2 * DEPTH
        sources = seq_size // DEPTH * 2
        wide = rows + 2 * HALO
        dma = pltpu.SemaphoreType.DMA
        vmem = pltpu.VMEM
        return pl.pallas_call(
            functools.partial(kernel, seq_size, tp_size),
            out_shape=jax.ShapeDtypeStruct((rows, width), BF16),
            in_specs=[pl.BlockSpec(memory_space=pltpu.HBM)] * 10,
            out_specs=pl.BlockSpec(memory_space=pltpu.VMEM),
            scratch_shapes=[
                vmem(frames.shape, BF16),
                vmem(query.shape, BF16),
                vmem(key.shape, BF16),
                vmem(value.shape, BF16),
                vmem(w_out.shape, BF16),
                vmem(w_in.shape, BF16),
                vmem(w_conv.shape, F32),
                vmem(w_proj.shape, BF16),
                vmem(w_blend.shape, F32),
                vmem(w_merge.shape, BF16),
                vmem((HEADS_HERE, rows, 128), BF16),
                vmem((HEADS_HERE, 2 * HALO, 128), BF16),
                vmem((sources, rows, 128), BF16),
                vmem((sources * rows, 128), BF16),
                vmem((groups, 2 * HALO, 128), BF16),
                vmem((groups, 2 * HALO, 128), BF16),
                vmem((groups, 2 * HALO, 128), BF16),
                vmem((rows, units), BF16),
                vmem((rows, units), BF16),
                vmem((HALO, units), BF16),
                vmem((HALO, units), BF16),
                vmem((8, 128), F32),
                vmem((tp_size, 8, 128), F32),
                vmem((tp_size, 8, 128), F32),
                vmem((tp_size, 8, 128), F32),
                vmem((wide, units), F32),
                vmem((2, tp_size, rows, width), BF16),
                vmem((2, tp_size, rows, width), BF16),
                vmem((2, tp_size, HALO, width), BF16),
                vmem((2, tp_size, HALO, width), BF16),
                vmem((wide, width), F32),
                vmem((TAPS, width), F32),
                vmem((rows, features), F32),
                vmem((tp_size, rows, width), BF16),
                vmem((tp_size, rows, width), BF16),
                dma((4,)),
                dma((6,)),
                dma((2 * RING,)),
                dma((2 * RING,)),
                dma((2 * RING,)),
                dma((2 * RING,)),
                dma((2 * RING,)),
                dma((groups,)),
                dma((groups,)),
                dma((groups,)),
                dma((groups,)),
                dma((2,)),
                dma((2,)),
                dma((tp_size,)),
                dma((tp_size,)),
                dma((2, tp_size)),
                dma((2, tp_size)),
                dma((2, tp_size)),
                dma((2, tp_size)),
                dma((2, 2, tp_size)),
                dma((2, 2, tp_size)),
                dma((tp_size,)),
                dma((tp_size,)),
            ],
            compiler_params=pltpu.CompilerParams(
                collective_id=0,
                has_side_effects=True,
                vmem_limit_bytes=63 * 1024 * 1024,
            ),
        )(*args)

    return jax.shard_map(
        on_device,
        mesh=mesh,
        in_specs=(
            P("seq", None),
            P("seq", "tp"),
            P("seq", "tp"),
            P("seq", "tp"),
            P("tp", None),
            P(None, None, "tp"),
            P(None, "tp"),
            P("tp", None),
            P(None, None, "tp"),
            P(None, "tp", None),
        ),
        out_specs=P("seq", "tp"),
        check_vma=False,
    )
```

```python
import functools

import jax
import jax.numpy as jnp
from jax import lax
from jax.experimental import pallas as pl
from jax.experimental.pallas import tpu as pltpu
from jax.sharding import PartitionSpec as P

HEAD = 64
CH = 2048
TAPS = 31
HALO = 16
HEADS_HERE = 4
RING = 8
DEPTH = 8
LOG2E = 1.4426950408889634
LN2 = 0.6931471805599453
F32 = jnp.float32
BF16 = jnp.bfloat16
MESH = pl.DeviceIdType.MESH


def low_lanes(rows):
    return lax.broadcasted_iota(jnp.int32, (rows, 128), 1) < HEAD


def depthwise(pad_ref, taps_ref, column, rows):
    lanes = pl.ds(column, 128)
    total = jnp.zeros((rows, 128), F32)
    for phase in range(8):
        shifted = pad_ref[pl.ds(phase, rows + 24 if phase else rows + 32), lanes]
        for start in range(0, 33, 8):
            j = start + phase - 1
            if 0 <= j < TAPS:
                total = total + taps_ref[pl.ds(j, 1), lanes] * shifted[start : start + rows]
    return total


def kernel(
    seq_size,
    tp_size,
    frames_hbm,
    query_hbm,
    key_hbm,
    value_hbm,
    w_out_hbm,
    w_in_hbm,
    w_conv_hbm,
    w_proj_hbm,
    w_blend_hbm,
    w_merge_hbm,
    out,
    frames,
    query,
    key,
    value,
    w_out,
    w_in,
    w_conv,
    w_proj,
    w_blend,
    w_merge,
    kv_send,
    q_send,
    kv_all,
    kv_ones,
    q_all,
    o_send,
    o_recv,
    gate_half,
    resid_half,
    gate_prev,
    gate_next,
    stat_send,
    stat_recv,
    stat_prev,
    stat_next,
    gate_pad,
    part_send,
    part_recv,
    part_prev,
    part_next,
    blend_pad,
    taps_pad,
    fin_acc,
    fin_send,
    fin_recv,
    near_sem,
    weight_sem,
    kv_ss,
    kv_rs,
    across_ss,
    direct_ss,
    across_rs,
    q_ss,
    q_rs,
    o_ss,
    o_rs,
    gate_ss,
    gate_rs,
    stat_ss,
    stat_rs,
    stat_hs,
    stat_hr,
    part_ss,
    part_rs,
    part_hs,
    part_hr,
    fin_ss,
    fin_rs,
):
    rows = query.shape[0]
    wide = rows + 2 * HALO
    seq = lax.axis_index("seq")
    tp = lax.axis_index("tp")
    groups = 2 * DEPTH
    sides = seq_size // (RING * DEPTH)
    nearby = 2 * RING
    y_at = lax.rem(seq, RING)
    z_at = lax.rem(seq // RING, DEPTH)
    x_at = seq // (RING * DEPTH)
    group = 2 * z_at + lax.rem(y_at, 2)
    head_at = lax.rem(group, HEADS_HERE)
    place = lax.rem(z_at, 2) * RING + y_at
    across = lax.rem(seq + RING * DEPTH, seq_size)
    after = lax.rem(seq + 1, seq_size)
    before = lax.rem(seq + seq_size - 1, seq_size)

    def group_seq(other):
        return (x_at * DEPTH + other // 2) * RING + 2 * (y_at // 2) + lax.rem(other, 2)

    def group_peer(i):
        other = lax.rem(group + i, groups)
        return other, group_seq(other)

    def key_peer(i):
        y = lax.rem(y_at + lax.rem(i, RING), RING)
        z_low = lax.rem(z_at + i // RING, 2)
        return 2 * z_low + lax.rem(y, 2), (x_at * DEPTH + 2 * (z_at // 2) + z_low) * RING + y

    def key_place(i):
        y = lax.rem(y_at + RING - lax.rem(i, RING), RING)
        return lax.rem(z_at + i // RING, 2) * RING + y

    def tp_peer(i):
        return 2 * lax.rem(tp // 2 + i // 2, tp_size // 2) + lax.rem(tp + i, 2)

    def send(src, dst, send_sem, recv_sem, to_seq, to_tp):
        return pltpu.make_async_remote_copy(
            src_ref=src,
            dst_ref=dst,
            send_sem=send_sem,
            recv_sem=recv_sem,
            device_id=(to_seq, to_tp),
            device_id_type=MESH,
        )

    near = [
        pltpu.make_async_copy(src, dst, near_sem.at[i])
        for i, (src, dst) in enumerate(
            (
                (key_hbm, key),
                (value_hbm, value),
                (query_hbm, query),
                (frames_hbm, frames),
            )
        )
    ]
    weights = [
        pltpu.make_async_copy(src, dst, weight_sem.at[i])
        for i, (src, dst) in enumerate(
            (
                (w_in_hbm, w_in),
                (w_conv_hbm, w_conv),
                (w_proj_hbm, w_proj),
                (w_blend_hbm, w_blend),
                (w_merge_hbm, w_merge),
                (w_out_hbm, w_out),
            )
        )
    ]
    for copy in near[:3]:
        copy.start()

    def hops(i):
        return min(i % RING, RING - i % RING) + i // RING

    near_first = sorted(range(1, nearby), key=hops)
    direct = [i for i in range(1, nearby) if i % RING in (0, 1, RING - 1)]
    relayed = [i for i in near_first if i not in direct]

    barrier = pltpu.get_barrier_semaphore()

    def greet(to_seq, to_tp):
        pl.semaphore_signal(barrier, inc=1, device_id=(to_seq, to_tp), device_id_type=MESH)

    far_groups = sorted(range(1, groups), key=lambda i: -min(i // 2, DEPTH - i // 2))
    for to_group, to_key in zip(far_groups, reversed(near_first)):
        greet(group_peer(to_group)[1], tp)
        greet(key_peer(to_key)[1], tp)
    for i in direct:
        greet(lax.rem(key_peer(i)[1] + RING * DEPTH, seq_size), tp)
    for i in range(tp_size):
        greet(after, i)
        greet(before, i)
    greet(across, tp)
    for i in range(1, tp_size):
        greet(seq, tp_peer(i))
    for copy in near[3:] + weights:
        copy.start()

    for copy in near[:3]:
        copy.wait()
    low = low_lanes(rows)
    for pair in range(HEADS_HERE // 2):
        lanes = pl.ds(pair * 128, 128)
        k2 = key[:, lanes].astype(F32)
        v2 = value[:, lanes].astype(F32)
        q2 = query[:, lanes].astype(F32)
        kv_send[2 * pair] = jnp.where(low, k2, pltpu.roll(v2, HEAD, 1)).astype(BF16)
        kv_send[2 * pair + 1] = jnp.where(low, pltpu.roll(k2, HEAD, 1), v2).astype(BF16)
        for h, q in ((2 * pair, q2), (2 * pair + 1, pltpu.roll(q2, HEAD, 1))):
            q_send[h, pl.ds(0, HALO)] = jnp.where(
                low_lanes(HALO), q[:HALO], pltpu.roll(q[2 * HALO :], HEAD, 1)
            ).astype(BF16)
            q_send[h, pl.ds(HALO, HALO)] = q[HALO : 2 * HALO].astype(BF16)
    kv_all[x_at * nearby + place] = kv_send[head_at]
    q_all[group] = q_send[head_at]

    pl.semaphore_wait(barrier, (groups - 1) + nearby + len(direct) + (tp_size - 1) + 2 * tp_size)

    def kv_copy(i):
        other, to = key_peer(i)
        return send(
            kv_send.at[other], kv_all.at[x_at * nearby + place], kv_ss.at[i], kv_rs.at[i], to, tp
        )

    def direct_copy(i):
        other, to = key_peer(i)
        to = lax.rem(to + RING * DEPTH, seq_size)
        return send(
            kv_send.at[other],
            kv_all.at[x_at * nearby + place],
            direct_ss.at[i],
            across_rs.at[place],
            to,
            tp,
        )

    def across_copy(at):
        slot = kv_all.at[x_at * nearby + at]
        return send(slot, slot, across_ss.at[at], across_rs.at[at], across, tp)

    def q_copy(i):
        other, to = group_peer(i)
        return send(
            q_send.at[lax.rem(other, HEADS_HERE)],
            q_all.at[group],
            q_ss.at[i],
            q_rs.at[i],
            to,
            tp,
        )

    for i in reversed(relayed):
        kv_copy(i).start()
    across_copy(place).start()
    for i in direct:
        direct_copy(i).start()
    for i in direct:
        kv_copy(i).start()

    near[3].wait()
    features = frames[...].astype(F32)
    centered = features - jnp.mean(features, -1, keepdims=True)
    variance = jnp.mean(centered * centered, -1, keepdims=True)
    normed = (centered * lax.rsqrt(variance + 1e-05)).astype(BF16)

    weights[0].wait()

    def hidden_half(half):
        product = jnp.dot(normed, w_in[:, half, :], preferred_element_type=F32)
        return (0.5 * product * (1.0 + lax.erf(product * 0.7071067811865476))).astype(BF16)

    gate = hidden_half(1)
    gate_half[...] = gate
    gate_float = gate.astype(F32)
    sums = jnp.sum(gate_float, -1, keepdims=True)
    squares = jnp.sum(gate_float * gate_float, -1, keepdims=True)
    stat_lane = lax.broadcasted_iota(jnp.int32, (8, 128), 1)
    stats = jnp.zeros((8, 128), F32)
    for k in range(rows // 8):
        at = slice(8 * k, 8 * k + 8)
        stats = jnp.where(stat_lane // 8 == k, sums[at], stats)
        stats = jnp.where(stat_lane // 8 == 8 + k, squares[at], stats)
    stat_send[...] = stats

    tail = pl.ds(rows - HALO, HALO)
    head = pl.ds(0, HALO)

    def gate_copies():
        return (
            send(gate_half.at[tail], gate_prev, gate_ss.at[0], gate_rs.at[0], after, tp),
            send(gate_half.at[head], gate_next, gate_ss.at[1], gate_rs.at[1], before, tp),
        )

    def stat_copy(i):
        return send(
            stat_send, stat_recv.at[tp], stat_ss.at[i], stat_rs.at[i], seq, tp_peer(i)
        )

    def stat_halo(i):
        to = tp_peer(i)
        return (
            send(stat_send, stat_prev.at[tp], stat_hs.at[0, i], stat_hr.at[0, i], after, to),
            send(stat_send, stat_next.at[tp], stat_hs.at[1, i], stat_hr.at[1, i], before, to),
        )

    for i in reversed(range(tp_size)):
        for copy in stat_halo(i):
            copy.start()
    for copy in gate_copies():
        copy.start()
    for i in reversed(range(1, tp_size)):
        stat_copy(i).start()
    stat_recv[tp] = stat_send[...]

    def hand_on(chosen):
        for i in chosen:
            kv_copy(i).wait_recv()
            across_copy(key_place(i)).start()

    hand_on(relayed[:4])
    for i in sorted(range(1, groups), key=lambda i: -min(i // 2, DEPTH - i // 2)):
        q_copy(i).start()
    hand_on(relayed[4:])
    resid_half[...] = hidden_half(0)
    for i in direct:
        kv_copy(i).wait_recv()

    @pl.loop(1, tp_size)
    def _(i):
        stat_copy(i).wait_recv()

    @pl.loop(0, tp_size)
    def _(i):
        for copy in stat_halo(i):
            copy.wait_recv()

    for copy in gate_copies():
        copy.wait_recv()

    def gate_normed(part, stats, blocks, keep):
        total = jnp.sum(stats[...], 0) / CH
        average = jnp.concatenate([total[:, 8 * k : 8 * k + 1] for k in blocks], 0)
        square = jnp.concatenate([total[:, HEAD + 8 * k : HEAD + 8 * k + 1] for k in blocks], 0)
        variance = square - average * average
        result = (part[...].astype(F32) - average) * lax.rsqrt(variance + 1e-05)
        result = result.astype(BF16).astype(F32)
        return result if keep is None else jnp.where(keep, result, 0.0)

    first, last = seq == 0, seq == seq_size - 1
    gate_pad[pl.ds(0, HALO)] = gate_normed(gate_prev, stat_prev, range(rows // 8 - 2, rows // 8), jnp.logical_not(first))
    gate_pad[pl.ds(HALO, rows)] = gate_normed(gate_half, stat_recv, range(rows // 8), None)
    gate_pad[pl.ds(HALO + rows, HALO)] = gate_normed(gate_next, stat_next, range(2), jnp.logical_not(last))
    weights[1].wait()
    weights[2].wait()
    gated = []
    for column in range(0, resid_half.shape[1], 128):
        conv = depthwise(gate_pad, w_conv, column, rows)
        resid = resid_half[:, pl.ds(column, 128)].astype(F32)
        gated.append((resid * conv).astype(BF16))

    width = out.shape[1]

    def part_copy(which, i):
        to = tp_peer(i)
        return send(
            part_send.at[which, to],
            part_recv.at[which, tp],
            part_ss.at[which, i],
            part_rs.at[which, i],
            seq,
            to,
        )

    def part_halo(which, i):
        to = tp_peer(i)
        return (
            send(
                part_send.at[which, to, tail],
                part_prev.at[which, tp],
                part_hs.at[which, 0, i],
                part_hr.at[which, 0, i],
                after,
                to,
            ),
            send(
                part_send.at[which, to, head],
                part_next.at[which, tp],
                part_hs.at[which, 1, i],
                part_hr.at[which, 1, i],
                before,
                to,
            ),
        )

    def columns_of(to):
        return pl.ds(pl.multiple_of(to * width, width), width)

    def scatter_part(which, rows_here, weight):
        for i in reversed(range(tp_size)):
            to = tp_peer(i)
            piece = jnp.dot(rows_here, weight[:, columns_of(to)], preferred_element_type=F32)
            part_send[which, to] = piece.astype(BF16)
            for copy in part_halo(which, i):
                copy.start()
            if i:
                part_copy(which, i).start()
        part_recv[which, tp] = part_send[which, tp]

    def merge_part(which):
        @pl.loop(1, tp_size)
        def _(i):
            part_copy(which, i).wait_recv()

        @pl.loop(0, tp_size)
        def _(i):
            for copy in part_halo(which, i):
                copy.wait_recv()

        def joined(ref):
            return jnp.sum(ref[which].astype(F32), 0).astype(BF16).astype(F32)

        own = joined(part_recv)
        blend_pad[pl.ds(0, HALO)] = jnp.where(first, 0.0, joined(part_prev))
        blend_pad[pl.ds(HALO, rows)] = own
        blend_pad[pl.ds(HALO + rows, HALO)] = jnp.where(last, 0.0, joined(part_next))
        taps_pad[...] = w_blend[:, which, :]
        mixture = [
            (own[:, c : c + 128] + depthwise(blend_pad, taps_pad, c, rows)).astype(BF16)
            for c in range(0, width, 128)
        ]
        return jnp.concatenate(mixture, 1)

    scatter_part(1, jnp.concatenate(gated, 1), w_proj)

    @pl.loop(1, groups)
    def _(i):
        q_copy(i).wait_recv()

    @pl.loop(0, nearby)
    def _(i):
        across_copy(i).wait_recv()

    keys = sides * nearby * rows
    kv = kv_all[...].reshape(keys, 128)
    kv_ones[...] = jnp.where(low_lanes(keys), jnp.ones((), BF16), kv)

    def o_copy(other):
        return send(
            o_send.at[other], o_recv.at[group], o_ss.at[other], o_rs.at[group], group_seq(other), tp
        )

    per_step = 4

    @pl.loop(0, groups // per_step)
    def _(step):
        start = group + groups + jnp.where(step < 2, 6 + 4 * step, 12 * step - 22)
        count = per_step * rows
        pieces = []
        for i in range(per_step):
            q = q_all[lax.rem(start + i, groups)]
            q_end = pltpu.roll(q[:HALO].astype(F32), HEAD, 1).astype(BF16)
            pieces += [q, q_end]
        q = jnp.concatenate(pieces, 0)
        q = jnp.where(low_lanes(count), q, jnp.zeros((), BF16))
        kv = kv_all[...].reshape(keys, 128)
        scores = lax.dot_general(q, kv, (((1,), (1,)), ((), ())), preferred_element_type=F32)
        peak = jnp.max(scores, -1, keepdims=True)
        weight = jnp.exp2((scores - peak) * (LOG2E * HEAD**-0.5)).astype(BF16)
        mixed = jnp.dot(weight, kv_ones[...], preferred_element_type=F32)
        low_q = low_lanes(count)
        total = jnp.where(low_q, mixed, pltpu.roll(mixed, HEAD, 1))
        level = peak * HEAD**-0.5 + jnp.log(total)
        level_high = level.astype(BF16).astype(F32)
        level_low = level - level_high
        mixed = mixed / total
        lane = lax.broadcasted_iota(jnp.int32, (HALO, 128), 1)
        for i in range(per_step):
            thirds = [slice(i * rows + k * HALO, i * rows + (k + 1) * HALO) for k in range(3)]
            spare = jnp.zeros((HALO, 128), F32)
            for k, at in enumerate(thirds):
                spare = jnp.where(lane // 8 == 2 * k, level_high[at], spare)
                spare = jnp.where(lane // 8 == 2 * k + 1, level_low[at], spare)
            o_low = low_lanes(HALO)
            first_rows = jnp.where(o_low, pltpu.roll(mixed[thirds[2]], HEAD, 1), mixed[thirds[0]])
            other = lax.rem(start + i, groups)
            o_send[other, pl.ds(0, HALO)] = first_rows.astype(BF16)
            o_send[other, pl.ds(HALO, HALO)] = jnp.where(o_low, spare, mixed[thirds[1]]).astype(
                BF16
            )
        for i in range(per_step):
            other = lax.rem(start + i, groups)

            @pl.when(other != group)
            def _():
                o_copy(other).start()

            @pl.when(other == group)
            def _():
                o_recv[other] = o_send[other]

    for i in (3, 4):
        weights[i].wait()
    fin_acc[...] = jnp.dot(merge_part(1), w_merge[1], preferred_element_type=F32)
    weights[5].wait()

    @pl.loop(1, nearby)
    def _(i):
        kv_copy(i).wait_send()
        q_copy(i).wait_send()

    for i in direct:
        direct_copy(i).wait_send()
    for i in relayed:
        across_copy(key_place(i)).wait_send()
    across_copy(place).wait_send()
    for copy in gate_copies():
        copy.wait_send()

    def sent_part(which):
        @pl.loop(1, tp_size)
        def _(i):
            part_copy(which, i).wait_send()

        @pl.loop(0, tp_size)
        def _(i):
            for copy in part_halo(which, i):
                copy.wait_send()

    @pl.loop(1, tp_size)
    def _(i):
        stat_copy(i).wait_send()

    @pl.loop(0, tp_size)
    def _(i):
        for copy in stat_halo(i):
            copy.wait_send()

    sent_part(1)

    def o_arrival(other):
        return send(
            o_send.at[other], o_recv.at[other], o_ss.at[other], o_rs.at[other], group_seq(other), tp
        )

    @pl.loop(1, groups)
    def _(i):
        o_arrival(group_peer(i)[0]).wait_recv()

    heads = []
    for h in range(HEADS_HERE):
        pieces, levels = [], []
        for b in range(groups // HEADS_HERE):
            piece = o_recv[b * HEADS_HERE + h].astype(F32)
            spare = piece[HALO:]
            pieces.append(jnp.concatenate([piece, pltpu.roll(piece[:HALO], HEAD, 1)], 0))
            levels.append(
                jnp.concatenate(
                    [
                        spare[:, 16 * k : 16 * k + 1] + spare[:, 16 * k + 8 : 16 * k + 9]
                        for k in range(3)
                    ],
                    0,
                )
            )
        peak = functools.reduce(jnp.maximum, levels)
        shares = [jnp.exp(level - peak) for level in levels]
        whole = functools.reduce(jnp.add, shares)
        mixed = functools.reduce(jnp.add, [s * p for s, p in zip(shares, pieces)])
        heads.append(mixed / whole)
    attended = jnp.concatenate(
        [
            jnp.where(low, pltpu.roll(heads[2 * pair], HEAD, 1), heads[2 * pair + 1]).astype(BF16)
            for pair in range(HEADS_HERE // 2)
        ],
        1,
    )
    scatter_part(0, attended, w_out)
    mixture = merge_part(0)

    def fin_copy(i):
        to = tp_peer(i)
        return send(fin_send.at[to], fin_recv.at[tp], fin_ss.at[i], fin_rs.at[i], seq, to)

    for i in reversed(range(tp_size)):
        to = tp_peer(i)
        piece = jnp.dot(mixture, w_merge[0, :, columns_of(to)], preferred_element_type=F32)
        fin_send[to] = (fin_acc[:, columns_of(to)] + piece).astype(BF16)
        if i:
            fin_copy(i).start()
    fin_recv[tp] = fin_send[tp]

    @pl.loop(1, groups)
    def _(i):
        o_arrival(group_peer(i)[0]).wait_send()

    sent_part(0)

    @pl.loop(1, tp_size)
    def _(i):
        fin_copy(i).wait_recv()

    own = frames[:, pl.ds(pl.multiple_of(tp * width, width), width)].astype(F32)
    out[...] = (own + jnp.sum(fin_recv[...].astype(F32), 0)).astype(BF16)

    for i in range(1, tp_size):
        fin_copy(i).wait_send()


def solution(mesh):
    seq_size, tp_size = mesh.shape["seq"], mesh.shape["tp"]

    def on_device(*args):
        frames, query, key, value, w_out, w_in, w_conv, w_proj, w_blend, w_merge = args
        rows, width = query.shape
        features = frames.shape[1]
        units = w_in.shape[2]
        groups = 2 * DEPTH
        sources = seq_size // DEPTH * 2
        wide = rows + 2 * HALO
        dma = pltpu.SemaphoreType.DMA
        vmem = pltpu.VMEM
        return pl.pallas_call(
            functools.partial(kernel, seq_size, tp_size),
            out_shape=jax.ShapeDtypeStruct((rows, width), BF16),
            in_specs=[pl.BlockSpec(memory_space=pltpu.HBM)] * 10,
            out_specs=pl.BlockSpec(memory_space=pltpu.VMEM),
            scratch_shapes=[
                vmem(frames.shape, BF16),
                vmem(query.shape, BF16),
                vmem(key.shape, BF16),
                vmem(value.shape, BF16),
                vmem(w_out.shape, BF16),
                vmem(w_in.shape, BF16),
                vmem(w_conv.shape, F32),
                vmem(w_proj.shape, BF16),
                vmem(w_blend.shape, F32),
                vmem(w_merge.shape, BF16),
                vmem((HEADS_HERE, rows, 128), BF16),
                vmem((HEADS_HERE, 2 * HALO, 128), BF16),
                vmem((sources, rows, 128), BF16),
                vmem((sources * rows, 128), BF16),
                vmem((groups, 2 * HALO, 128), BF16),
                vmem((groups, 2 * HALO, 128), BF16),
                vmem((groups, 2 * HALO, 128), BF16),
                vmem((rows, units), BF16),
                vmem((rows, units), BF16),
                vmem((HALO, units), BF16),
                vmem((HALO, units), BF16),
                vmem((8, 128), F32),
                vmem((tp_size, 8, 128), F32),
                vmem((tp_size, 8, 128), F32),
                vmem((tp_size, 8, 128), F32),
                vmem((wide, units), F32),
                vmem((2, tp_size, rows, width), BF16),
                vmem((2, tp_size, rows, width), BF16),
                vmem((2, tp_size, HALO, width), BF16),
                vmem((2, tp_size, HALO, width), BF16),
                vmem((wide, width), F32),
                vmem((TAPS, width), F32),
                vmem((rows, features), F32),
                vmem((tp_size, rows, width), BF16),
                vmem((tp_size, rows, width), BF16),
                dma((4,)),
                dma((6,)),
                dma((2 * RING,)),
                dma((2 * RING,)),
                dma((2 * RING,)),
                dma((2 * RING,)),
                dma((2 * RING,)),
                dma((groups,)),
                dma((groups,)),
                dma((groups,)),
                dma((groups,)),
                dma((2,)),
                dma((2,)),
                dma((tp_size,)),
                dma((tp_size,)),
                dma((2, tp_size)),
                dma((2, tp_size)),
                dma((2, tp_size)),
                dma((2, tp_size)),
                dma((2, 2, tp_size)),
                dma((2, 2, tp_size)),
                dma((tp_size,)),
                dma((tp_size,)),
            ],
            compiler_params=pltpu.CompilerParams(
                collective_id=0,
                has_side_effects=True,
                vmem_limit_bytes=63 * 1024 * 1024,
            ),
        )(*args)

    return jax.shard_map(
        on_device,
        mesh=mesh,
        in_specs=(
            P("seq", None),
            P("seq", "tp"),
            P("seq", "tp"),
            P("seq", "tp"),
            P("tp", None),
            P(None, None, "tp"),
            P(None, "tp"),
            P("tp", None),
            P(None, None, "tp"),
            P(None, "tp", None),
        ),
        out_specs=P("seq", "tp"),
        check_vma=False,
    )
```

```python
import functools

import jax
import jax.numpy as jnp
from jax import lax
from jax.experimental import pallas as pl
from jax.experimental.pallas import tpu as pltpu
from jax.sharding import PartitionSpec as P

HEAD = 64
CH = 2048
TAPS = 31
HALO = 16
HEADS_HERE = 4
RING = 8
DEPTH = 8
LOG2E = 1.4426950408889634
LN2 = 0.6931471805599453
F32 = jnp.float32
BF16 = jnp.bfloat16
MESH = pl.DeviceIdType.MESH


def low_lanes(rows):
    return lax.broadcasted_iota(jnp.int32, (rows, 128), 1) < HEAD


def depthwise(pad_ref, taps_ref, column, rows):
    lanes = pl.ds(column, 128)
    total = jnp.zeros((rows, 128), F32)
    for phase in range(8):
        shifted = pad_ref[pl.ds(phase, rows + 24 if phase else rows + 32), lanes]
        for start in range(0, 33, 8):
            j = start + phase - 1
            if 0 <= j < TAPS:
                total = total + taps_ref[pl.ds(j, 1), lanes] * shifted[start : start + rows]
    return total


def kernel(
    seq_size,
    tp_size,
    frames_hbm,
    query_hbm,
    key_hbm,
    value_hbm,
    w_out_hbm,
    w_in_hbm,
    w_conv_hbm,
    w_proj_hbm,
    w_blend_hbm,
    w_merge_hbm,
    out,
    frames,
    query,
    key,
    value,
    w_out,
    w_in,
    w_conv,
    w_proj,
    w_blend,
    w_merge,
    kv_send,
    q_send,
    kv_all,
    kv_ones,
    q_all,
    o_send,
    o_recv,
    gate_half,
    resid_half,
    gate_prev,
    gate_next,
    stat_send,
    stat_recv,
    stat_prev,
    stat_next,
    gate_pad,
    part_send,
    part_recv,
    part_prev,
    part_next,
    blend_pad,
    taps_pad,
    fin_acc,
    fin_send,
    fin_recv,
    near_sem,
    weight_sem,
    kv_ss,
    kv_rs,
    across_ss,
    direct_ss,
    across_rs,
    q_ss,
    q_rs,
    o_ss,
    o_rs,
    gate_ss,
    gate_rs,
    stat_ss,
    stat_rs,
    stat_hs,
    stat_hr,
    part_ss,
    part_rs,
    part_hs,
    part_hr,
    fin_ss,
    fin_rs,
):
    rows = query.shape[0]
    wide = rows + 2 * HALO
    seq = lax.axis_index("seq")
    tp = lax.axis_index("tp")
    groups = 2 * DEPTH
    sides = seq_size // (RING * DEPTH)
    nearby = 2 * RING
    y_at = lax.rem(seq, RING)
    z_at = lax.rem(seq // RING, DEPTH)
    x_at = seq // (RING * DEPTH)
    group = 2 * z_at + lax.rem(y_at, 2)
    head_at = lax.rem(group, HEADS_HERE)
    place = lax.rem(z_at, 2) * RING + y_at
    across = lax.rem(seq + RING * DEPTH, seq_size)
    after = lax.rem(seq + 1, seq_size)
    before = lax.rem(seq + seq_size - 1, seq_size)

    def group_seq(other):
        return (x_at * DEPTH + other // 2) * RING + 2 * (y_at // 2) + lax.rem(other, 2)

    def group_peer(i):
        other = lax.rem(group + i, groups)
        return other, group_seq(other)

    def key_peer(i):
        y = lax.rem(y_at + lax.rem(i, RING), RING)
        z_low = lax.rem(z_at + i // RING, 2)
        return 2 * z_low + lax.rem(y, 2), (x_at * DEPTH + 2 * (z_at // 2) + z_low) * RING + y

    def key_place(i):
        y = lax.rem(y_at + RING - lax.rem(i, RING), RING)
        return lax.rem(z_at + i // RING, 2) * RING + y

    def tp_peer(i):
        return 2 * lax.rem(tp // 2 + i // 2, tp_size // 2) + lax.rem(tp + i, 2)

    def send(src, dst, send_sem, recv_sem, to_seq, to_tp):
        return pltpu.make_async_remote_copy(
            src_ref=src,
            dst_ref=dst,
            send_sem=send_sem,
            recv_sem=recv_sem,
            device_id=(to_seq, to_tp),
            device_id_type=MESH,
        )

    near = [
        pltpu.make_async_copy(src, dst, near_sem.at[i])
        for i, (src, dst) in enumerate(
            (
                (key_hbm, key),
                (value_hbm, value),
                (query_hbm, query),
                (frames_hbm, frames),
            )
        )
    ]
    weights = [
        pltpu.make_async_copy(src, dst, weight_sem.at[i])
        for i, (src, dst) in enumerate(
            (
                (w_in_hbm, w_in),
                (w_conv_hbm, w_conv),
                (w_proj_hbm, w_proj),
                (w_blend_hbm, w_blend),
                (w_merge_hbm, w_merge),
                (w_out_hbm, w_out),
            )
        )
    ]
    for copy in near[:3]:
        copy.start()

    def hops(i):
        return min(i % RING, RING - i % RING) + i // RING

    near_first = sorted(range(1, nearby), key=hops)
    direct = [i for i in range(1, nearby) if i % RING in (0, 1, RING - 1)]
    relayed = [i for i in near_first if i not in direct]

    first, last = seq == 0, seq == seq_size - 1

    def halo_start(copies):
        pl.when(jnp.logical_not(last))(copies[0].start)
        pl.when(jnp.logical_not(first))(copies[1].start)

    def halo_sent(copies):
        pl.when(jnp.logical_not(last))(copies[0].wait_send)
        pl.when(jnp.logical_not(first))(copies[1].wait_send)

    def halo_arrived(copies):
        pl.when(jnp.logical_not(first))(copies[0].wait_recv)
        pl.when(jnp.logical_not(last))(copies[1].wait_recv)

    @pl.when(first)
    def _():
        for ref in (gate_prev, stat_prev, part_prev):
            ref[...] = jnp.zeros(ref.shape, ref.dtype)

    @pl.when(last)
    def _():
        for ref in (gate_next, stat_next, part_next):
            ref[...] = jnp.zeros(ref.shape, ref.dtype)

    barrier = pltpu.get_barrier_semaphore()

    def greet(to_seq, to_tp):
        pl.semaphore_signal(barrier, inc=1, device_id=(to_seq, to_tp), device_id_type=MESH)

    far_groups = sorted(range(1, groups), key=lambda i: -min(i // 2, DEPTH - i // 2))
    for to_group, to_key in zip(far_groups, reversed(near_first)):
        greet(group_peer(to_group)[1], tp)
        greet(key_peer(to_key)[1], tp)
    for i in direct:
        greet(lax.rem(key_peer(i)[1] + RING * DEPTH, seq_size), tp)
    for i in range(tp_size):
        greet(after, i)
        greet(before, i)
    greet(across, tp)
    for i in range(1, tp_size):
        greet(seq, tp_peer(i))
    for copy in near[3:] + weights:
        copy.start()

    for copy in near[:3]:
        copy.wait()
    low = low_lanes(rows)
    for pair in range(HEADS_HERE // 2):
        lanes = pl.ds(pair * 128, 128)
        k2 = key[:, lanes].astype(F32)
        v2 = value[:, lanes].astype(F32)
        q2 = query[:, lanes].astype(F32)
        kv_send[2 * pair] = jnp.where(low, k2, pltpu.roll(v2, HEAD, 1)).astype(BF16)
        kv_send[2 * pair + 1] = jnp.where(low, pltpu.roll(k2, HEAD, 1), v2).astype(BF16)
        for h, q in ((2 * pair, q2), (2 * pair + 1, pltpu.roll(q2, HEAD, 1))):
            q_send[h, pl.ds(0, HALO)] = jnp.where(
                low_lanes(HALO), q[:HALO], pltpu.roll(q[2 * HALO :], HEAD, 1)
            ).astype(BF16)
            q_send[h, pl.ds(HALO, HALO)] = q[HALO : 2 * HALO].astype(BF16)
    kv_all[x_at * nearby + place] = kv_send[head_at]
    q_all[group] = q_send[head_at]

    pl.semaphore_wait(barrier, (groups - 1) + nearby + len(direct) + (tp_size - 1) + 2 * tp_size)

    def kv_copy(i):
        other, to = key_peer(i)
        return send(
            kv_send.at[other], kv_all.at[x_at * nearby + place], kv_ss.at[i], kv_rs.at[i], to, tp
        )

    def direct_copy(i):
        other, to = key_peer(i)
        to = lax.rem(to + RING * DEPTH, seq_size)
        return send(
            kv_send.at[other],
            kv_all.at[x_at * nearby + place],
            direct_ss.at[i],
            across_rs.at[place],
            to,
            tp,
        )

    def across_copy(at):
        slot = kv_all.at[x_at * nearby + at]
        return send(slot, slot, across_ss.at[at], across_rs.at[at], across, tp)

    def q_copy(i):
        other, to = group_peer(i)
        return send(
            q_send.at[lax.rem(other, HEADS_HERE)],
            q_all.at[group],
            q_ss.at[i],
            q_rs.at[i],
            to,
            tp,
        )

    for i in reversed(relayed):
        kv_copy(i).start()
    across_copy(place).start()
    for i in direct:
        direct_copy(i).start()
    for i in direct:
        kv_copy(i).start()

    near[3].wait()
    features = frames[...].astype(F32)
    centered = features - jnp.mean(features, -1, keepdims=True)
    variance = jnp.mean(centered * centered, -1, keepdims=True)
    normed = (centered * lax.rsqrt(variance + 1e-05)).astype(BF16)

    weights[0].wait()

    def hidden_half(half):
        product = jnp.dot(normed, w_in[:, half, :], preferred_element_type=F32)
        return (0.5 * product * (1.0 + lax.erf(product * 0.7071067811865476))).astype(BF16)

    gate = hidden_half(1)
    gate_half[...] = gate
    gate_float = gate.astype(F32)
    sums = jnp.sum(gate_float, -1, keepdims=True)
    squares = jnp.sum(gate_float * gate_float, -1, keepdims=True)
    stat_lane = lax.broadcasted_iota(jnp.int32, (8, 128), 1)
    stats = jnp.zeros((8, 128), F32)
    for k in range(rows // 8):
        at = slice(8 * k, 8 * k + 8)
        stats = jnp.where(stat_lane // 8 == k, sums[at], stats)
        stats = jnp.where(stat_lane // 8 == 8 + k, squares[at], stats)
    stat_send[...] = stats

    tail = pl.ds(rows - HALO, HALO)
    head = pl.ds(0, HALO)

    def gate_copies():
        return (
            send(gate_half.at[tail], gate_prev, gate_ss.at[0], gate_rs.at[0], after, tp),
            send(gate_half.at[head], gate_next, gate_ss.at[1], gate_rs.at[1], before, tp),
        )

    def stat_copy(i):
        return send(
            stat_send, stat_recv.at[tp], stat_ss.at[i], stat_rs.at[i], seq, tp_peer(i)
        )

    def stat_halo(i):
        to = tp_peer(i)
        return (
            send(stat_send, stat_prev.at[tp], stat_hs.at[0, i], stat_hr.at[0, i], after, to),
            send(stat_send, stat_next.at[tp], stat_hs.at[1, i], stat_hr.at[1, i], before, to),
        )

    for i in reversed(range(tp_size)):
        halo_start(stat_halo(i))
    halo_start(gate_copies())
    for i in reversed(range(1, tp_size)):
        stat_copy(i).start()
    stat_recv[tp] = stat_send[...]

    def hand_on(chosen):
        for i in chosen:
            kv_copy(i).wait_recv()
            across_copy(key_place(i)).start()

    hand_on(relayed[:4])
    for i in sorted(range(1, groups), key=lambda i: -min(i // 2, DEPTH - i // 2)):
        q_copy(i).start()
    hand_on(relayed[4:])
    resid_half[...] = hidden_half(0)
    for i in direct:
        kv_copy(i).wait_recv()

    @pl.loop(1, tp_size)
    def _(i):
        stat_copy(i).wait_recv()

    @pl.loop(0, tp_size)
    def _(i):
        halo_arrived(stat_halo(i))

    halo_arrived(gate_copies())

    def gate_normed(part, stats, blocks, keep):
        total = jnp.sum(stats[...], 0) / CH
        average = jnp.concatenate([total[:, 8 * k : 8 * k + 1] for k in blocks], 0)
        square = jnp.concatenate([total[:, HEAD + 8 * k : HEAD + 8 * k + 1] for k in blocks], 0)
        variance = square - average * average
        result = (part[...].astype(F32) - average) * lax.rsqrt(variance + 1e-05)
        result = result.astype(BF16).astype(F32)
        return result if keep is None else jnp.where(keep, result, 0.0)

    gate_pad[pl.ds(0, HALO)] = gate_normed(gate_prev, stat_prev, range(rows // 8 - 2, rows // 8), jnp.logical_not(first))
    gate_pad[pl.ds(HALO, rows)] = gate_normed(gate_half, stat_recv, range(rows // 8), None)
    gate_pad[pl.ds(HALO + rows, HALO)] = gate_normed(gate_next, stat_next, range(2), jnp.logical_not(last))
    weights[1].wait()
    weights[2].wait()
    gated = []
    for column in range(0, resid_half.shape[1], 128):
        conv = depthwise(gate_pad, w_conv, column, rows)
        resid = resid_half[:, pl.ds(column, 128)].astype(F32)
        gated.append((resid * conv).astype(BF16))

    width = out.shape[1]

    def part_copy(which, i):
        to = tp_peer(i)
        return send(
            part_send.at[which, to],
            part_recv.at[which, tp],
            part_ss.at[which, i],
            part_rs.at[which, i],
            seq,
            to,
        )

    def part_halo(which, i):
        to = tp_peer(i)
        return (
            send(
                part_send.at[which, to, tail],
                part_prev.at[which, tp],
                part_hs.at[which, 0, i],
                part_hr.at[which, 0, i],
                after,
                to,
            ),
            send(
                part_send.at[which, to, head],
                part_next.at[which, tp],
                part_hs.at[which, 1, i],
                part_hr.at[which, 1, i],
                before,
                to,
            ),
        )

    def columns_of(to):
        return pl.ds(pl.multiple_of(to * width, width), width)

    def scatter_part(which, rows_here, weight):
        for i in reversed(range(tp_size)):
            to = tp_peer(i)
            piece = jnp.dot(rows_here, weight[:, columns_of(to)], preferred_element_type=F32)
            part_send[which, to] = piece.astype(BF16)
            halo_start(part_halo(which, i))
            if i:
                part_copy(which, i).start()
        part_recv[which, tp] = part_send[which, tp]

    def merge_part(which):
        @pl.loop(1, tp_size)
        def _(i):
            part_copy(which, i).wait_recv()

        @pl.loop(0, tp_size)
        def _(i):
            halo_arrived(part_halo(which, i))

        def joined(ref):
            return jnp.sum(ref[which].astype(F32), 0).astype(BF16).astype(F32)

        own = joined(part_recv)
        blend_pad[pl.ds(0, HALO)] = jnp.where(first, 0.0, joined(part_prev))
        blend_pad[pl.ds(HALO, rows)] = own
        blend_pad[pl.ds(HALO + rows, HALO)] = jnp.where(last, 0.0, joined(part_next))
        taps_pad[...] = w_blend[:, which, :]
        mixture = [
            (own[:, c : c + 128] + depthwise(blend_pad, taps_pad, c, rows)).astype(BF16)
            for c in range(0, width, 128)
        ]
        return jnp.concatenate(mixture, 1)

    scatter_part(1, jnp.concatenate(gated, 1), w_proj)

    @pl.loop(1, groups)
    def _(i):
        q_copy(i).wait_recv()

    @pl.loop(0, nearby)
    def _(i):
        across_copy(i).wait_recv()

    keys = sides * nearby * rows
    kv = kv_all[...].reshape(keys, 128)
    kv_ones[...] = jnp.where(low_lanes(keys), jnp.ones((), BF16), kv)

    def o_copy(other):
        return send(
            o_send.at[other], o_recv.at[group], o_ss.at[other], o_rs.at[group], group_seq(other), tp
        )

    per_step = 4

    @pl.loop(0, groups // per_step)
    def _(step):
        start = group + groups + jnp.where(step < 2, 6 + 4 * step, 12 * step - 22)
        count = per_step * rows
        pieces = []
        for i in range(per_step):
            q = q_all[lax.rem(start + i, groups)]
            q_end = pltpu.roll(q[:HALO].astype(F32), HEAD, 1).astype(BF16)
            pieces += [q, q_end]
        q = jnp.concatenate(pieces, 0)
        q = jnp.where(low_lanes(count), q, jnp.zeros((), BF16))
        kv = kv_all[...].reshape(keys, 128)
        scores = lax.dot_general(q, kv, (((1,), (1,)), ((), ())), preferred_element_type=F32)
        peak = jnp.max(scores, -1, keepdims=True)
        weight = jnp.exp2((scores - peak) * (LOG2E * HEAD**-0.5)).astype(BF16)
        mixed = jnp.dot(weight, kv_ones[...], preferred_element_type=F32)
        low_q = low_lanes(count)
        total = jnp.where(low_q, mixed, pltpu.roll(mixed, HEAD, 1))
        level = peak * HEAD**-0.5 + jnp.log(total)
        level_high = level.astype(BF16).astype(F32)
        level_low = level - level_high
        mixed = mixed / total
        lane = lax.broadcasted_iota(jnp.int32, (HALO, 128), 1)
        for i in range(per_step):
            thirds = [slice(i * rows + k * HALO, i * rows + (k + 1) * HALO) for k in range(3)]
            spare = jnp.zeros((HALO, 128), F32)
            for k, at in enumerate(thirds):
                spare = jnp.where(lane // 8 == 2 * k, level_high[at], spare)
                spare = jnp.where(lane // 8 == 2 * k + 1, level_low[at], spare)
            o_low = low_lanes(HALO)
            first_rows = jnp.where(o_low, pltpu.roll(mixed[thirds[2]], HEAD, 1), mixed[thirds[0]])
            other = lax.rem(start + i, groups)
            o_send[other, pl.ds(0, HALO)] = first_rows.astype(BF16)
            o_send[other, pl.ds(HALO, HALO)] = jnp.where(o_low, spare, mixed[thirds[1]]).astype(
                BF16
            )
        for i in range(per_step):
            other = lax.rem(start + i, groups)

            @pl.when(other != group)
            def _():
                o_copy(other).start()

            @pl.when(other == group)
            def _():
                o_recv[other] = o_send[other]

    for i in (3, 4):
        weights[i].wait()
    fin_acc[...] = jnp.dot(merge_part(1), w_merge[1], preferred_element_type=F32)
    weights[5].wait()

    @pl.loop(1, nearby)
    def _(i):
        kv_copy(i).wait_send()
        q_copy(i).wait_send()

    for i in direct:
        direct_copy(i).wait_send()
    for i in relayed:
        across_copy(key_place(i)).wait_send()
    across_copy(place).wait_send()
    halo_sent(gate_copies())

    def sent_part(which):
        @pl.loop(1, tp_size)
        def _(i):
            part_copy(which, i).wait_send()

        @pl.loop(0, tp_size)
        def _(i):
            halo_sent(part_halo(which, i))

    @pl.loop(1, tp_size)
    def _(i):
        stat_copy(i).wait_send()

    @pl.loop(0, tp_size)
    def _(i):
        halo_sent(stat_halo(i))

    sent_part(1)

    def o_arrival(other):
        return send(
            o_send.at[other], o_recv.at[other], o_ss.at[other], o_rs.at[other], group_seq(other), tp
        )

    @pl.loop(1, groups)
    def _(i):
        o_arrival(group_peer(i)[0]).wait_recv()

    heads = []
    for h in range(HEADS_HERE):
        pieces, levels = [], []
        for b in range(groups // HEADS_HERE):
            piece = o_recv[b * HEADS_HERE + h].astype(F32)
            spare = piece[HALO:]
            pieces.append(jnp.concatenate([piece, pltpu.roll(piece[:HALO], HEAD, 1)], 0))
            levels.append(
                jnp.concatenate(
                    [
                        spare[:, 16 * k : 16 * k + 1] + spare[:, 16 * k + 8 : 16 * k + 9]
                        for k in range(3)
                    ],
                    0,
                )
            )
        peak = functools.reduce(jnp.maximum, levels)
        shares = [jnp.exp(level - peak) for level in levels]
        whole = functools.reduce(jnp.add, shares)
        mixed = functools.reduce(jnp.add, [s * p for s, p in zip(shares, pieces)])
        heads.append(mixed / whole)
    attended = jnp.concatenate(
        [
            jnp.where(low, pltpu.roll(heads[2 * pair], HEAD, 1), heads[2 * pair + 1]).astype(BF16)
            for pair in range(HEADS_HERE // 2)
        ],
        1,
    )
    scatter_part(0, attended, w_out)
    mixture = merge_part(0)

    def fin_copy(i):
        to = tp_peer(i)
        return send(fin_send.at[to], fin_recv.at[tp], fin_ss.at[i], fin_rs.at[i], seq, to)

    for i in reversed(range(tp_size)):
        to = tp_peer(i)
        piece = jnp.dot(mixture, w_merge[0, :, columns_of(to)], preferred_element_type=F32)
        fin_send[to] = (fin_acc[:, columns_of(to)] + piece).astype(BF16)
        if i:
            fin_copy(i).start()
    fin_recv[tp] = fin_send[tp]

    @pl.loop(1, groups)
    def _(i):
        o_arrival(group_peer(i)[0]).wait_send()

    sent_part(0)

    @pl.loop(1, tp_size)
    def _(i):
        fin_copy(i).wait_recv()

    own = frames[:, pl.ds(pl.multiple_of(tp * width, width), width)].astype(F32)
    out[...] = (own + jnp.sum(fin_recv[...].astype(F32), 0)).astype(BF16)

    for i in range(1, tp_size):
        fin_copy(i).wait_send()


def solution(mesh):
    seq_size, tp_size = mesh.shape["seq"], mesh.shape["tp"]

    def on_device(*args):
        frames, query, key, value, w_out, w_in, w_conv, w_proj, w_blend, w_merge = args
        rows, width = query.shape
        features = frames.shape[1]
        units = w_in.shape[2]
        groups = 2 * DEPTH
        sources = seq_size // DEPTH * 2
        wide = rows + 2 * HALO
        dma = pltpu.SemaphoreType.DMA
        vmem = pltpu.VMEM
        return pl.pallas_call(
            functools.partial(kernel, seq_size, tp_size),
            out_shape=jax.ShapeDtypeStruct((rows, width), BF16),
            in_specs=[pl.BlockSpec(memory_space=pltpu.HBM)] * 10,
            out_specs=pl.BlockSpec(memory_space=pltpu.VMEM),
            scratch_shapes=[
                vmem(frames.shape, BF16),
                vmem(query.shape, BF16),
                vmem(key.shape, BF16),
                vmem(value.shape, BF16),
                vmem(w_out.shape, BF16),
                vmem(w_in.shape, BF16),
                vmem(w_conv.shape, F32),
                vmem(w_proj.shape, BF16),
                vmem(w_blend.shape, F32),
                vmem(w_merge.shape, BF16),
                vmem((HEADS_HERE, rows, 128), BF16),
                vmem((HEADS_HERE, 2 * HALO, 128), BF16),
                vmem((sources, rows, 128), BF16),
                vmem((sources * rows, 128), BF16),
                vmem((groups, 2 * HALO, 128), BF16),
                vmem((groups, 2 * HALO, 128), BF16),
                vmem((groups, 2 * HALO, 128), BF16),
                vmem((rows, units), BF16),
                vmem((rows, units), BF16),
                vmem((HALO, units), BF16),
                vmem((HALO, units), BF16),
                vmem((8, 128), F32),
                vmem((tp_size, 8, 128), F32),
                vmem((tp_size, 8, 128), F32),
                vmem((tp_size, 8, 128), F32),
                vmem((wide, units), F32),
                vmem((2, tp_size, rows, width), BF16),
                vmem((2, tp_size, rows, width), BF16),
                vmem((2, tp_size, HALO, width), BF16),
                vmem((2, tp_size, HALO, width), BF16),
                vmem((wide, width), F32),
                vmem((TAPS, width), F32),
                vmem((rows, features), F32),
                vmem((tp_size, rows, width), BF16),
                vmem((tp_size, rows, width), BF16),
                dma((4,)),
                dma((6,)),
                dma((2 * RING,)),
                dma((2 * RING,)),
                dma((2 * RING,)),
                dma((2 * RING,)),
                dma((2 * RING,)),
                dma((groups,)),
                dma((groups,)),
                dma((groups,)),
                dma((groups,)),
                dma((2,)),
                dma((2,)),
                dma((tp_size,)),
                dma((tp_size,)),
                dma((2, tp_size)),
                dma((2, tp_size)),
                dma((2, tp_size)),
                dma((2, tp_size)),
                dma((2, 2, tp_size)),
                dma((2, 2, tp_size)),
                dma((tp_size,)),
                dma((tp_size,)),
            ],
            compiler_params=pltpu.CompilerParams(
                collective_id=0,
                has_side_effects=True,
                vmem_limit_bytes=63 * 1024 * 1024,
            ),
        )(*args)

    return jax.shard_map(
        on_device,
        mesh=mesh,
        in_specs=(
            P("seq", None),
            P("seq", "tp"),
            P("seq", "tp"),
            P("seq", "tp"),
            P("tp", None),
            P(None, None, "tp"),
            P(None, "tp"),
            P("tp", None),
            P(None, None, "tp"),
            P(None, "tp", None),
        ),
        out_specs=P("seq", "tp"),
        check_vma=False,
    )
```

```python
import functools

import jax
import jax.numpy as jnp
from jax import lax
from jax.experimental import pallas as pl
from jax.experimental.pallas import tpu as pltpu
from jax.sharding import PartitionSpec as P

HEAD = 64
CH = 2048
TAPS = 31
HALO = 16
HEADS_HERE = 4
RING = 8
DEPTH = 8
LOG2E = 1.4426950408889634
LN2 = 0.6931471805599453
F32 = jnp.float32
BF16 = jnp.bfloat16
MESH = pl.DeviceIdType.MESH


def low_lanes(rows):
    return lax.broadcasted_iota(jnp.int32, (rows, 128), 1) < HEAD


def depthwise(pad_ref, taps_ref, column, rows):
    lanes = pl.ds(column, 128)
    total = jnp.zeros((rows, 128), F32)
    for phase in range(8):
        shifted = pad_ref[pl.ds(phase, rows + 24 if phase else rows + 32), lanes]
        for start in range(0, 33, 8):
            j = start + phase - 1
            if 0 <= j < TAPS:
                total = total + taps_ref[pl.ds(j, 1), lanes] * shifted[start : start + rows]
    return total


def kernel(
    seq_size,
    tp_size,
    frames_hbm,
    query_hbm,
    key_hbm,
    value_hbm,
    w_out_hbm,
    w_in_hbm,
    w_conv_hbm,
    w_proj_hbm,
    w_blend_hbm,
    w_merge_hbm,
    out,
    frames,
    query,
    key,
    value,
    w_out,
    w_in,
    w_conv,
    w_proj,
    w_blend,
    w_merge,
    kv_send,
    q_send,
    kv_all,
    kv_ones,
    q_all,
    o_send,
    o_recv,
    gate_half,
    resid_half,
    gate_prev,
    gate_next,
    stat_send,
    stat_recv,
    stat_prev,
    stat_next,
    gate_pad,
    part_send,
    part_recv,
    part_prev,
    part_next,
    blend_pad,
    taps_pad,
    fin_acc,
    fin_send,
    fin_recv,
    near_sem,
    weight_sem,
    kv_ss,
    kv_rs,
    across_ss,
    direct_ss,
    across_rs,
    q_ss,
    q_rs,
    o_ss,
    o_rs,
    gate_ss,
    gate_rs,
    stat_ss,
    stat_rs,
    stat_hs,
    stat_hr,
    part_ss,
    part_rs,
    part_hs,
    part_hr,
    fin_ss,
    fin_rs,
):
    rows = query.shape[0]
    wide = rows + 2 * HALO
    seq = lax.axis_index("seq")
    tp = lax.axis_index("tp")
    groups = 2 * DEPTH
    sides = seq_size // (RING * DEPTH)
    nearby = 2 * RING
    y_at = lax.rem(seq, RING)
    z_at = lax.rem(seq // RING, DEPTH)
    x_at = seq // (RING * DEPTH)
    group = 2 * z_at + lax.rem(y_at, 2)
    head_at = lax.rem(group, HEADS_HERE)
    place = lax.rem(z_at, 2) * RING + y_at
    across = lax.rem(seq + RING * DEPTH, seq_size)
    after = lax.rem(seq + 1, seq_size)
    before = lax.rem(seq + seq_size - 1, seq_size)

    def group_seq(other):
        return (x_at * DEPTH + other // 2) * RING + 2 * (y_at // 2) + lax.rem(other, 2)

    def group_peer(i):
        other = lax.rem(group + i, groups)
        return other, group_seq(other)

    def key_peer(i):
        y = lax.rem(y_at + lax.rem(i, RING), RING)
        z_low = lax.rem(z_at + i // RING, 2)
        return 2 * z_low + lax.rem(y, 2), (x_at * DEPTH + 2 * (z_at // 2) + z_low) * RING + y

    def key_place(i):
        y = lax.rem(y_at + RING - lax.rem(i, RING), RING)
        return lax.rem(z_at + i // RING, 2) * RING + y

    def tp_peer(i):
        return 2 * lax.rem(tp // 2 + i // 2, tp_size // 2) + lax.rem(tp + i, 2)

    def send(src, dst, send_sem, recv_sem, to_seq, to_tp):
        return pltpu.make_async_remote_copy(
            src_ref=src,
            dst_ref=dst,
            send_sem=send_sem,
            recv_sem=recv_sem,
            device_id=(to_seq, to_tp),
            device_id_type=MESH,
        )

    near = [
        pltpu.make_async_copy(src, dst, near_sem.at[i])
        for i, (src, dst) in enumerate(
            (
                (key_hbm, key),
                (value_hbm, value),
                (query_hbm, query),
                (frames_hbm, frames),
            )
        )
    ]
    weights = [
        pltpu.make_async_copy(src, dst, weight_sem.at[i])
        for i, (src, dst) in enumerate(
            (
                (w_in_hbm, w_in),
                (w_conv_hbm, w_conv),
                (w_proj_hbm, w_proj),
                (w_blend_hbm, w_blend),
                (w_merge_hbm, w_merge),
                (w_out_hbm, w_out),
            )
        )
    ]
    for copy in near[:3]:
        copy.start()

    def hops(i):
        return min(i % RING, RING - i % RING) + i // RING

    near_first = sorted(range(1, nearby), key=hops)
    direct = [i for i in range(1, nearby) if i % RING in (0, 1, RING - 1)]
    relayed = [i for i in near_first if i not in direct]

    first, last = seq == 0, seq == seq_size - 1

    def halo_start(copies):
        pl.when(jnp.logical_not(last))(copies[0].start)
        pl.when(jnp.logical_not(first))(copies[1].start)

    def halo_sent(copies):
        pl.when(jnp.logical_not(last))(copies[0].wait_send)
        pl.when(jnp.logical_not(first))(copies[1].wait_send)

    def halo_arrived(copies):
        pl.when(jnp.logical_not(first))(copies[0].wait_recv)
        pl.when(jnp.logical_not(last))(copies[1].wait_recv)

    @pl.when(first)
    def _():
        for ref in (gate_prev, stat_prev, part_prev):
            ref[...] = jnp.zeros(ref.shape, ref.dtype)

    @pl.when(last)
    def _():
        for ref in (gate_next, stat_next, part_next):
            ref[...] = jnp.zeros(ref.shape, ref.dtype)

    barrier = pltpu.get_barrier_semaphore()

    def greet(to_seq, to_tp):
        pl.semaphore_signal(barrier, inc=1, device_id=(to_seq, to_tp), device_id_type=MESH)

    far_groups = sorted(range(1, groups), key=lambda i: -min(i // 2, DEPTH - i // 2))
    for to_group, to_key in zip(far_groups, reversed(near_first)):
        greet(group_peer(to_group)[1], tp)
        greet(key_peer(to_key)[1], tp)
    for i in direct:
        greet(lax.rem(key_peer(i)[1] + RING * DEPTH, seq_size), tp)
    for i in range(tp_size):
        greet(after, i)
        greet(before, i)
    greet(across, tp)
    for i in range(1, tp_size):
        greet(seq, tp_peer(i))
    for copy in near[3:] + weights:
        copy.start()

    for copy in near[:3]:
        copy.wait()
    low = low_lanes(rows)
    for pair in range(HEADS_HERE // 2):
        lanes = pl.ds(pair * 128, 128)
        k2 = key[:, lanes].astype(F32)
        v2 = value[:, lanes].astype(F32)
        q2 = query[:, lanes].astype(F32)
        kv_send[2 * pair] = jnp.where(low, k2, pltpu.roll(v2, HEAD, 1)).astype(BF16)
        kv_send[2 * pair + 1] = jnp.where(low, pltpu.roll(k2, HEAD, 1), v2).astype(BF16)
        for h, q in ((2 * pair, q2), (2 * pair + 1, pltpu.roll(q2, HEAD, 1))):
            q_send[h, pl.ds(0, HALO)] = jnp.where(
                low_lanes(HALO), q[:HALO], pltpu.roll(q[2 * HALO :], HEAD, 1)
            ).astype(BF16)
            q_send[h, pl.ds(HALO, HALO)] = q[HALO : 2 * HALO].astype(BF16)
    kv_all[x_at * nearby + place] = kv_send[head_at]
    q_all[group] = q_send[head_at]

    pl.semaphore_wait(barrier, (groups - 1) + nearby + len(direct) + (tp_size - 1) + 2 * tp_size)

    def kv_copy(i):
        other, to = key_peer(i)
        return send(
            kv_send.at[other], kv_all.at[x_at * nearby + place], kv_ss.at[i], kv_rs.at[i], to, tp
        )

    def direct_copy(i):
        other, to = key_peer(i)
        to = lax.rem(to + RING * DEPTH, seq_size)
        return send(
            kv_send.at[other],
            kv_all.at[x_at * nearby + place],
            direct_ss.at[i],
            across_rs.at[place],
            to,
            tp,
        )

    def across_copy(at):
        slot = kv_all.at[x_at * nearby + at]
        return send(slot, slot, across_ss.at[at], across_rs.at[at], across, tp)

    def q_copy(i):
        other, to = group_peer(i)
        return send(
            q_send.at[lax.rem(other, HEADS_HERE)],
            q_all.at[group],
            q_ss.at[i],
            q_rs.at[i],
            to,
            tp,
        )

    for i in reversed(relayed):
        kv_copy(i).start()
    across_copy(place).start()
    for i in direct:
        direct_copy(i).start()
    for i in direct:
        kv_copy(i).start()

    near[3].wait()
    features = frames[...].astype(F32)
    centered = features - jnp.mean(features, -1, keepdims=True)
    variance = jnp.mean(centered * centered, -1, keepdims=True)
    normed = (centered * lax.rsqrt(variance + 1e-05)).astype(BF16)

    for i in sorted(range(1, groups), key=lambda i: -min(i // 2, DEPTH - i // 2)):
        q_copy(i).start()

    weights[0].wait()

    def hidden_half(half):
        product = jnp.dot(normed, w_in[:, half, :], preferred_element_type=F32)
        return (0.5 * product * (1.0 + lax.erf(product * 0.7071067811865476))).astype(BF16)

    gate = hidden_half(1)
    gate_half[...] = gate
    gate_float = gate.astype(F32)
    sums = jnp.sum(gate_float, -1, keepdims=True)
    squares = jnp.sum(gate_float * gate_float, -1, keepdims=True)
    stat_lane = lax.broadcasted_iota(jnp.int32, (8, 128), 1)
    stats = jnp.zeros((8, 128), F32)
    for k in range(rows // 8):
        at = slice(8 * k, 8 * k + 8)
        stats = jnp.where(stat_lane // 8 == k, sums[at], stats)
        stats = jnp.where(stat_lane // 8 == 8 + k, squares[at], stats)
    stat_send[...] = stats

    tail = pl.ds(rows - HALO, HALO)
    head = pl.ds(0, HALO)

    def gate_copies():
        return (
            send(gate_half.at[tail], gate_prev, gate_ss.at[0], gate_rs.at[0], after, tp),
            send(gate_half.at[head], gate_next, gate_ss.at[1], gate_rs.at[1], before, tp),
        )

    def stat_copy(i):
        return send(
            stat_send, stat_recv.at[tp], stat_ss.at[i], stat_rs.at[i], seq, tp_peer(i)
        )

    def stat_halo(i):
        to = tp_peer(i)
        return (
            send(stat_send, stat_prev.at[tp], stat_hs.at[0, i], stat_hr.at[0, i], after, to),
            send(stat_send, stat_next.at[tp], stat_hs.at[1, i], stat_hr.at[1, i], before, to),
        )

    for i in reversed(range(tp_size)):
        halo_start(stat_halo(i))
    halo_start(gate_copies())
    for i in reversed(range(1, tp_size)):
        stat_copy(i).start()
    stat_recv[tp] = stat_send[...]

    def hand_on(chosen):
        for i in chosen:
            kv_copy(i).wait_recv()
            across_copy(key_place(i)).start()

    hand_on(relayed[:4])
    hand_on(relayed[4:])
    resid_half[...] = hidden_half(0)
    for i in direct:
        kv_copy(i).wait_recv()

    @pl.loop(1, tp_size)
    def _(i):
        stat_copy(i).wait_recv()

    @pl.loop(0, tp_size)
    def _(i):
        halo_arrived(stat_halo(i))

    halo_arrived(gate_copies())

    def gate_normed(part, stats, blocks, keep):
        total = jnp.sum(stats[...], 0) / CH
        average = jnp.concatenate([total[:, 8 * k : 8 * k + 1] for k in blocks], 0)
        square = jnp.concatenate([total[:, HEAD + 8 * k : HEAD + 8 * k + 1] for k in blocks], 0)
        variance = square - average * average
        result = (part[...].astype(F32) - average) * lax.rsqrt(variance + 1e-05)
        result = result.astype(BF16).astype(F32)
        return result if keep is None else jnp.where(keep, result, 0.0)

    gate_pad[pl.ds(0, HALO)] = gate_normed(gate_prev, stat_prev, range(rows // 8 - 2, rows // 8), jnp.logical_not(first))
    gate_pad[pl.ds(HALO, rows)] = gate_normed(gate_half, stat_recv, range(rows // 8), None)
    gate_pad[pl.ds(HALO + rows, HALO)] = gate_normed(gate_next, stat_next, range(2), jnp.logical_not(last))
    weights[1].wait()
    weights[2].wait()
    gated = []
    for column in range(0, resid_half.shape[1], 128):
        conv = depthwise(gate_pad, w_conv, column, rows)
        resid = resid_half[:, pl.ds(column, 128)].astype(F32)
        gated.append((resid * conv).astype(BF16))

    width = out.shape[1]

    def part_copy(which, i):
        to = tp_peer(i)
        return send(
            part_send.at[which, to],
            part_recv.at[which, tp],
            part_ss.at[which, i],
            part_rs.at[which, i],
            seq,
            to,
        )

    def part_halo(which, i):
        to = tp_peer(i)
        return (
            send(
                part_send.at[which, to, tail],
                part_prev.at[which, tp],
                part_hs.at[which, 0, i],
                part_hr.at[which, 0, i],
                after,
                to,
            ),
            send(
                part_send.at[which, to, head],
                part_next.at[which, tp],
                part_hs.at[which, 1, i],
                part_hr.at[which, 1, i],
                before,
                to,
            ),
        )

    def columns_of(to):
        return pl.ds(pl.multiple_of(to * width, width), width)

    def scatter_part(which, rows_here, weight):
        for i in reversed(range(tp_size)):
            to = tp_peer(i)
            piece = jnp.dot(rows_here, weight[:, columns_of(to)], preferred_element_type=F32)
            part_send[which, to] = piece.astype(BF16)
            halo_start(part_halo(which, i))
            if i:
                part_copy(which, i).start()
        part_recv[which, tp] = part_send[which, tp]

    def merge_part(which):
        @pl.loop(1, tp_size)
        def _(i):
            part_copy(which, i).wait_recv()

        @pl.loop(0, tp_size)
        def _(i):
            halo_arrived(part_halo(which, i))

        def joined(ref):
            return jnp.sum(ref[which].astype(F32), 0).astype(BF16).astype(F32)

        own = joined(part_recv)
        blend_pad[pl.ds(0, HALO)] = jnp.where(first, 0.0, joined(part_prev))
        blend_pad[pl.ds(HALO, rows)] = own
        blend_pad[pl.ds(HALO + rows, HALO)] = jnp.where(last, 0.0, joined(part_next))
        taps_pad[...] = w_blend[:, which, :]
        mixture = [
            (own[:, c : c + 128] + depthwise(blend_pad, taps_pad, c, rows)).astype(BF16)
            for c in range(0, width, 128)
        ]
        return jnp.concatenate(mixture, 1)

    @pl.loop(1, groups)
    def _(i):
        q_copy(i).wait_recv()

    @pl.loop(0, nearby)
    def _(i):
        across_copy(i).wait_recv()

    keys = sides * nearby * rows
    kv = kv_all[...].reshape(keys, 128)
    kv_ones[...] = jnp.where(low_lanes(keys), jnp.ones((), BF16), kv)

    def o_copy(other):
        return send(
            o_send.at[other], o_recv.at[group], o_ss.at[other], o_rs.at[group], group_seq(other), tp
        )

    per_step = 4

    @pl.loop(0, groups // per_step)
    def _(step):
        start = group + groups + jnp.where(step < 2, 6 + 4 * step, 12 * step - 22)
        count = per_step * rows
        pieces = []
        for i in range(per_step):
            q = q_all[lax.rem(start + i, groups)]
            q_end = pltpu.roll(q[:HALO].astype(F32), HEAD, 1).astype(BF16)
            pieces += [q, q_end]
        q = jnp.concatenate(pieces, 0)
        q = jnp.where(low_lanes(count), q, jnp.zeros((), BF16))
        kv = kv_all[...].reshape(keys, 128)
        scores = lax.dot_general(q, kv, (((1,), (1,)), ((), ())), preferred_element_type=F32)
        peak = jnp.max(scores, -1, keepdims=True)
        weight = jnp.exp2((scores - peak) * (LOG2E * HEAD**-0.5)).astype(BF16)
        mixed = jnp.dot(weight, kv_ones[...], preferred_element_type=F32)
        low_q = low_lanes(count)
        total = jnp.where(low_q, mixed, pltpu.roll(mixed, HEAD, 1))
        level = peak * HEAD**-0.5 + jnp.log(total)
        level_high = level.astype(BF16).astype(F32)
        level_low = level - level_high
        mixed = mixed / total
        lane = lax.broadcasted_iota(jnp.int32, (HALO, 128), 1)
        for i in range(per_step):
            thirds = [slice(i * rows + k * HALO, i * rows + (k + 1) * HALO) for k in range(3)]
            spare = jnp.zeros((HALO, 128), F32)
            for k, at in enumerate(thirds):
                spare = jnp.where(lane // 8 == 2 * k, level_high[at], spare)
                spare = jnp.where(lane // 8 == 2 * k + 1, level_low[at], spare)
            o_low = low_lanes(HALO)
            first_rows = jnp.where(o_low, pltpu.roll(mixed[thirds[2]], HEAD, 1), mixed[thirds[0]])
            other = lax.rem(start + i, groups)
            o_send[other, pl.ds(0, HALO)] = first_rows.astype(BF16)
            o_send[other, pl.ds(HALO, HALO)] = jnp.where(o_low, spare, mixed[thirds[1]]).astype(
                BF16
            )
        for i in range(per_step):
            other = lax.rem(start + i, groups)

            @pl.when(other != group)
            def _():
                o_copy(other).start()

            @pl.when(other == group)
            def _():
                o_recv[other] = o_send[other]

    scatter_part(1, jnp.concatenate(gated, 1), w_proj)

    for i in (3, 4):
        weights[i].wait()
    weights[5].wait()

    @pl.loop(1, nearby)
    def _(i):
        kv_copy(i).wait_send()
        q_copy(i).wait_send()

    for i in direct:
        direct_copy(i).wait_send()
    for i in relayed:
        across_copy(key_place(i)).wait_send()
    across_copy(place).wait_send()
    halo_sent(gate_copies())

    def sent_part(which):
        @pl.loop(1, tp_size)
        def _(i):
            part_copy(which, i).wait_send()

        @pl.loop(0, tp_size)
        def _(i):
            halo_sent(part_halo(which, i))

    @pl.loop(1, tp_size)
    def _(i):
        stat_copy(i).wait_send()

    @pl.loop(0, tp_size)
    def _(i):
        halo_sent(stat_halo(i))

    def o_arrival(other):
        return send(
            o_send.at[other], o_recv.at[other], o_ss.at[other], o_rs.at[other], group_seq(other), tp
        )

    @pl.loop(1, groups)
    def _(i):
        o_arrival(group_peer(i)[0]).wait_recv()

    heads = []
    for h in range(HEADS_HERE):
        pieces, levels = [], []
        for b in range(groups // HEADS_HERE):
            piece = o_recv[b * HEADS_HERE + h].astype(F32)
            spare = piece[HALO:]
            pieces.append(jnp.concatenate([piece, pltpu.roll(piece[:HALO], HEAD, 1)], 0))
            levels.append(
                jnp.concatenate(
                    [
                        spare[:, 16 * k : 16 * k + 1] + spare[:, 16 * k + 8 : 16 * k + 9]
                        for k in range(3)
                    ],
                    0,
                )
            )
        peak = functools.reduce(jnp.maximum, levels)
        shares = [jnp.exp(level - peak) for level in levels]
        whole = functools.reduce(jnp.add, shares)
        mixed = functools.reduce(jnp.add, [s * p for s, p in zip(shares, pieces)])
        heads.append(mixed / whole)
    attended = jnp.concatenate(
        [
            jnp.where(low, pltpu.roll(heads[2 * pair], HEAD, 1), heads[2 * pair + 1]).astype(BF16)
            for pair in range(HEADS_HERE // 2)
        ],
        1,
    )
    scatter_part(0, attended, w_out)
    fin_acc[...] = jnp.dot(merge_part(1), w_merge[1], preferred_element_type=F32)
    mixture = merge_part(0)

    def fin_copy(i):
        to = tp_peer(i)
        return send(fin_send.at[to], fin_recv.at[tp], fin_ss.at[i], fin_rs.at[i], seq, to)

    for i in reversed(range(tp_size)):
        to = tp_peer(i)
        piece = jnp.dot(mixture, w_merge[0, :, columns_of(to)], preferred_element_type=F32)
        fin_send[to] = (fin_acc[:, columns_of(to)] + piece).astype(BF16)
        if i:
            fin_copy(i).start()
    fin_recv[tp] = fin_send[tp]

    @pl.loop(1, groups)
    def _(i):
        o_arrival(group_peer(i)[0]).wait_send()

    sent_part(0)
    sent_part(1)

    @pl.loop(1, tp_size)
    def _(i):
        fin_copy(i).wait_recv()

    own = frames[:, pl.ds(pl.multiple_of(tp * width, width), width)].astype(F32)
    out[...] = (own + jnp.sum(fin_recv[...].astype(F32), 0)).astype(BF16)

    for i in range(1, tp_size):
        fin_copy(i).wait_send()


def solution(mesh):
    seq_size, tp_size = mesh.shape["seq"], mesh.shape["tp"]

    def on_device(*args):
        frames, query, key, value, w_out, w_in, w_conv, w_proj, w_blend, w_merge = args
        rows, width = query.shape
        features = frames.shape[1]
        units = w_in.shape[2]
        groups = 2 * DEPTH
        sources = seq_size // DEPTH * 2
        wide = rows + 2 * HALO
        dma = pltpu.SemaphoreType.DMA
        vmem = pltpu.VMEM
        return pl.pallas_call(
            functools.partial(kernel, seq_size, tp_size),
            out_shape=jax.ShapeDtypeStruct((rows, width), BF16),
            in_specs=[pl.BlockSpec(memory_space=pltpu.HBM)] * 10,
            out_specs=pl.BlockSpec(memory_space=pltpu.VMEM),
            scratch_shapes=[
                vmem(frames.shape, BF16),
                vmem(query.shape, BF16),
                vmem(key.shape, BF16),
                vmem(value.shape, BF16),
                vmem(w_out.shape, BF16),
                vmem(w_in.shape, BF16),
                vmem(w_conv.shape, F32),
                vmem(w_proj.shape, BF16),
                vmem(w_blend.shape, F32),
                vmem(w_merge.shape, BF16),
                vmem((HEADS_HERE, rows, 128), BF16),
                vmem((HEADS_HERE, 2 * HALO, 128), BF16),
                vmem((sources, rows, 128), BF16),
                vmem((sources * rows, 128), BF16),
                vmem((groups, 2 * HALO, 128), BF16),
                vmem((groups, 2 * HALO, 128), BF16),
                vmem((groups, 2 * HALO, 128), BF16),
                vmem((rows, units), BF16),
                vmem((rows, units), BF16),
                vmem((HALO, units), BF16),
                vmem((HALO, units), BF16),
                vmem((8, 128), F32),
                vmem((tp_size, 8, 128), F32),
                vmem((tp_size, 8, 128), F32),
                vmem((tp_size, 8, 128), F32),
                vmem((wide, units), F32),
                vmem((2, tp_size, rows, width), BF16),
                vmem((2, tp_size, rows, width), BF16),
                vmem((2, tp_size, HALO, width), BF16),
                vmem((2, tp_size, HALO, width), BF16),
                vmem((wide, width), F32),
                vmem((TAPS, width), F32),
                vmem((rows, features), F32),
                vmem((tp_size, rows, width), BF16),
                vmem((tp_size, rows, width), BF16),
                dma((4,)),
                dma((6,)),
                dma((2 * RING,)),
                dma((2 * RING,)),
                dma((2 * RING,)),
                dma((2 * RING,)),
                dma((2 * RING,)),
                dma((groups,)),
                dma((groups,)),
                dma((groups,)),
                dma((groups,)),
                dma((2,)),
                dma((2,)),
                dma((tp_size,)),
                dma((tp_size,)),
                dma((2, tp_size)),
                dma((2, tp_size)),
                dma((2, tp_size)),
                dma((2, tp_size)),
                dma((2, 2, tp_size)),
                dma((2, 2, tp_size)),
                dma((tp_size,)),
                dma((tp_size,)),
            ],
            compiler_params=pltpu.CompilerParams(
                collective_id=0,
                has_side_effects=True,
                vmem_limit_bytes=63 * 1024 * 1024,
            ),
        )(*args)

    return jax.shard_map(
        on_device,
        mesh=mesh,
        in_specs=(
            P("seq", None),
            P("seq", "tp"),
            P("seq", "tp"),
            P("seq", "tp"),
            P("tp", None),
            P(None, None, "tp"),
            P(None, "tp"),
            P("tp", None),
            P(None, None, "tp"),
            P(None, "tp", None),
        ),
        out_specs=P("seq", "tp"),
        check_vma=False,
    )
```

```python
import functools

import jax
import jax.numpy as jnp
from jax import lax
from jax.experimental import pallas as pl
from jax.experimental.pallas import tpu as pltpu
from jax.sharding import PartitionSpec as P

HEAD = 64
CH = 2048
TAPS = 31
HALO = 16
HEADS_HERE = 4
RING = 8
DEPTH = 8
LOG2E = 1.4426950408889634
LN2 = 0.6931471805599453
F32 = jnp.float32
BF16 = jnp.bfloat16
MESH = pl.DeviceIdType.MESH


def low_lanes(rows):
    return lax.broadcasted_iota(jnp.int32, (rows, 128), 1) < HEAD


def depthwise(pad_ref, taps_ref, column, rows):
    lanes = pl.ds(column, 128)
    total = jnp.zeros((rows, 128), F32)
    for phase in range(8):
        shifted = pad_ref[pl.ds(phase, rows + 24 if phase else rows + 32), lanes]
        for start in range(0, 33, 8):
            j = start + phase - 1
            if 0 <= j < TAPS:
                total = total + taps_ref[pl.ds(j, 1), lanes] * shifted[start : start + rows]
    return total


def kernel(
    seq_size,
    tp_size,
    frames_hbm,
    query_hbm,
    key_hbm,
    value_hbm,
    w_out_hbm,
    w_in_hbm,
    w_conv_hbm,
    w_proj_hbm,
    w_blend_hbm,
    w_merge_hbm,
    out,
    frames,
    query,
    key,
    value,
    w_out,
    w_in,
    w_conv,
    w_proj,
    w_blend,
    w_merge,
    kv_send,
    q_send,
    kv_all,
    kv_ones,
    q_all,
    o_send,
    o_recv,
    gate_half,
    resid_half,
    gate_prev,
    gate_next,
    stat_send,
    stat_recv,
    stat_prev,
    stat_next,
    gate_pad,
    part_send,
    part_recv,
    part_prev,
    part_next,
    blend_pad,
    taps_pad,
    fin_acc,
    fin_send,
    fin_recv,
    near_sem,
    weight_sem,
    kv_ss,
    kv_rs,
    across_ss,
    direct_ss,
    across_rs,
    q_ss,
    q_rs,
    o_ss,
    o_rs,
    gate_ss,
    gate_rs,
    stat_ss,
    stat_rs,
    stat_hs,
    stat_hr,
    part_ss,
    part_rs,
    part_hs,
    part_hr,
    fin_ss,
    fin_rs,
):
    rows = query.shape[0]
    wide = rows + 2 * HALO
    seq = lax.axis_index("seq")
    tp = lax.axis_index("tp")
    groups = 2 * DEPTH
    sides = seq_size // (RING * DEPTH)
    nearby = 2 * RING
    y_at = lax.rem(seq, RING)
    z_at = lax.rem(seq // RING, DEPTH)
    x_at = seq // (RING * DEPTH)
    group = 2 * z_at + lax.rem(y_at, 2)
    head_at = lax.rem(group, HEADS_HERE)
    place = lax.rem(z_at, 2) * RING + y_at
    across = lax.rem(seq + RING * DEPTH, seq_size)
    after = lax.rem(seq + 1, seq_size)
    before = lax.rem(seq + seq_size - 1, seq_size)

    def group_seq(other):
        return (x_at * DEPTH + other // 2) * RING + 2 * (y_at // 2) + lax.rem(other, 2)

    def group_peer(i):
        other = lax.rem(group + i, groups)
        return other, group_seq(other)

    def key_peer(i):
        y = lax.rem(y_at + lax.rem(i, RING), RING)
        z_low = lax.rem(z_at + i // RING, 2)
        return 2 * z_low + lax.rem(y, 2), (x_at * DEPTH + 2 * (z_at // 2) + z_low) * RING + y

    def key_place(i):
        y = lax.rem(y_at + RING - lax.rem(i, RING), RING)
        return lax.rem(z_at + i // RING, 2) * RING + y

    def tp_peer(i):
        return 2 * lax.rem(tp // 2 + i // 2, tp_size // 2) + lax.rem(tp + i, 2)

    def send(src, dst, send_sem, recv_sem, to_seq, to_tp):
        return pltpu.make_async_remote_copy(
            src_ref=src,
            dst_ref=dst,
            send_sem=send_sem,
            recv_sem=recv_sem,
            device_id=(to_seq, to_tp),
            device_id_type=MESH,
        )

    near = [
        pltpu.make_async_copy(src, dst, near_sem.at[i])
        for i, (src, dst) in enumerate(
            (
                (key_hbm, key),
                (value_hbm, value),
                (query_hbm, query),
                (frames_hbm, frames),
            )
        )
    ]
    weights = [
        pltpu.make_async_copy(src, dst, weight_sem.at[i])
        for i, (src, dst) in enumerate(
            (
                (w_in_hbm, w_in),
                (w_conv_hbm, w_conv),
                (w_proj_hbm, w_proj),
                (w_blend_hbm, w_blend),
                (w_merge_hbm, w_merge),
                (w_out_hbm, w_out),
            )
        )
    ]
    for copy in near[:3]:
        copy.start()

    def hops(i):
        return min(i % RING, RING - i % RING) + i // RING

    near_first = sorted(range(1, nearby), key=hops)
    direct = [i for i in range(1, nearby) if i % RING in (0, 1, RING - 1)]
    relayed = [i for i in near_first if i not in direct]

    first, last = seq == 0, seq == seq_size - 1

    def halo_start(copies):
        pl.when(jnp.logical_not(last))(copies[0].start)
        pl.when(jnp.logical_not(first))(copies[1].start)

    def halo_sent(copies):
        pl.when(jnp.logical_not(last))(copies[0].wait_send)
        pl.when(jnp.logical_not(first))(copies[1].wait_send)

    def halo_arrived(copies):
        pl.when(jnp.logical_not(first))(copies[0].wait_recv)
        pl.when(jnp.logical_not(last))(copies[1].wait_recv)

    @pl.when(first)
    def _():
        for ref in (gate_prev, stat_prev, part_prev):
            ref[...] = jnp.zeros(ref.shape, ref.dtype)

    @pl.when(last)
    def _():
        for ref in (gate_next, stat_next, part_next):
            ref[...] = jnp.zeros(ref.shape, ref.dtype)

    barrier = pltpu.get_barrier_semaphore()

    def greet(to_seq, to_tp):
        pl.semaphore_signal(barrier, inc=1, device_id=(to_seq, to_tp), device_id_type=MESH)

    far_groups = sorted(range(1, groups), key=lambda i: -min(i // 2, DEPTH - i // 2))
    for to_group, to_key in zip(far_groups, reversed(near_first)):
        greet(group_peer(to_group)[1], tp)
        greet(key_peer(to_key)[1], tp)
    for i in direct:
        greet(lax.rem(key_peer(i)[1] + RING * DEPTH, seq_size), tp)
    for i in range(tp_size):
        greet(after, i)
        greet(before, i)
    greet(across, tp)
    for i in range(1, tp_size):
        greet(seq, tp_peer(i))
    for copy in near[3:] + weights:
        copy.start()

    for copy in near[:2]:
        copy.wait()
    low = low_lanes(rows)
    for pair in range(HEADS_HERE // 2):
        lanes = pl.ds(pair * 128, 128)
        k2 = key[:, lanes].astype(F32)
        v2 = value[:, lanes].astype(F32)
        kv_send[2 * pair] = jnp.where(low, k2, pltpu.roll(v2, HEAD, 1)).astype(BF16)
        kv_send[2 * pair + 1] = jnp.where(low, pltpu.roll(k2, HEAD, 1), v2).astype(BF16)
    kv_all[x_at * nearby + place] = kv_send[head_at]

    pl.semaphore_wait(barrier, (groups - 1) + nearby + len(direct) + (tp_size - 1) + 2 * tp_size)

    def kv_copy(i):
        other, to = key_peer(i)
        return send(
            kv_send.at[other], kv_all.at[x_at * nearby + place], kv_ss.at[i], kv_rs.at[i], to, tp
        )

    def direct_copy(i):
        other, to = key_peer(i)
        to = lax.rem(to + RING * DEPTH, seq_size)
        return send(
            kv_send.at[other],
            kv_all.at[x_at * nearby + place],
            direct_ss.at[i],
            across_rs.at[place],
            to,
            tp,
        )

    def across_copy(at):
        slot = kv_all.at[x_at * nearby + at]
        return send(slot, slot, across_ss.at[at], across_rs.at[at], across, tp)

    def q_copy(i):
        other, to = group_peer(i)
        return send(
            q_send.at[lax.rem(other, HEADS_HERE)],
            q_all.at[group],
            q_ss.at[i],
            q_rs.at[i],
            to,
            tp,
        )

    for i in reversed(relayed):
        kv_copy(i).start()
    across_copy(place).start()
    for i in direct:
        direct_copy(i).start()
    for i in direct:
        kv_copy(i).start()

    near[3].wait()
    features = frames[...].astype(F32)
    centered = features - jnp.mean(features, -1, keepdims=True)
    variance = jnp.mean(centered * centered, -1, keepdims=True)
    normed = (centered * lax.rsqrt(variance + 1e-05)).astype(BF16)

    near[2].wait()
    for pair in range(HEADS_HERE // 2):
        q2 = query[:, pl.ds(pair * 128, 128)].astype(F32)
        for h, q in ((2 * pair, q2), (2 * pair + 1, pltpu.roll(q2, HEAD, 1))):
            q_send[h, pl.ds(0, HALO)] = jnp.where(
                low_lanes(HALO), q[:HALO], pltpu.roll(q[2 * HALO :], HEAD, 1)
            ).astype(BF16)
            q_send[h, pl.ds(HALO, HALO)] = q[HALO : 2 * HALO].astype(BF16)
    q_all[group] = q_send[head_at]
    for i in sorted(range(1, groups), key=lambda i: -min(i // 2, DEPTH - i // 2)):
        q_copy(i).start()

    weights[0].wait()

    def hidden_half(half):
        product = jnp.dot(normed, w_in[:, half, :], preferred_element_type=F32)
        return (0.5 * product * (1.0 + lax.erf(product * 0.7071067811865476))).astype(BF16)

    gate = hidden_half(1)
    gate_half[...] = gate
    gate_float = gate.astype(F32)
    sums = jnp.sum(gate_float, -1, keepdims=True)
    squares = jnp.sum(gate_float * gate_float, -1, keepdims=True)
    stat_lane = lax.broadcasted_iota(jnp.int32, (8, 128), 1)
    stats = jnp.zeros((8, 128), F32)
    for k in range(rows // 8):
        at = slice(8 * k, 8 * k + 8)
        stats = jnp.where(stat_lane // 8 == k, sums[at], stats)
        stats = jnp.where(stat_lane // 8 == 8 + k, squares[at], stats)
    stat_send[...] = stats

    tail = pl.ds(rows - HALO, HALO)
    head = pl.ds(0, HALO)

    def gate_copies():
        return (
            send(gate_half.at[tail], gate_prev, gate_ss.at[0], gate_rs.at[0], after, tp),
            send(gate_half.at[head], gate_next, gate_ss.at[1], gate_rs.at[1], before, tp),
        )

    def stat_copy(i):
        return send(
            stat_send, stat_recv.at[tp], stat_ss.at[i], stat_rs.at[i], seq, tp_peer(i)
        )

    def stat_halo(i):
        to = tp_peer(i)
        return (
            send(stat_send, stat_prev.at[tp], stat_hs.at[0, i], stat_hr.at[0, i], after, to),
            send(stat_send, stat_next.at[tp], stat_hs.at[1, i], stat_hr.at[1, i], before, to),
        )

    for i in reversed(range(tp_size)):
        halo_start(stat_halo(i))
    halo_start(gate_copies())
    for i in reversed(range(1, tp_size)):
        stat_copy(i).start()
    stat_recv[tp] = stat_send[...]

    def hand_on(chosen):
        for i in chosen:
            kv_copy(i).wait_recv()
            across_copy(key_place(i)).start()

    hand_on(relayed[:4])
    hand_on(relayed[4:])
    resid_half[...] = hidden_half(0)
    for i in direct:
        kv_copy(i).wait_recv()

    @pl.loop(1, tp_size)
    def _(i):
        stat_copy(i).wait_recv()

    @pl.loop(0, tp_size)
    def _(i):
        halo_arrived(stat_halo(i))

    halo_arrived(gate_copies())

    def gate_normed(part, stats, blocks, keep):
        total = jnp.sum(stats[...], 0) / CH
        average = jnp.concatenate([total[:, 8 * k : 8 * k + 1] for k in blocks], 0)
        square = jnp.concatenate([total[:, HEAD + 8 * k : HEAD + 8 * k + 1] for k in blocks], 0)
        variance = square - average * average
        result = (part[...].astype(F32) - average) * lax.rsqrt(variance + 1e-05)
        result = result.astype(BF16).astype(F32)
        return result if keep is None else jnp.where(keep, result, 0.0)

    gate_pad[pl.ds(0, HALO)] = gate_normed(gate_prev, stat_prev, range(rows // 8 - 2, rows // 8), jnp.logical_not(first))
    gate_pad[pl.ds(HALO, rows)] = gate_normed(gate_half, stat_recv, range(rows // 8), None)
    gate_pad[pl.ds(HALO + rows, HALO)] = gate_normed(gate_next, stat_next, range(2), jnp.logical_not(last))
    weights[1].wait()
    weights[2].wait()
    gated = []
    for column in range(0, resid_half.shape[1], 128):
        conv = depthwise(gate_pad, w_conv, column, rows)
        resid = resid_half[:, pl.ds(column, 128)].astype(F32)
        gated.append((resid * conv).astype(BF16))

    width = out.shape[1]

    def part_copy(which, i):
        to = tp_peer(i)
        return send(
            part_send.at[which, to],
            part_recv.at[which, tp],
            part_ss.at[which, i],
            part_rs.at[which, i],
            seq,
            to,
        )

    def part_halo(which, i):
        to = tp_peer(i)
        return (
            send(
                part_send.at[which, to, tail],
                part_prev.at[which, tp],
                part_hs.at[which, 0, i],
                part_hr.at[which, 0, i],
                after,
                to,
            ),
            send(
                part_send.at[which, to, head],
                part_next.at[which, tp],
                part_hs.at[which, 1, i],
                part_hr.at[which, 1, i],
                before,
                to,
            ),
        )

    def columns_of(to):
        return pl.ds(pl.multiple_of(to * width, width), width)

    def scatter_part(which, rows_here, weight):
        for i in reversed(range(tp_size)):
            to = tp_peer(i)
            piece = jnp.dot(rows_here, weight[:, columns_of(to)], preferred_element_type=F32)
            part_send[which, to] = piece.astype(BF16)
            halo_start(part_halo(which, i))
            if i:
                part_copy(which, i).start()
        part_recv[which, tp] = part_send[which, tp]

    def merge_part(which):
        @pl.loop(1, tp_size)
        def _(i):
            part_copy(which, i).wait_recv()

        @pl.loop(0, tp_size)
        def _(i):
            halo_arrived(part_halo(which, i))

        def joined(ref):
            return jnp.sum(ref[which].astype(F32), 0).astype(BF16).astype(F32)

        own = joined(part_recv)
        blend_pad[pl.ds(0, HALO)] = jnp.where(first, 0.0, joined(part_prev))
        blend_pad[pl.ds(HALO, rows)] = own
        blend_pad[pl.ds(HALO + rows, HALO)] = jnp.where(last, 0.0, joined(part_next))
        taps_pad[...] = w_blend[:, which, :]
        mixture = [
            (own[:, c : c + 128] + depthwise(blend_pad, taps_pad, c, rows)).astype(BF16)
            for c in range(0, width, 128)
        ]
        return jnp.concatenate(mixture, 1)

    @pl.loop(1, groups)
    def _(i):
        q_copy(i).wait_recv()

    @pl.loop(0, nearby)
    def _(i):
        across_copy(i).wait_recv()

    keys = sides * nearby * rows
    kv = kv_all[...].reshape(keys, 128)
    kv_ones[...] = jnp.where(low_lanes(keys), jnp.ones((), BF16), kv)

    def o_copy(other):
        return send(
            o_send.at[other], o_recv.at[group], o_ss.at[other], o_rs.at[group], group_seq(other), tp
        )

    per_step = 4

    @pl.loop(0, groups // per_step)
    def _(step):
        start = group + groups + jnp.where(step < 2, 6 + 4 * step, 12 * step - 22)
        count = per_step * rows
        pieces = []
        for i in range(per_step):
            q = q_all[lax.rem(start + i, groups)]
            q_end = pltpu.roll(q[:HALO].astype(F32), HEAD, 1).astype(BF16)
            pieces += [q, q_end]
        q = jnp.concatenate(pieces, 0)
        q = jnp.where(low_lanes(count), q, jnp.zeros((), BF16))
        kv = kv_all[...].reshape(keys, 128)
        scores = lax.dot_general(q, kv, (((1,), (1,)), ((), ())), preferred_element_type=F32)
        peak = jnp.max(scores, -1, keepdims=True)
        weight = jnp.exp2((scores - peak) * (LOG2E * HEAD**-0.5)).astype(BF16)
        mixed = jnp.dot(weight, kv_ones[...], preferred_element_type=F32)
        low_q = low_lanes(count)
        total = jnp.where(low_q, mixed, pltpu.roll(mixed, HEAD, 1))
        level = peak * HEAD**-0.5 + jnp.log(total)
        level_high = level.astype(BF16).astype(F32)
        level_low = level - level_high
        mixed = mixed / total
        lane = lax.broadcasted_iota(jnp.int32, (HALO, 128), 1)
        for i in range(per_step):
            thirds = [slice(i * rows + k * HALO, i * rows + (k + 1) * HALO) for k in range(3)]
            spare = jnp.zeros((HALO, 128), F32)
            for k, at in enumerate(thirds):
                spare = jnp.where(lane // 8 == 2 * k, level_high[at], spare)
                spare = jnp.where(lane // 8 == 2 * k + 1, level_low[at], spare)
            o_low = low_lanes(HALO)
            first_rows = jnp.where(o_low, pltpu.roll(mixed[thirds[2]], HEAD, 1), mixed[thirds[0]])
            other = lax.rem(start + i, groups)
            o_send[other, pl.ds(0, HALO)] = first_rows.astype(BF16)
            o_send[other, pl.ds(HALO, HALO)] = jnp.where(o_low, spare, mixed[thirds[1]]).astype(
                BF16
            )
        for i in range(per_step):
            other = lax.rem(start + i, groups)

            @pl.when(other != group)
            def _():
                o_copy(other).start()

            @pl.when(other == group)
            def _():
                o_recv[other] = o_send[other]

    scatter_part(1, jnp.concatenate(gated, 1), w_proj)

    for i in (3, 4):
        weights[i].wait()
    weights[5].wait()

    @pl.loop(1, nearby)
    def _(i):
        kv_copy(i).wait_send()
        q_copy(i).wait_send()

    for i in direct:
        direct_copy(i).wait_send()
    for i in relayed:
        across_copy(key_place(i)).wait_send()
    across_copy(place).wait_send()
    halo_sent(gate_copies())

    def sent_part(which):
        @pl.loop(1, tp_size)
        def _(i):
            part_copy(which, i).wait_send()

        @pl.loop(0, tp_size)
        def _(i):
            halo_sent(part_halo(which, i))

    @pl.loop(1, tp_size)
    def _(i):
        stat_copy(i).wait_send()

    @pl.loop(0, tp_size)
    def _(i):
        halo_sent(stat_halo(i))

    def o_arrival(other):
        return send(
            o_send.at[other], o_recv.at[other], o_ss.at[other], o_rs.at[other], group_seq(other), tp
        )

    @pl.loop(1, groups)
    def _(i):
        o_arrival(group_peer(i)[0]).wait_recv()

    heads = []
    for h in range(HEADS_HERE):
        pieces, levels = [], []
        for b in range(groups // HEADS_HERE):
            piece = o_recv[b * HEADS_HERE + h].astype(F32)
            spare = piece[HALO:]
            pieces.append(jnp.concatenate([piece, pltpu.roll(piece[:HALO], HEAD, 1)], 0))
            levels.append(
                jnp.concatenate(
                    [
                        spare[:, 16 * k : 16 * k + 1] + spare[:, 16 * k + 8 : 16 * k + 9]
                        for k in range(3)
                    ],
                    0,
                )
            )
        peak = functools.reduce(jnp.maximum, levels)
        shares = [jnp.exp(level - peak) for level in levels]
        whole = functools.reduce(jnp.add, shares)
        mixed = functools.reduce(jnp.add, [s * p for s, p in zip(shares, pieces)])
        heads.append(mixed / whole)
    attended = jnp.concatenate(
        [
            jnp.where(low, pltpu.roll(heads[2 * pair], HEAD, 1), heads[2 * pair + 1]).astype(BF16)
            for pair in range(HEADS_HERE // 2)
        ],
        1,
    )
    scatter_part(0, attended, w_out)
    fin_acc[...] = jnp.dot(merge_part(1), w_merge[1], preferred_element_type=F32)
    mixture = merge_part(0)

    def fin_copy(i):
        to = tp_peer(i)
        return send(fin_send.at[to], fin_recv.at[tp], fin_ss.at[i], fin_rs.at[i], seq, to)

    for i in reversed(range(tp_size)):
        to = tp_peer(i)
        piece = jnp.dot(mixture, w_merge[0, :, columns_of(to)], preferred_element_type=F32)
        fin_send[to] = (fin_acc[:, columns_of(to)] + piece).astype(BF16)
        if i:
            fin_copy(i).start()
    fin_recv[tp] = fin_send[tp]

    @pl.loop(1, groups)
    def _(i):
        o_arrival(group_peer(i)[0]).wait_send()

    sent_part(0)
    sent_part(1)

    @pl.loop(1, tp_size)
    def _(i):
        fin_copy(i).wait_recv()

    own = frames[:, pl.ds(pl.multiple_of(tp * width, width), width)].astype(F32)
    out[...] = (own + jnp.sum(fin_recv[...].astype(F32), 0)).astype(BF16)

    for i in range(1, tp_size):
        fin_copy(i).wait_send()


def solution(mesh):
    seq_size, tp_size = mesh.shape["seq"], mesh.shape["tp"]

    def on_device(*args):
        frames, query, key, value, w_out, w_in, w_conv, w_proj, w_blend, w_merge = args
        rows, width = query.shape
        features = frames.shape[1]
        units = w_in.shape[2]
        groups = 2 * DEPTH
        sources = seq_size // DEPTH * 2
        wide = rows + 2 * HALO
        dma = pltpu.SemaphoreType.DMA
        vmem = pltpu.VMEM
        return pl.pallas_call(
            functools.partial(kernel, seq_size, tp_size),
            out_shape=jax.ShapeDtypeStruct((rows, width), BF16),
            in_specs=[pl.BlockSpec(memory_space=pltpu.HBM)] * 10,
            out_specs=pl.BlockSpec(memory_space=pltpu.VMEM),
            scratch_shapes=[
                vmem(frames.shape, BF16),
                vmem(query.shape, BF16),
                vmem(key.shape, BF16),
                vmem(value.shape, BF16),
                vmem(w_out.shape, BF16),
                vmem(w_in.shape, BF16),
                vmem(w_conv.shape, F32),
                vmem(w_proj.shape, BF16),
                vmem(w_blend.shape, F32),
                vmem(w_merge.shape, BF16),
                vmem((HEADS_HERE, rows, 128), BF16),
                vmem((HEADS_HERE, 2 * HALO, 128), BF16),
                vmem((sources, rows, 128), BF16),
                vmem((sources * rows, 128), BF16),
                vmem((groups, 2 * HALO, 128), BF16),
                vmem((groups, 2 * HALO, 128), BF16),
                vmem((groups, 2 * HALO, 128), BF16),
                vmem((rows, units), BF16),
                vmem((rows, units), BF16),
                vmem((HALO, units), BF16),
                vmem((HALO, units), BF16),
                vmem((8, 128), F32),
                vmem((tp_size, 8, 128), F32),
                vmem((tp_size, 8, 128), F32),
                vmem((tp_size, 8, 128), F32),
                vmem((wide, units), F32),
                vmem((2, tp_size, rows, width), BF16),
                vmem((2, tp_size, rows, width), BF16),
                vmem((2, tp_size, HALO, width), BF16),
                vmem((2, tp_size, HALO, width), BF16),
                vmem((wide, width), F32),
                vmem((TAPS, width), F32),
                vmem((rows, features), F32),
                vmem((tp_size, rows, width), BF16),
                vmem((tp_size, rows, width), BF16),
                dma((4,)),
                dma((6,)),
                dma((2 * RING,)),
                dma((2 * RING,)),
                dma((2 * RING,)),
                dma((2 * RING,)),
                dma((2 * RING,)),
                dma((groups,)),
                dma((groups,)),
                dma((groups,)),
                dma((groups,)),
                dma((2,)),
                dma((2,)),
                dma((tp_size,)),
                dma((tp_size,)),
                dma((2, tp_size)),
                dma((2, tp_size)),
                dma((2, tp_size)),
                dma((2, tp_size)),
                dma((2, 2, tp_size)),
                dma((2, 2, tp_size)),
                dma((tp_size,)),
                dma((tp_size,)),
            ],
            compiler_params=pltpu.CompilerParams(
                collective_id=0,
                has_side_effects=True,
                vmem_limit_bytes=63 * 1024 * 1024,
            ),
        )(*args)

    return jax.shard_map(
        on_device,
        mesh=mesh,
        in_specs=(
            P("seq", None),
            P("seq", "tp"),
            P("seq", "tp"),
            P("seq", "tp"),
            P("tp", None),
            P(None, None, "tp"),
            P(None, "tp"),
            P("tp", None),
            P(None, None, "tp"),
            P(None, "tp", None),
        ),
        out_specs=P("seq", "tp"),
        check_vma=False,
    )
```
